512 devices in a mesh: ctx: 32 (over x_hi, z, core), tp: 16 (over x_lo, y).
Axes of the slice: x: 4 (x_hi: 2, x_lo: 2; x = x_hi * 2 + x_lo), y: 8, z: 8, core: 2. Of those that a mesh axis runs over, the one named last changes fastest.
Arguments:
- queries: bfloat16 [5120, 4096], P('ctx', 'tp'), may hold values from -2.109375 to 2.109375
- keys: bfloat16 [5120, 4096], P('ctx', 'tp'), may hold values from -2.109375 to 2.109375
- values: bfloat16 [5120, 4096], P('ctx', 'tp'), may hold values from -6 to 6
- rates: float32 [32, 5120], P('tp', 'ctx'), may hold values from 2.5e-05 to 0.06, as said below
- init_weight: float32 [32, 128, 128], P('tp'), may hold values from -1.5 to 1.5
- out_weight: bfloat16 [4096, 6144], P('tp'), may hold values from -0.09375 to 0.09375
Outputs:
- mixed: bfloat16 [5120, 6144], P('ctx', 'tp')
The draws below stay inside these ranges and needn't reach their ends.
Inputs may be any that keep to these rules, and one draw needn't show every extreme that they name: `rates`: positive.
All inputs are finite; a program needn't handle non-finite values.
Results may differ from the reference program's by a relative error of at most 0.0049.
Values sent between devices are 32-bit elements; how exact they have to be, the bound alone decides.
No kernel may reach another device: no remote copies, remote signals or barrier semaphores. Data moves between devices by JAX's collectives and lax.ppermute only.
A program may use at most 64 MiB of HBM per device.

```python
from functools import partial
import jax
import jax.numpy as jnp
from jax import lax

D = 6144
HEAD_DIM = 128
MB = 16
TOK_CTX = 160
HEADS = 32
STREAM_LENGTH = 5120


def draw_rates(key, part):
    key = jax.random.fold_in(key, 7)
    master_seed, element_seed, portion_seed, segment_seed = jax.random.split(key, 4)
    base_rate = jnp.exp(jax.random.uniform(master_seed, (HEADS, 1), jnp.float32, jnp.log(0.0001), jnp.log(0.015)))
    token_factor = jnp.exp(jax.random.uniform(element_seed, (HEADS, STREAM_LENGTH), jnp.float32, jnp.log(0.5), jnp.log(2.0)))
    shard_count = STREAM_LENGTH // TOK_CTX
    shard_factor = jnp.exp(jax.random.uniform(portion_seed, (HEADS, shard_count, 1), jnp.float32, jnp.log(0.5), jnp.log(2.0)))
    shard_factor = jnp.broadcast_to(shard_factor, (HEADS, shard_count, TOK_CTX)).reshape(HEADS, STREAM_LENGTH)
    combined_answer = base_rate * token_factor * shard_factor
    segment_lead_places = jax.random.randint(segment_seed, (4,), 0, STREAM_LENGTH // 32)
    segment_indices = jnp.arange(STREAM_LENGTH, dtype=jnp.int32) // 32
    within_segment = jnp.any(segment_indices[None, :] == segment_lead_places[:, None], axis=0)
    combined_answer = jnp.where(within_segment[None, :], 0.06, combined_answer)
    return jnp.minimum(combined_answer, 0.06).astype(jnp.float32)


def block_scale(rng, shape, shards, low, largest):
    factor_of = 1.0
    for axis_at, parts in shards:
        heights = jax.random.uniform(jax.random.fold_in(jax.random.fold_in(rng, 6), axis_at), (parts,), jnp.float32, low / len(shards), largest / len(shards))
        factor_of = factor_of * jnp.repeat(jnp.exp(heights), shape[axis_at] // parts).reshape((-1,) + (1,) * (len(shape) - 1 - axis_at))
    return factor_of


def scatter_about(rng, extent, scale, bound, shards=(), held_as=jnp.bfloat16):
    drawn = scale * jax.random.normal(rng, extent, jnp.float32)
    if shards:
        drawn = drawn * block_scale(rng, extent, shards, -0.22, 0.18)
    return jnp.clip(drawn, -bound, bound).astype(held_as)


def setup_inputs(seed: int = 0) -> dict:
    seeds = jax.random.split(jax.random.key(seed), 7)
    queries = scatter_about(seeds[0], (STREAM_LENGTH, HEADS * HEAD_DIM), (4 / HEAD_DIM ** 0.5), 2.109375, ((0, 32), (1, 16)))
    keys = scatter_about(seeds[1], (STREAM_LENGTH, HEADS * HEAD_DIM), (4 / HEAD_DIM ** 0.5), 2.109375, ((0, 32), (1, 16)))
    values = scatter_about(seeds[2], (STREAM_LENGTH, HEADS * HEAD_DIM), 1.0, 6.0, ((0, 32), (1, 16)))
    rates = draw_rates(jax.random.fold_in(seeds[6], 71), 0)
    init_weight = scatter_about(seeds[4], (HEADS, HEAD_DIM, HEAD_DIM), 0.25, 1.5, ((0, 16),), jnp.float32)
    out_weight = scatter_about(seeds[5], (HEADS * HEAD_DIM, D), (HEADS * HEAD_DIM) ** -0.5, 0.09375, ((0, 16),))
    return {"queries": queries, "keys": keys, "values": values, "rates": rates, "init_weight": init_weight, "out_weight": out_weight}


exact_sum = partial(jnp.einsum, precision=lax.Precision.HIGHEST)


def reference(queries, keys, values, rates, init_weight, out_weight):
    block_count = STREAM_LENGTH // MB

    def to_blocks(source):
        shaped = source.astype(jnp.float32).reshape(block_count, MB, HEADS, HEAD_DIM)
        return shaped.transpose(0, 2, 1, 3)

    query_blocks = to_blocks(queries)
    key_blocks = to_blocks(keys)
    value_blocks = to_blocks(values)
    rate_blocks = rates.reshape(HEADS, block_count, MB).transpose(1, 0, 2)
    causal_mask = jnp.tril(jnp.ones((MB, MB), jnp.float32))

    def advance(weight_now, inputs):
        query_rows, key_rows, value_rows, rate_rows = inputs
        weights_mix = exact_sum("hsd,htd->hst", query_rows, key_rows) * causal_mask * rate_rows[:, None, :]
        errors = exact_sum("hsd,hde->hse", key_rows, weight_now) - value_rows
        outputs = exact_sum("hsd,hde->hse", query_rows, weight_now) - exact_sum("hst,hte->hse", weights_mix, errors)
        weight_next = weight_now - exact_sum("hsd,hse->hde", key_rows * rate_rows[:, :, None], errors)
        return weight_next, outputs

    final_weight, outputs = lax.scan(advance, init_weight.astype(jnp.float32),
                                     (query_blocks, key_blocks, value_blocks, rate_blocks))
    flat_outputs = outputs.transpose(0, 2, 1, 3).reshape(STREAM_LENGTH, HEADS * HEAD_DIM).astype(jnp.bfloat16)
    total = jnp.dot(flat_outputs, out_weight, preferred_element_type=jnp.float32)
    return total.astype(jnp.bfloat16)
```

```python
import functools

import jax
import jax.numpy as jnp
from jax import lax
from jax.experimental import pallas as pl
from jax.experimental.pallas import tpu as pltpu
from jax.sharding import Mesh, PartitionSpec as P

MB = 16
HW = 128
XH, Z, CORE, XL, Y = "xh", "z", "core", "xl", "y"
SIZES = (2, 8, 2, 2, 8)
f32 = jnp.float32
bf16 = jnp.bfloat16
VM = pl.BlockSpec(memory_space=pltpu.VMEM)
SM = pl.BlockSpec(memory_space=pltpu.SMEM)


def exact(a, b, contract=((1,), (0,))):
    return lax.dot_general(
        a, b, (contract, ((), ())), precision=lax.Precision.HIGHEST, preferred_element_type=f32
    )


def single(a, b, contract=((1,), (0,))):
    return lax.dot_general(a, b, (contract, ((), ())), preferred_element_type=f32)


def call(kernel, out_shapes, *args, scalars=0, scratch=(), cost=1e6):
    outs = [jax.ShapeDtypeStruct(s, d) for s, d in out_shapes]
    return pl.pallas_call(
        kernel,
        out_shape=outs,
        in_specs=[SM] * scalars + [VM] * (len(args) - scalars),
        out_specs=[VM] * len(outs),
        scratch_shapes=list(scratch),
        compiler_params=pltpu.CompilerParams(vmem_limit_bytes=40 * 2**20),
        cost_estimate=pl.CostEstimate(flops=int(cost), bytes_accessed=int(cost / 100), transcendentals=0),
    )(*args)


def shard_maps(core_ref, q_ref, k_ref, v_ref, r_ref, keep_ref, send_ref, lead_ref, rest_ref, x_ref):
    rows = q_ref.shape[0]
    core = core_ref[0]
    s_at = lax.broadcasted_iota(jnp.int32, (rows, rows), 0)
    t_at = lax.broadcasted_iota(jnp.int32, (rows, rows), 1)
    earlier_block = (t_at // MB) < (s_at // MB)
    causal = t_at <= s_at
    diagonal = t_at == s_at
    eye = (
        lax.broadcasted_iota(jnp.int32, (HW, 2 * HW), 0)
        == lax.broadcasted_iota(jnp.int32, (HW, 2 * HW), 1)
    ).astype(f32)
    mix, key_gram, columns = [], [], []
    for h in range(2):
        at = slice(h * HW, (h + 1) * HW)
        q, k, v = q_ref[:, at], k_ref[:, at], v_ref[:, at]
        r = r_ref[h : h + 1, :]
        columns.append(jnp.sum(jnp.where(diagonal, r, 0.0), axis=1, keepdims=True))
        key_gram.append(jnp.where(earlier_block, single(k, k, ((1,), (1,))) * r, 0.0))
        mix.append(jnp.where(causal, single(q, k, ((1,), (1,))) * r, 0.0))
        x_ref[h, :, :HW] = k.astype(f32)
        x_ref[h, :, HW:] = v.astype(f32)
    for i in range(1, rows // MB):
        at = slice(i * MB, (i + 1) * MB)
        for h in range(2):
            x_ref[h, at, :] = x_ref[h, at, :] - exact(key_gram[h][at, :], x_ref[h])
    maps = []
    for h in range(2):
        at = slice(h * HW, (h + 1) * HW)
        x = x_ref[h]
        y = exact(mix[h], x)
        lead_ref[:, at] = q_ref[:, at].astype(f32) - y[:, :HW]
        rest_ref[:, at] = y[:, HW:]
        ab = exact(k_ref[:, at].astype(f32) * columns[h], x, ((0,), (0,)))
        sign = jnp.where(lax.broadcasted_iota(jnp.int32, (HW, 2 * HW), 1) < HW, -1.0, 1.0)
        maps.append(eye + sign * ab)
    first = core == 0
    keep_ref[...] = jnp.where(first, maps[0], maps[1])
    send_ref[...] = jnp.where(first, maps[1], maps[0])


def after(second, first):
    moved = exact(second[:, :HW], first)
    return moved + jnp.where(lax.broadcasted_iota(jnp.int32, second.shape, 1) < HW, 0.0, second)


def chip_map(core_ref, keep_ref, got_ref, out_ref):
    first = core_ref[0] == 0
    early = jnp.where(first, keep_ref[...], got_ref[...])
    late = jnp.where(first, got_ref[...], keep_ref[...])
    out_ref[...] = after(late, early)


def ring_prefix(at_ref, w0_ref, own, l1, l2, l3, r1, r2, r3, far, pre_ref, end_ref, maps, state):
    z = at_ref[0]
    x_hi = at_ref[1]
    n = SIZES[1]
    for offset, ref in ((0, own), (-1, l1), (-2, l2), (-3, l3), (1, r1), (2, r2), (3, r3), (4, far)):
        maps[lax.rem(z + (offset + n), n)] = ref[...]
    eye = (
        lax.broadcasted_iota(jnp.int32, (HW, HW), 0) == lax.broadcasted_iota(jnp.int32, (HW, HW), 1)
    ).astype(f32)
    now = jnp.concatenate([eye, jnp.where(x_hi == 0, w0_ref[...], 0.0)], axis=1)
    state[0] = now
    for i in range(n):
        now = after(maps[i], now)
        state[i + 1] = now
    pre_ref[...] = state[z]
    end_ref[...] = now[:, HW:]


def shard_states(at_ref, pre_ref, got_ref, keep_map_ref, got_map_ref, keep_ref, send_ref):
    x_hi, core = at_ref[1], at_ref[2]
    first = core == 0
    pre = pre_ref[...]
    start = jnp.where(x_hi == 0, pre[:, HW:], exact(pre[:, :HW], got_ref[...]) + pre[:, HW:])
    early = jnp.where(first, keep_map_ref[...], got_map_ref[...])
    middle = exact(early[:, :HW], start) + early[:, HW:]
    keep_ref[...] = jnp.where(first, start, middle)
    send_ref[...] = jnp.where(first, middle, start)


def outputs(at_ref, keep_ref, got_ref, lead_ref, rest_ref, z_ref):
    first = at_ref[2] == 0
    states = (
        jnp.where(first, keep_ref[...], got_ref[...]),
        jnp.where(first, got_ref[...], keep_ref[...]),
    )
    for h in range(2):
        at = slice(h * HW, (h + 1) * HW)
        z = exact(lead_ref[:, at], states[h]) + rest_ref[:, at]
        z_ref[:, at] = z.astype(bf16).astype(f32)


def narrow(at_ref, mine_ref, other_ref, out_ref):
    first = at_ref[2] == 0
    out_ref[:HW, :] = jnp.where(first, mine_ref[...], other_ref[...]).astype(bf16)
    out_ref[HW:, :] = jnp.where(first, other_ref[...], mine_ref[...]).astype(bf16)


def project(z_ref, zx_ref, w_ref, wx_ref, out_ref):
    out_ref[0] = single(z_ref[...].astype(bf16), w_ref[...]) + single(
        zx_ref[...].astype(bf16), wx_ref[...]
    )


def rotated(x, axis, by):
    n = lax.axis_size(axis)
    return lax.ppermute(x, axis, [(i, (i + by) % n) for i in range(n)])


def gather_ring(x, axis):
    half = x.shape[0] // 2
    before, beyond = [x], [x]
    for _ in range(3):
        before.append(rotated(before[-1], axis, 1))
        beyond.append(rotated(beyond[-1], axis, -1))
    low = rotated(before[-1][:half], axis, 1)
    high = rotated(beyond[-1][half:], axis, -1)
    return before[1:], beyond[1:], jnp.concatenate([low, high], axis=0)


def scatter_ring(pieces, axis):
    n = lax.axis_size(axis)
    me = lax.axis_index(axis)
    half = pieces.shape[1] // 2

    def piece(offset):
        return lax.dynamic_index_in_dim(pieces, lax.rem(me + (offset + n), n), 0, keepdims=False)

    far = piece(4)
    down = jnp.concatenate([rotated(far[:half], axis, -1), jnp.zeros_like(far[half:])], axis=0) + piece(-3)
    up = jnp.concatenate([jnp.zeros_like(far[:half]), rotated(far[half:], axis, 1)], axis=0) + piece(3)
    for step in (2, 1):
        down = rotated(down, axis, -1) + piece(-step)
        up = rotated(up, axis, 1) + piece(step)
    return rotated(down, axis, -1) + rotated(up, axis, 1) + piece(0)


def local(queries, keys, values, rates, init_weight, out_weight):
    rows = queries.shape[0]
    x_hi, z, core, x_lo = (lax.axis_index(a) for a in (XH, Z, CORE, XL))
    at = jnp.stack([z, x_hi, core]).astype(jnp.int32)
    core_at = core.reshape(1).astype(jnp.int32)
    features = out_weight.shape[1] // 2
    chunk = features // SIZES[4]

    mine_columns = lax.dynamic_slice_in_dim(out_weight, x_lo * features, features, 1)
    to_send = lax.dynamic_slice(out_weight, (core * HW, (1 - x_lo) * features), (HW, features))
    from_pair = rotated(to_send.astype(f32), XL, 1)
    from_core = rotated(from_pair, CORE, 1)

    keep, send, lead, rest = call(
        shard_maps,
        [((HW, 2 * HW), f32)] * 2 + [((rows, 2 * HW), f32)] * 2,
        core_at, queries, keys, values, rates,
        scalars=1, scratch=[pltpu.VMEM((2, rows, 2 * HW), f32)], cost=2e9,
    )
    got = rotated(send, CORE, 1)
    (own,) = call(chip_map, [((HW, 2 * HW), f32)], core_at, keep, got, scalars=1)
    before, beyond, far = gather_ring(own, Z)
    w0 = lax.dynamic_index_in_dim(init_weight, core, 0, keepdims=False)
    pre, end = call(
        ring_prefix,
        [((HW, 2 * HW), f32), ((HW, HW), f32)],
        at, w0, own, *before, *beyond, far,
        scalars=1,
        scratch=[pltpu.VMEM((8, HW, 2 * HW), f32), pltpu.VMEM((9, HW, 2 * HW), f32)],
    )
    arrived = lax.ppermute(end, XH, [(0, 1)])
    kept, leaving = call(
        shard_states, [((HW, HW), f32)] * 2, at, pre, arrived, keep, got, scalars=1
    )
    came = rotated(leaving, CORE, 1)
    (z_rows,) = call(outputs, [((rows, 2 * HW), f32)], at, kept, came, lead, rest, scalars=1)
    z_pair = rotated(z_rows, XL, 1)

    (pair_columns,) = call(narrow, [((2 * HW, features), bf16)], at, from_pair, from_core, scalars=1)
    pieces = pl.pallas_call(
        project,
        grid=(SIZES[4],),
        out_shape=jax.ShapeDtypeStruct((SIZES[4], rows, chunk), f32),
        in_specs=[
            pl.BlockSpec((rows, 2 * HW), lambda i: (0, 0)),
            pl.BlockSpec((rows, 2 * HW), lambda i: (0, 0)),
            pl.BlockSpec((2 * HW, chunk), lambda i: (0, i)),
            pl.BlockSpec((2 * HW, chunk), lambda i: (0, i)),
        ],
        out_specs=pl.BlockSpec((1, rows, chunk), lambda i: (i, 0, 0)),
        compiler_params=pltpu.CompilerParams(vmem_limit_bytes=40 * 2**20),
    )(z_rows, z_pair, mine_columns, pair_columns)
    return scatter_ring(pieces, Y).astype(bf16)


def solution(mesh):
    fine = Mesh(mesh.devices.reshape(SIZES), (XH, Z, CORE, XL, Y))
    ctx, tp = (XH, Z, CORE), (XL, Y)
    in_specs = (P(ctx, tp), P(ctx, tp), P(ctx, tp), P(tp, ctx), P(tp, None, None), P(tp, None))
    return jax.shard_map(local, mesh=fine, in_specs=in_specs, out_specs=P(ctx, tp), check_vma=False)
```

```python
import jax
import jax.numpy as jnp
from jax import lax
from jax.experimental import pallas as pl
from jax.experimental.pallas import tpu as pltpu
from jax.sharding import Mesh, PartitionSpec as P

MB = 16
HW = 128
XH, Z, CORE, XL, Y = "xh", "z", "core", "xl", "y"
SIZES = (2, 8, 2, 2, 8)
f32 = jnp.float32
bf16 = jnp.bfloat16
VM = pl.BlockSpec(memory_space=pltpu.VMEM)
SM = pl.BlockSpec(memory_space=pltpu.SMEM)
MIB = 2**20


def exact(a, b, contract=((1,), (0,))):
    return lax.dot_general(
        a, b, (contract, ((), ())), precision=lax.Precision.HIGHEST, preferred_element_type=f32
    )


def single(a, b, contract=((1,), (0,))):
    return lax.dot_general(a, b, (contract, ((), ())), preferred_element_type=f32)


def call(kernel, out_shapes, at, *args, later=(), scratch=(), limit=4, us=1.0):
    outs = [jax.ShapeDtypeStruct(s, d) for s, d in out_shapes]
    n = 1 + len(args)

    def body(*refs):
        kernel(*refs[:n], *refs[n + len(later) :])

    return pl.pallas_call(
        body,
        out_shape=outs,
        in_specs=[SM] + [VM] * len(args) + [pl.BlockSpec(memory_space=pl.ANY)] * len(later),
        out_specs=[VM] * len(outs),
        scratch_shapes=list(scratch),
        compiler_params=pltpu.CompilerParams(vmem_limit_bytes=limit * MIB),
        cost_estimate=pl.CostEstimate(flops=int(us * 1e9), bytes_accessed=1 << 17, transcendentals=0),
    )(at, *args, *later)


def place(at_ref):
    return at_ref[0], at_ref[1], at_ref[2]


def left_half(shape):
    return lax.broadcasted_iota(jnp.int32, shape, 1) < HW


def identity(columns):
    rows_at = lax.broadcasted_iota(jnp.int32, (HW, columns), 0)
    return (rows_at == lax.broadcasted_iota(jnp.int32, (HW, columns), 1)).astype(f32)


def after(second, first):
    return exact(second[:, :HW], first) + jnp.where(left_half(second.shape), 0.0, second)


def applied(pair, state):
    return exact(pair[:, :HW], state) + pair[:, HW:]


def shard_maps(at_ref, q_ref, k_ref, v_ref, r_ref, keep_ref, send_ref, rows_ref, x_ref):
    rows = q_ref.shape[0]
    _, _, core = place(at_ref)
    s_at = lax.broadcasted_iota(jnp.int32, (rows, rows), 0)
    t_at = lax.broadcasted_iota(jnp.int32, (rows, rows), 1)
    earlier_block = (t_at // MB) < (s_at // MB)
    causal = t_at <= s_at
    diagonal = t_at == s_at
    mix, key_gram, columns = [], [], []
    for h in range(2):
        at = slice(h * HW, (h + 1) * HW)
        q, k, v = q_ref[:, at], k_ref[:, at], v_ref[:, at]
        r = r_ref[h : h + 1, :]
        columns.append(jnp.sum(jnp.where(diagonal, r, 0.0), axis=1, keepdims=True))
        key_gram.append(jnp.where(earlier_block, single(k, k, ((1,), (1,))) * r, 0.0))
        mix.append(jnp.where(causal, single(q, k, ((1,), (1,))) * r, 0.0))
        x_ref[h, :, :HW] = k.astype(f32)
        x_ref[h, :, HW:] = v.astype(f32)
    for i in range(1, rows // MB):
        at = slice(i * MB, (i + 1) * MB)
        for h in range(2):
            x_ref[h, at, :] = x_ref[h, at, :] - exact(key_gram[h][at, :], x_ref[h])
    maps = []
    for h in range(2):
        at = slice(h * HW, (h + 1) * HW)
        x = x_ref[h]
        y = exact(mix[h], x)
        rows_ref[:, at] = q_ref[:, at].astype(f32) - y[:, :HW]
        rows_ref[:, (2 + h) * HW : (3 + h) * HW] = y[:, HW:]
        ab = exact(k_ref[:, at].astype(f32) * columns[h], x, ((0,), (0,)))
        maps.append(identity(2 * HW) + jnp.where(left_half(ab.shape), -ab, ab))
    first = core == 0
    keep_ref[...] = jnp.where(first, maps[0], maps[1])
    send_ref[...] = jnp.where(first, maps[1], maps[0])


def chip_map(at_ref, keep_ref, got_ref, out_ref):
    first = place(at_ref)[2] == 0
    early = jnp.where(first, keep_ref[...], got_ref[...])
    late = jnp.where(first, got_ref[...], keep_ref[...])
    out_ref[...] = after(late, early)


def join_chips(at_ref, own_ref, got_ref, both_ref, pre_ref):
    upper = lax.rem(place(at_ref)[0], 2) == 1
    low = jnp.where(upper, got_ref[...], own_ref[...])
    high = jnp.where(upper, own_ref[...], got_ref[...])
    both_ref[...] = after(high, low)
    pre_ref[...] = jnp.where(upper, low, identity(2 * HW))


def join_pairs(at_ref, own_ref, got_ref, pre_in_ref, both_ref, pre_ref):
    upper = lax.rem(place(at_ref)[0], 4) >= 2
    low = jnp.where(upper, got_ref[...], own_ref[...])
    high = jnp.where(upper, own_ref[...], got_ref[...])
    both_ref[...] = after(high, low)
    pre = pre_in_ref[...]
    pre_ref[...] = jnp.where(upper, after(pre, low), pre)


def join_ring(at_ref, own_ref, got_ref, pre_in_ref, first_ref, end_ref, pre_ref):
    z, _, core = place(at_ref)
    upper = z >= 4
    low = jnp.where(upper, got_ref[...], own_ref[...])
    high = jnp.where(upper, own_ref[...], got_ref[...])
    end_ref[...] = applied(high, applied(low, first_ref[core]))
    pre = pre_in_ref[...]
    pre_ref[...] = jnp.where(upper, after(pre, low), pre)


def shard_states(at_ref, pre_ref, arrived_ref, first_ref, keep_ref, got_ref, out_ref):
    _, x_hi, core = place(at_ref)
    start = applied(pre_ref[...], jnp.where(x_hi == 0, first_ref[core], arrived_ref[...]))
    out_ref[:, :HW] = start
    out_ref[:, HW:] = applied(jnp.where(core == 0, keep_ref[...], got_ref[...]), start)


def piece_weights(to_ref, own_ref, pair_ref, out_ref):
    del to_ref
    out_ref[0, : 2 * HW, :] = own_ref[...]
    out_ref[0, 2 * HW :, :] = pair_ref[0].astype(bf16)


def pair_weights(to_ref, w_ref, later_ref, out_ref):
    del to_ref, later_ref
    out_ref[0] = w_ref[...].astype(f32)


def outputs(at_ref, s00, s01, s10, s11, r00, r01, r10, r11, w_ref, z_ref, piece_ref):
    core = place(at_ref)[2]
    first = core == 0
    rows = r00.shape[0]
    for g, (mine, others, own_rows, far_rows) in enumerate(((s00, s01, r00, r01), (s10, s11, r10, r11))):
        for h in range(2):
            states = jnp.where(core == h, mine[...], others[...])
            near = jnp.where(first, states[:, :HW], states[:, HW:])
            far = jnp.where(first, states[:, HW:], states[:, :HW])
            at = slice((2 * g + h) * HW, (2 * g + h + 1) * HW)
            lead, rest = slice(h * HW, (h + 1) * HW), slice((2 + h) * HW, (3 + h) * HW)
            z_ref[:rows, at] = (exact(own_rows[:, lead], near) + own_rows[:, rest]).astype(bf16)
            z_ref[rows:, at] = (exact(far_rows[:, lead], far) + far_rows[:, rest]).astype(bf16)
    piece_ref[...] = single(z_ref[:rows, :], w_ref[0])


def project(z_ref, w_ref, out_ref):
    for i in range(4):
        out_ref[i] = single(z_ref[...], w_ref[i + 1])


def swapped(x, axes):
    n = 2 ** len(axes)
    return lax.ppermute(x, axes, [(i, n - 1 - i) for i in range(n)])


def ring_step(x):
    n = SIZES[4]
    pairs = [(i, (i - 1) % n) for i in range(n)] + [(n + i, n + (i + 1) % n) for i in range(n)]
    return lax.ppermute(x, (CORE, Y), pairs)


def local(queries, keys, values, rates, init_weight, out_weight):
    rows = queries.shape[0]
    x_hi, z, core, x_lo, y = (lax.axis_index(a) for a in (XH, Z, CORE, XL, Y))
    at = jnp.stack([z, x_hi, core]).astype(jnp.int32)
    chunk = out_weight.shape[1] // (SIZES[3] * SIZES[4])
    square, wide = ((HW, HW), f32), ((HW, 2 * HW), f32)

    keep, send, own_rows = call(
        shard_maps, [wide, wide, ((rows, 4 * HW), f32)], at, queries, keys, values, rates,
        scratch=[pltpu.VMEM((2, rows, 2 * HW), f32)], limit=8, us=3,
    )
    away = jnp.array([4, 3, 2, 1, 0], jnp.int32) * (2 * core - 1)
    dest = lax.rem(y + away + SIZES[4], SIZES[4]).astype(jnp.int32)
    to_pair = pl.pallas_call(
        pair_weights,
        grid_spec=pltpu.PrefetchScalarGridSpec(
            num_scalar_prefetch=1,
            grid=(5,),
            in_specs=[
                pl.BlockSpec((2 * HW, chunk), lambda i, to: (0, to[i])),
                pl.BlockSpec(memory_space=pl.ANY),
            ],
            out_specs=pl.BlockSpec((1, 2 * HW, chunk), lambda i, to: (i, 0, 0)),
        ),
        out_shape=jax.ShapeDtypeStruct((5, 2 * HW, chunk), f32),
        compiler_params=pltpu.CompilerParams(vmem_limit_bytes=4 * MIB),
    )(dest + (1 - x_lo) * SIZES[4], out_weight, send)
    from_pair = swapped(to_pair, (XL,))

    rows_core, rows_pair, rows_both = (
        swapped(own_rows, (CORE,)), swapped(own_rows, (XL,)), swapped(own_rows, (CORE, XL))
    )
    got = swapped(send, (CORE,))
    (chip,) = call(chip_map, [wide], at, keep, got)

    def across_z(x, to):
        return lax.ppermute(x, Z, [(i, to(i)) for i in range(SIZES[1])])

    both, pre = call(join_chips, [wide, wide], at, chip, across_z(chip, lambda i: i ^ 1), later=[rows_core])
    four, pre = call(join_pairs, [wide, wide], at, both, across_z(both, lambda i: i ^ 2), pre, later=[rows_pair])
    end, pre = call(join_ring, [square, wide], at, four, across_z(four, lambda i: 7 - i), pre, init_weight, later=[rows_both])
    arrived = lax.ppermute(end, XH, [(0, 1)])
    weights = pl.pallas_call(
        piece_weights,
        grid_spec=pltpu.PrefetchScalarGridSpec(
            num_scalar_prefetch=1,
            grid=(5,),
            in_specs=[
                pl.BlockSpec((2 * HW, chunk), lambda i, to: (0, to[i])),
                pl.BlockSpec((1, 2 * HW, chunk), lambda i, to: (i, 0, 0)),
            ],
            out_specs=pl.BlockSpec((1, 4 * HW, chunk), lambda i, to: (i, 0, 0)),
        ),
        out_shape=jax.ShapeDtypeStruct((5, 4 * HW, chunk), bf16),
        compiler_params=pltpu.CompilerParams(vmem_limit_bytes=4 * MIB),
    )(dest + x_lo * SIZES[4], out_weight, from_pair)

    (states,) = call(shard_states, [wide], at, pre, arrived, init_weight, keep, got, later=[weights])

    states_pair = swapped(states, (XL,))
    states_core = swapped(states, (CORE,))
    states_both = swapped(states_pair, (CORE,))

    z_rows, leaving = call(
        outputs, [((2 * rows, 4 * HW), bf16), ((rows, chunk), f32)], at,
        states, states_core, states_pair, states_both, own_rows, rows_core, rows_pair, rows_both, weights,
        limit=16,
    )
    arriving = ring_step(leaving)
    pieces = pl.pallas_call(
        project,
        out_shape=jax.ShapeDtypeStruct((4, 2 * rows, chunk), f32),
        in_specs=[VM, VM],
        out_specs=VM,
        compiler_params=pltpu.CompilerParams(vmem_limit_bytes=16 * MIB),
        cost_estimate=pl.CostEstimate(flops=int(1e9), bytes_accessed=1 << 21, transcendentals=0),
    )(z_rows, weights)
    total = pieces[0].at[:rows].add(arriving)
    for i in (1, 2):
        total = ring_step(total) + pieces[i]
    total = ring_step(total)
    others = swapped(total[rows:], (CORE,))
    return (total[:rows] + others + pieces[3, :rows]).astype(bf16)


def solution(mesh):
    fine = Mesh(mesh.devices.reshape(SIZES), (XH, Z, CORE, XL, Y))
    ctx, tp = (XH, Z, CORE), (XL, Y)
    in_specs = (P(ctx, tp), P(ctx, tp), P(ctx, tp), P(tp, ctx), P(tp, None, None), P(tp, None))
    return jax.shard_map(local, mesh=fine, in_specs=in_specs, out_specs=P(ctx, tp), check_vma=False)
```

```python
import jax
import jax.numpy as jnp
from jax import lax
from jax.experimental import pallas as pl
from jax.experimental.pallas import tpu as pltpu
from jax.sharding import Mesh, PartitionSpec as P

MB = 16
HW = 128
XH, Z, CORE, XL, Y = "xh", "z", "core", "xl", "y"
SIZES = (2, 8, 2, 2, 8)
f32 = jnp.float32
bf16 = jnp.bfloat16
VM = pl.BlockSpec(memory_space=pltpu.VMEM)
SM = pl.BlockSpec(memory_space=pltpu.SMEM)
MIB = 2**20


def exact(a, b, contract=((1,), (0,))):
    return lax.dot_general(
        a, b, (contract, ((), ())), precision=lax.Precision.HIGHEST, preferred_element_type=f32
    )


def single(a, b, contract=((1,), (0,))):
    return lax.dot_general(a, b, (contract, ((), ())), preferred_element_type=f32)


def call(kernel, out_shapes, at, *args, later=(), scratch=(), limit=4, us=1.0):
    outs = [jax.ShapeDtypeStruct(s, d) for s, d in out_shapes]
    n = 1 + len(args)

    def body(*refs):
        kernel(*refs[:n], *refs[n + len(later) :])

    return pl.pallas_call(
        body,
        out_shape=outs,
        in_specs=[SM] + [VM] * len(args) + [pl.BlockSpec(memory_space=pl.ANY)] * len(later),
        out_specs=[VM] * len(outs),
        scratch_shapes=list(scratch),
        compiler_params=pltpu.CompilerParams(vmem_limit_bytes=limit * MIB),
        cost_estimate=pl.CostEstimate(flops=int(us * 1e9), bytes_accessed=1 << 17, transcendentals=0),
    )(at, *args, *later)


def place(at_ref):
    return at_ref[0], at_ref[1], at_ref[2]


def left_half(shape):
    return lax.broadcasted_iota(jnp.int32, shape, 1) < HW


def identity(columns):
    rows_at = lax.broadcasted_iota(jnp.int32, (HW, columns), 0)
    return (rows_at == lax.broadcasted_iota(jnp.int32, (HW, columns), 1)).astype(f32)


def after(second, first):
    return exact(second[:, :HW], first) + jnp.where(left_half(second.shape), 0.0, second)


def applied(pair, state):
    return exact(pair[:, :HW], state) + pair[:, HW:]


def shard_maps(at_ref, q_ref, k_ref, v_ref, r_ref, keep_ref, send_ref, rows_ref, x_ref):
    rows = q_ref.shape[0]
    _, _, core = place(at_ref)
    s_at = lax.broadcasted_iota(jnp.int32, (rows, rows), 0)
    t_at = lax.broadcasted_iota(jnp.int32, (rows, rows), 1)
    earlier_block = (t_at // MB) < (s_at // MB)
    causal = t_at <= s_at
    diagonal = t_at == s_at
    mix, key_gram, columns = [], [], []
    for h in range(2):
        at = slice(h * HW, (h + 1) * HW)
        q, k, v = q_ref[:, at], k_ref[:, at], v_ref[:, at]
        r = r_ref[h : h + 1, :]
        columns.append(jnp.sum(jnp.where(diagonal, r, 0.0), axis=1, keepdims=True))
        key_gram.append(jnp.where(earlier_block, single(k, k, ((1,), (1,))) * r, 0.0))
        mix.append(jnp.where(causal, single(q, k, ((1,), (1,))) * r, 0.0))
        x_ref[h, :, :HW] = k.astype(f32)
        x_ref[h, :, HW:] = v.astype(f32)
    for i in range(1, rows // MB):
        at = slice(i * MB, (i + 1) * MB)
        for h in range(2):
            x_ref[h, at, :] = x_ref[h, at, :] - exact(key_gram[h][at, :], x_ref[h])
    maps = []
    for h in range(2):
        at = slice(h * HW, (h + 1) * HW)
        x = x_ref[h]
        y = exact(mix[h], x)
        rows_ref[:, at] = q_ref[:, at].astype(f32) - y[:, :HW]
        rows_ref[:, (2 + h) * HW : (3 + h) * HW] = y[:, HW:]
        ab = exact(k_ref[:, at].astype(f32) * columns[h], x, ((0,), (0,)))
        maps.append(identity(2 * HW) + jnp.where(left_half(ab.shape), -ab, ab))
    first = core == 0
    keep_ref[...] = jnp.where(first, maps[0], maps[1])
    send_ref[...] = jnp.where(first, maps[1], maps[0])


def chip_map(at_ref, keep_ref, got_ref, out_ref):
    first = place(at_ref)[2] == 0
    early = jnp.where(first, keep_ref[...], got_ref[...])
    late = jnp.where(first, got_ref[...], keep_ref[...])
    out_ref[...] = after(late, early)


def join_chips(at_ref, own_ref, got_ref, both_ref, pre_ref):
    upper = lax.rem(place(at_ref)[0], 2) == 1
    low = jnp.where(upper, got_ref[...], own_ref[...])
    high = jnp.where(upper, own_ref[...], got_ref[...])
    both_ref[...] = after(high, low)
    pre_ref[...] = jnp.where(upper, low, identity(2 * HW))


def join_pairs(at_ref, own_ref, got_ref, pre_in_ref, both_ref, pre_ref):
    upper = lax.rem(place(at_ref)[0], 4) >= 2
    low = jnp.where(upper, got_ref[...], own_ref[...])
    high = jnp.where(upper, own_ref[...], got_ref[...])
    both_ref[...] = after(high, low)
    pre = pre_in_ref[...]
    pre_ref[...] = jnp.where(upper, after(pre, low), pre)


def join_ring(at_ref, own_ref, got_ref, pre_in_ref, first_ref, end_ref, pre_ref):
    z, _, core = place(at_ref)
    upper = z >= 4
    low = jnp.where(upper, got_ref[...], own_ref[...])
    high = jnp.where(upper, own_ref[...], got_ref[...])
    end_ref[...] = applied(high, applied(low, first_ref[core]))
    pre = pre_in_ref[...]
    pre_ref[...] = jnp.where(upper, after(pre, low), pre)


def shard_prefixes(at_ref, pre_ref, keep_ref, got_ref, mine_ref, other_ref):
    first = place(at_ref)[2] == 0
    pre = pre_ref[...]
    middle = after(jnp.where(first, keep_ref[...], got_ref[...]), pre)
    mine_ref[...] = jnp.where(first, pre, middle)
    other_ref[...] = jnp.where(first, middle, pre)


def shard_states(at_ref, mine_ref, other_ref, arrived_ref, first_ref, keep_ref, send_ref):
    _, x_hi, core = place(at_ref)
    state = jnp.where(x_hi == 0, first_ref[core], arrived_ref[...])
    send_ref[...] = applied(other_ref[...], state)
    keep_ref[...] = applied(mine_ref[...], state)


def outputs(at_ref, keep_ref, got_ref, rows_ref, z_ref):
    core = place(at_ref)[2]
    for h in range(2):
        state = jnp.where(core == h, keep_ref[...], got_ref[...])
        at = slice(h * HW, (h + 1) * HW)
        z = exact(rows_ref[:, at], state) + rows_ref[:, (2 + h) * HW : (3 + h) * HW]
        z_ref[:, at] = z.astype(bf16).astype(f32)


def pair_weights(to_ref, w_ref, later_ref, near_ref, far_ref):
    del to_ref, later_ref
    near_ref[...] = w_ref[:HW, :].astype(f32)
    far_ref[...] = w_ref[HW:, :].astype(f32)


def piece(z, z_pair, to, w_ref, near_ref, far_ref):
    chunk = w_ref.shape[1] // (SIZES[3] * SIZES[4])
    x_lo, y = to
    at = pl.ds(pl.multiple_of(y * chunk, HW), chunk)
    own_at = pl.ds(pl.multiple_of((x_lo * SIZES[4] + y) * chunk, HW), chunk)
    return (
        single(z, w_ref[:, own_at])
        + single(z_pair[:, :HW], near_ref[:, at].astype(bf16))
        + single(z_pair[:, HW:], far_ref[:, at].astype(bf16))
    )


def farthest(at_ref, z_ref, zx_ref, w_ref, near_ref, far_ref, low_ref, high_ref):
    half = low_ref.shape[0]
    to = (at_ref[3], lax.rem(at_ref[4] + 4, SIZES[4]))
    out = piece(z_ref[...].astype(bf16), zx_ref[...].astype(bf16), to, w_ref, near_ref, far_ref)
    low_ref[...] = out[:half]
    high_ref[...] = out[half:]


OFFSETS = (-3, 3, -2, 2, -1, 1, 0)


def nearer(at_ref, z_ref, zx_ref, w_ref, near_ref, far_ref, *out_refs):
    z, zx = z_ref[...].astype(bf16), zx_ref[...].astype(bf16)
    for offset, out_ref in zip(OFFSETS, out_refs):
        to = (at_ref[3], lax.rem(at_ref[4] + (offset + SIZES[4]), SIZES[4]))
        out_ref[...] = piece(z, zx, to, w_ref, near_ref, far_ref)


def swapped(x, axes):
    n = 2 ** len(axes)
    return lax.ppermute(x, axes, [(i, n - 1 - i) for i in range(n)])


def passed(x, axis, by):
    n = lax.axis_size(axis)
    return lax.ppermute(x, axis, [(i, (i + by) % n) for i in range(n)])


def local(queries, keys, values, rates, init_weight, out_weight):
    rows = queries.shape[0]
    x_hi, z, core, x_lo, y = (lax.axis_index(a) for a in (XH, Z, CORE, XL, Y))
    at = jnp.stack([z, x_hi, core, x_lo, y]).astype(jnp.int32)
    columns = out_weight.shape[1] // SIZES[3]
    chunk = columns // SIZES[4]
    square, wide, out_piece = ((HW, HW), f32), ((HW, 2 * HW), f32), ((rows, chunk), f32)

    keep, send, own_rows = call(
        shard_maps, [wide, wide, ((rows, 4 * HW), f32)], at, queries, keys, values, rates,
        scratch=[pltpu.VMEM((2, rows, 2 * HW), f32)], limit=56, us=3,
    )
    got = swapped(send, (CORE,))

    def across_z(x, to):
        return lax.ppermute(x, Z, [(i, to(i)) for i in range(SIZES[1])])

    (chip,) = call(chip_map, [wide], at, keep, got)
    parts = 4
    near_out, far_out = pl.pallas_call(
        pair_weights,
        grid_spec=pltpu.PrefetchScalarGridSpec(
            num_scalar_prefetch=1,
            grid=(parts,),
            in_specs=[
                pl.BlockSpec((2 * HW, columns // parts), lambda i, to: (0, to[0] * parts + i)),
                pl.BlockSpec(memory_space=pl.ANY),
            ],
            out_specs=[pl.BlockSpec((HW, columns // parts), lambda i, to: (0, i))] * 2,
        ),
        out_shape=[jax.ShapeDtypeStruct((HW, columns), f32)] * 2,
        compiler_params=pltpu.CompilerParams(vmem_limit_bytes=6 * MIB),
    )((1 - x_lo).reshape(1).astype(jnp.int32), out_weight, chip)
    near = swapped(near_out, (XL,))
    far = swapped(far_out, (XH, XL))

    both, pre = call(join_chips, [wide, wide], at, chip, across_z(chip, lambda i: i ^ 1), later=[near_out], us=3)
    four, pre = call(join_pairs, [wide, wide], at, both, across_z(both, lambda i: i ^ 2), pre, us=3)
    end, pre = call(join_ring, [square, wide], at, four, across_z(four, lambda i: 7 - i), pre, init_weight, us=3)
    arrived = lax.ppermute(end, XH, [(0, 1)])
    mine, other = call(shard_prefixes, [wide, wide], at, pre, keep, got, us=3)
    kept, leaving = call(shard_states, [square, square], at, mine, other, arrived, init_weight, us=3)
    (z_rows,) = call(outputs, [((rows, 2 * HW), f32)], at, kept, swapped(leaving, (CORE,)), own_rows)
    z_pair = swapped(z_rows, (XL,))

    factors = (z_rows, z_pair, out_weight, near, far)
    low, high = call(farthest, [((rows // 2, chunk), f32)] * 2, at, *factors, limit=16)
    down, up = passed(low, Y, -1), passed(high, Y, 1)
    pieces = call(nearer, [out_piece] * len(OFFSETS), at, *factors, later=[low], limit=16)
    down = pieces[0] + jnp.concatenate([down, jnp.zeros_like(down)], axis=0)
    up = pieces[1] + jnp.concatenate([jnp.zeros_like(up), up], axis=0)
    for i in (2, 4):
        down = passed(down, Y, -1) + pieces[i]
        up = passed(up, Y, 1) + pieces[i + 1]
    return (passed(down, Y, -1) + passed(up, Y, 1) + pieces[6]).astype(bf16)


def solution(mesh):
    fine = Mesh(mesh.devices.reshape(SIZES), (XH, Z, CORE, XL, Y))
    ctx, tp = (XH, Z, CORE), (XL, Y)
    in_specs = (P(ctx, tp), P(ctx, tp), P(ctx, tp), P(tp, ctx), P(tp, None, None), P(tp, None))
    return jax.shard_map(local, mesh=fine, in_specs=in_specs, out_specs=P(ctx, tp), check_vma=False)
```

```python
import jax
import jax.numpy as jnp
from jax import lax
from jax.experimental import pallas as pl
from jax.experimental.pallas import tpu as pltpu
from jax.sharding import Mesh, PartitionSpec as P

MB = 16
HW = 128
XH, Z, CORE, XL, Y = "xh", "z", "core", "xl", "y"
SIZES = (2, 8, 2, 2, 8)
f32 = jnp.float32
bf16 = jnp.bfloat16
VM = pl.BlockSpec(memory_space=pltpu.VMEM)
SM = pl.BlockSpec(memory_space=pltpu.SMEM)
MIB = 2**20


def exact(a, b, contract=((1,), (0,))):
    return lax.dot_general(
        a, b, (contract, ((), ())), precision=lax.Precision.HIGHEST, preferred_element_type=f32
    )


def single(a, b, contract=((1,), (0,))):
    return lax.dot_general(a, b, (contract, ((), ())), preferred_element_type=f32)


def call(kernel, out_shapes, place, *args, later=(), scratch=(), limit=4, us=1.0, space=VM):
    outs = [jax.ShapeDtypeStruct(s, d) for s, d in out_shapes]
    n = len(place) + len(args)

    def body(*refs):
        kernel(*refs[:n], *refs[n + len(later) :])

    return pl.pallas_call(
        body,
        out_shape=outs,
        in_specs=[SM] * len(place) + [space] * len(args) + [pl.BlockSpec(memory_space=pl.ANY)] * len(later),
        out_specs=[VM] * len(outs),
        scratch_shapes=list(scratch),
        compiler_params=pltpu.CompilerParams(vmem_limit_bytes=limit * MIB),
        cost_estimate=pl.CostEstimate(flops=int(us * 1e9), bytes_accessed=1 << 17, transcendentals=0),
    )(*place, *args, *later)


def left_half(shape):
    return lax.broadcasted_iota(jnp.int32, shape, 1) < HW


def identity(columns):
    rows_at = lax.broadcasted_iota(jnp.int32, (HW, columns), 0)
    return (rows_at == lax.broadcasted_iota(jnp.int32, (HW, columns), 1)).astype(f32)


def after(second, first):
    return exact(second[:, :HW], first) + jnp.where(left_half(second.shape), 0.0, second)


def applied(pair, state):
    return exact(pair[:, :HW], state) + pair[:, HW:]


def shard_maps(core_ref, q_hbm, k_hbm, v_hbm, r_hbm, keep_ref, send_ref, rows_ref, *scratch):
    q_ref, k_ref, v_ref, r_ref, x_ref, *done = scratch
    copies = [
        pltpu.make_async_copy(source, target, semaphore)
        for source, target, semaphore in zip((q_hbm, k_hbm, v_hbm, r_hbm), scratch, done)
    ]
    for copy in copies:
        copy.start()
    rows = q_ref.shape[0]
    core = core_ref[0]
    s_at = lax.broadcasted_iota(jnp.int32, (rows, rows), 0)
    t_at = lax.broadcasted_iota(jnp.int32, (rows, rows), 1)
    earlier_block = (t_at // MB) < (s_at // MB)
    causal = t_at <= s_at
    diagonal = t_at == s_at
    mix, key_gram, columns = [], [], []
    for copy in copies:
        copy.wait()
    for h in range(2):
        at = slice(h * HW, (h + 1) * HW)
        q, k, v = q_ref[:, at], k_ref[:, at], v_ref[:, at]
        r = r_ref[h : h + 1, :]
        columns.append(jnp.sum(jnp.where(diagonal, r, 0.0), axis=1, keepdims=True))
        key_gram.append(jnp.where(earlier_block, single(k, k, ((1,), (1,))) * r, 0.0))
        mix.append(jnp.where(causal, single(q, k, ((1,), (1,))) * r, 0.0))
        x_ref[h, :, :HW] = k.astype(f32)
        x_ref[h, :, HW:] = v.astype(f32)
    for i in range(1, rows // MB):
        at = slice(i * MB, (i + 1) * MB)
        for h in range(2):
            x_ref[h, at, :] = x_ref[h, at, :] - exact(key_gram[h][at, :], x_ref[h])
    maps = []
    for h in range(2):
        at = slice(h * HW, (h + 1) * HW)
        x = x_ref[h]
        y = exact(mix[h], x)
        rows_ref[:, at] = q_ref[:, at].astype(f32) - y[:, :HW]
        rows_ref[:, (2 + h) * HW : (3 + h) * HW] = y[:, HW:]
        ab = exact(k_ref[:, at].astype(f32) * columns[h], x, ((0,), (0,)))
        maps.append(identity(2 * HW) + jnp.where(left_half(ab.shape), -ab, ab))
    first = core == 0
    keep_ref[...] = jnp.where(first, maps[0], maps[1])
    send_ref[...] = jnp.where(first, maps[1], maps[0])


def chip_map(core_ref, keep_ref, got_ref, out_ref):
    first = core_ref[0] == 0
    early = jnp.where(first, keep_ref[...], got_ref[...])
    late = jnp.where(first, got_ref[...], keep_ref[...])
    out_ref[...] = after(late, early)


def join_chips(z_ref, own_ref, got_ref, both_ref, pre_ref):
    upper = lax.rem(z_ref[0], 2) == 1
    low = jnp.where(upper, got_ref[...], own_ref[...])
    high = jnp.where(upper, own_ref[...], got_ref[...])
    both_ref[...] = after(high, low)
    pre_ref[...] = jnp.where(upper, low, identity(2 * HW))


def join_pairs(z_ref, own_ref, got_ref, pre_in_ref, both_ref, pre_ref):
    upper = lax.rem(z_ref[0], 4) >= 2
    low = jnp.where(upper, got_ref[...], own_ref[...])
    high = jnp.where(upper, own_ref[...], got_ref[...])
    both_ref[...] = after(high, low)
    pre = pre_in_ref[...]
    pre_ref[...] = jnp.where(upper, after(pre, low), pre)


def join_ring(z_ref, core_ref, own_ref, got_ref, pre_in_ref, first_ref, end_ref, pre_ref):
    upper = z_ref[0] >= 4
    low = jnp.where(upper, got_ref[...], own_ref[...])
    high = jnp.where(upper, own_ref[...], got_ref[...])
    end_ref[...] = applied(high, applied(low, first_ref[core_ref[0]]))
    pre = pre_in_ref[...]
    pre_ref[...] = jnp.where(upper, after(pre, low), pre)


def shard_prefixes(core_ref, pre_ref, keep_ref, got_ref, mine_ref, other_ref):
    first = core_ref[0] == 0
    pre = pre_ref[...]
    middle = after(jnp.where(first, keep_ref[...], got_ref[...]), pre)
    mine_ref[...] = jnp.where(first, pre, middle)
    other_ref[...] = jnp.where(first, middle, pre)


def shard_states(x_hi_ref, core_ref, mine_ref, other_ref, arrived_ref, first_ref, keep_ref, send_ref):
    state = jnp.where(x_hi_ref[0] == 0, first_ref[core_ref[0]], arrived_ref[...])
    send_ref[...] = applied(other_ref[...], state)
    keep_ref[...] = applied(mine_ref[...], state)


def outputs(core_ref, keep_ref, got_ref, rows_ref, z_ref):
    core = core_ref[0]
    for h in range(2):
        state = jnp.where(core == h, keep_ref[...], got_ref[...])
        at = slice(h * HW, (h + 1) * HW)
        z = exact(rows_ref[:, at], state) + rows_ref[:, (2 + h) * HW : (3 + h) * HW]
        z_ref[:, at] = z.astype(bf16).astype(f32)


def pair_weights(to_ref, w_ref, later_ref, near_ref, far_ref):
    del to_ref, later_ref
    near_ref[...] = w_ref[:HW, :].astype(f32)
    far_ref[...] = w_ref[HW:, :].astype(f32)


def piece(z, z_pair, to, w_ref, near_ref, far_ref):
    chunk = w_ref.shape[1] // (SIZES[3] * SIZES[4])
    x_lo, y = to
    at = pl.ds(pl.multiple_of(y * chunk, HW), chunk)
    own_at = pl.ds(pl.multiple_of((x_lo * SIZES[4] + y) * chunk, HW), chunk)
    return (
        single(z, w_ref[:, own_at])
        + single(z_pair[:, :HW], near_ref[:, at].astype(bf16))
        + single(z_pair[:, HW:], far_ref[:, at].astype(bf16))
    )


def farthest(x_lo_ref, y_ref, z_ref, zx_ref, w_ref, near_ref, far_ref, low_ref, high_ref):
    half = low_ref.shape[0]
    to = (x_lo_ref[0], lax.rem(y_ref[0] + 4, SIZES[4]))
    out = piece(z_ref[...].astype(bf16), zx_ref[...].astype(bf16), to, w_ref, near_ref, far_ref)
    low_ref[...] = out[:half]
    high_ref[...] = out[half:]


OFFSETS = (-3, 3, -2, 2, -1, 1, 0)


def nearer(x_lo_ref, y_ref, z_ref, zx_ref, w_ref, near_ref, far_ref, *out_refs):
    z, zx = z_ref[...].astype(bf16), zx_ref[...].astype(bf16)
    for offset, out_ref in zip(OFFSETS, out_refs):
        to = (x_lo_ref[0], lax.rem(y_ref[0] + (offset + SIZES[4]), SIZES[4]))
        out_ref[...] = piece(z, zx, to, w_ref, near_ref, far_ref)


def swapped(x, axes):
    n = 2 ** len(axes)
    return lax.ppermute(x, axes, [(i, n - 1 - i) for i in range(n)])


def passed(x, axis, by):
    n = lax.axis_size(axis)
    return lax.ppermute(x, axis, [(i, (i + by) % n) for i in range(n)])


def local(queries, keys, values, rates, init_weight, out_weight):
    rows = queries.shape[0]
    x_hi, z, core, x_lo, y = (lax.axis_index(a).reshape(1) for a in (XH, Z, CORE, XL, Y))
    columns = out_weight.shape[1] // SIZES[3]
    chunk = columns // SIZES[4]
    square, wide, out_piece = ((HW, HW), f32), ((HW, 2 * HW), f32), ((rows, chunk), f32)

    keep, send, own_rows = call(
        shard_maps, [wide, wide, ((rows, 4 * HW), f32)], [core],
        *(pltpu.with_memory_space_constraint(x, pltpu.HBM) for x in (queries, keys, values, rates)),
        scratch=[pltpu.VMEM((rows, 2 * HW), bf16)] * 3
        + [pltpu.VMEM((2, rows), f32), pltpu.VMEM((2, rows, 2 * HW), f32)]
        + [pltpu.SemaphoreType.DMA] * 4,
        space=pl.BlockSpec(memory_space=pltpu.HBM), limit=8, us=3,
    )
    got = swapped(send, (CORE,))

    def across_z(x, to):
        return lax.ppermute(x, Z, [(i, to(i)) for i in range(SIZES[1])])

    (chip,) = call(chip_map, [wide], [core], keep, got)
    parts = 4
    near_out, far_out = pl.pallas_call(
        pair_weights,
        grid_spec=pltpu.PrefetchScalarGridSpec(
            num_scalar_prefetch=1,
            grid=(parts,),
            in_specs=[
                pl.BlockSpec((2 * HW, columns // parts), lambda i, to: (0, to[0] * parts + i)),
                pl.BlockSpec(memory_space=pl.ANY),
            ],
            out_specs=[pl.BlockSpec((HW, columns // parts), lambda i, to: (0, i))] * 2,
        ),
        out_shape=[jax.ShapeDtypeStruct((HW, columns), f32)] * 2,
        compiler_params=pltpu.CompilerParams(vmem_limit_bytes=6 * MIB),
    )(1 - x_lo, out_weight, chip)
    near = swapped(near_out, (XL,))
    far = swapped(far_out, (XH, XL))

    both, pre = call(join_chips, [wide, wide], [z], chip, across_z(chip, lambda i: i ^ 1), later=[near_out], us=2)
    four, pre = call(join_pairs, [wide, wide], [z], both, across_z(both, lambda i: i ^ 2), pre, us=2)
    end, pre = call(join_ring, [square, wide], [z, core], four, across_z(four, lambda i: 7 - i), pre, init_weight, us=2)
    arrived = lax.ppermute(end, XH, [(0, 1)])
    mine, other = call(shard_prefixes, [wide, wide], [core], pre, keep, got, us=2)
    kept, leaving = call(shard_states, [square, square], [x_hi, core], mine, other, arrived, init_weight, us=2)
    (z_rows,) = call(outputs, [((rows, 2 * HW), f32)], [core], kept, swapped(leaving, (CORE,)), own_rows)
    z_pair = swapped(z_rows, (XL,))

    factors = (z_rows, z_pair, out_weight, near, far)
    low, high = call(farthest, [((rows // 2, chunk), f32)] * 2, [x_lo, y], *factors, limit=16)
    down, up = passed(low, Y, -1), passed(high, Y, 1)
    pieces = call(nearer, [out_piece] * len(OFFSETS), [x_lo, y], *factors, later=[low], limit=16)
    down = pieces[0] + jnp.concatenate([down, jnp.zeros_like(down)], axis=0)
    up = pieces[1] + jnp.concatenate([jnp.zeros_like(up), up], axis=0)
    for i in (2, 4):
        down = passed(down, Y, -1) + pieces[i]
        up = passed(up, Y, 1) + pieces[i + 1]
    return (passed(down, Y, -1) + passed(up, Y, 1) + pieces[6]).astype(bf16)


def solution(mesh):
    fine = Mesh(mesh.devices.reshape(SIZES), (XH, Z, CORE, XL, Y))
    ctx, tp = (XH, Z, CORE), (XL, Y)
    in_specs = (P(ctx, tp), P(ctx, tp), P(ctx, tp), P(tp, ctx), P(tp, None, None), P(tp, None))
    return jax.shard_map(local, mesh=fine, in_specs=in_specs, out_specs=P(ctx, tp), check_vma=False)
```

```python
import jax
import jax.numpy as jnp
from jax import lax
from jax.experimental import pallas as pl
from jax.experimental.pallas import tpu as pltpu
from jax.sharding import Mesh, PartitionSpec as P

MB = 16
HW = 128
XH, Z, CORE, XL, Y = "xh", "z", "core", "xl", "y"
SIZES = (2, 8, 2, 2, 8)
f32 = jnp.float32
bf16 = jnp.bfloat16
VM = pl.BlockSpec(memory_space=pltpu.VMEM)
SM = pl.BlockSpec(memory_space=pltpu.SMEM)
MIB = 2**20


def exact(a, b, contract=((1,), (0,))):
    return lax.dot_general(
        a, b, (contract, ((), ())), precision=lax.Precision.HIGH, preferred_element_type=f32
    )


def single(a, b, contract=((1,), (0,))):
    return lax.dot_general(a, b, (contract, ((), ())), preferred_element_type=f32)


def call(kernel, out_shapes, place, *args, later=(), scratch=(), limit=4, us=1.0, space=pltpu.VMEM, pinned=False):
    outs = [pltpu.VMEM(s, d) if pinned else jax.ShapeDtypeStruct(s, d) for s, d in out_shapes]
    n = len(place) + len(args)

    def body(*refs):
        kernel(*refs[:n], *refs[n + len(later) :])

    return pl.pallas_call(
        body,
        out_shape=outs,
        in_specs=[SM] * len(place) + [pl.BlockSpec(memory_space=space)] * len(args) + [pl.BlockSpec(memory_space=pl.ANY)] * len(later),
        out_specs=[VM] * len(outs),
        scratch_shapes=list(scratch),
        compiler_params=pltpu.CompilerParams(vmem_limit_bytes=limit * MIB),
        cost_estimate=pl.CostEstimate(flops=int(us * 1e9), bytes_accessed=1 << 17, transcendentals=0),
    )(*place, *(pltpu.with_memory_space_constraint(x, space) for x in args), *later)


def left_half(shape):
    return lax.broadcasted_iota(jnp.int32, shape, 1) < HW


def identity(columns):
    rows_at = lax.broadcasted_iota(jnp.int32, (HW, columns), 0)
    return (rows_at == lax.broadcasted_iota(jnp.int32, (HW, columns), 1)).astype(f32)


def after(second, first):
    return exact(second[:, :HW], first) + jnp.where(left_half(second.shape), 0.0, second)


def applied(pair, state):
    return exact(pair[:, :HW], state) + pair[:, HW:]


def shard_maps(core_ref, q_hbm, k_hbm, v_hbm, r_hbm, w_hbm, keep_ref, send_ref, rows_ref, first_ref, *scratch):
    q_ref, k_ref, v_ref, r_ref, x_ref, *done = scratch
    copies = [
        pltpu.make_async_copy(source, target, semaphore)
        for source, target, semaphore in zip((q_hbm, k_hbm, v_hbm, r_hbm), scratch, done)
    ]
    copies.append(pltpu.make_async_copy(w_hbm.at[core_ref[0]], first_ref, done[4]))
    for copy in copies:
        copy.start()
    rows = q_ref.shape[0]
    core = core_ref[0]
    s_at = lax.broadcasted_iota(jnp.int32, (rows, rows), 0)
    t_at = lax.broadcasted_iota(jnp.int32, (rows, rows), 1)
    earlier_block = (t_at // MB) < (s_at // MB)
    causal = t_at <= s_at
    diagonal = t_at == s_at
    mix, key_gram, columns = [], [], []
    for copy in copies[:4]:
        copy.wait()
    for h in range(2):
        at = slice(h * HW, (h + 1) * HW)
        q, k, v = q_ref[:, at], k_ref[:, at], v_ref[:, at]
        r = r_ref[h : h + 1, :]
        columns.append(jnp.sum(jnp.where(diagonal, r, 0.0), axis=1, keepdims=True))
        key_gram.append(jnp.where(earlier_block, single(k, k, ((1,), (1,))) * r, 0.0))
        mix.append(jnp.where(causal, single(q, k, ((1,), (1,))) * r, 0.0))
        x_ref[h, :, :HW] = k.astype(f32)
        x_ref[h, :, HW:] = v.astype(f32)
    for i in range(1, rows // MB):
        at = slice(i * MB, (i + 1) * MB)
        for h in range(2):
            x_ref[h, at, :] = x_ref[h, at, :] - exact(key_gram[h][at, :], x_ref[h])
    maps = []
    for h in range(2):
        at = slice(h * HW, (h + 1) * HW)
        x = x_ref[h]
        y = exact(mix[h], x)
        rows_ref[:, at] = q_ref[:, at].astype(f32) - y[:, :HW]
        rows_ref[:, (2 + h) * HW : (3 + h) * HW] = y[:, HW:]
        ab = exact(k_ref[:, at].astype(f32) * columns[h], x, ((0,), (0,)))
        maps.append(identity(2 * HW) + jnp.where(left_half(ab.shape), -ab, ab))
    first = core == 0
    keep_ref[...] = jnp.where(first, maps[0], maps[1])
    send_ref[...] = jnp.where(first, maps[1], maps[0])
    copies[4].wait()


def chip_map(core_ref, keep_ref, got_ref, out_ref):
    first = core_ref[0] == 0
    early = jnp.where(first, keep_ref[...], got_ref[...])
    late = jnp.where(first, got_ref[...], keep_ref[...])
    out_ref[...] = after(late, early)


def join_chips(z_ref, own_ref, got_ref, both_ref, pre_ref):
    upper = lax.rem(z_ref[0], 2) == 1
    low = jnp.where(upper, got_ref[...], own_ref[...])
    high = jnp.where(upper, own_ref[...], got_ref[...])
    both_ref[...] = after(high, low)
    pre_ref[...] = jnp.where(upper, low, identity(2 * HW))


def join_pairs(z_ref, own_ref, got_ref, pre_in_ref, both_ref, pre_ref):
    upper = lax.rem(z_ref[0], 4) >= 2
    low = jnp.where(upper, got_ref[...], own_ref[...])
    high = jnp.where(upper, own_ref[...], got_ref[...])
    both_ref[...] = after(high, low)
    pre = pre_in_ref[...]
    pre_ref[...] = jnp.where(upper, after(pre, low), pre)


def join_ring(z_ref, own_ref, got_ref, pre_in_ref, first_ref, end_ref, pre_ref):
    upper = z_ref[0] >= 4
    low = jnp.where(upper, got_ref[...], own_ref[...])
    high = jnp.where(upper, own_ref[...], got_ref[...])
    end_ref[...] = applied(high, applied(low, first_ref[...]))
    pre = pre_in_ref[...]
    pre_ref[...] = jnp.where(upper, after(pre, low), pre)


def shard_prefixes(core_ref, pre_ref, keep_ref, got_ref, mine_ref, other_ref):
    first = core_ref[0] == 0
    pre = pre_ref[...]
    middle = after(jnp.where(first, keep_ref[...], got_ref[...]), pre)
    mine_ref[...] = jnp.where(first, pre, middle)
    other_ref[...] = jnp.where(first, middle, pre)


def shard_states(x_hi_ref, mine_ref, other_ref, arrived_ref, first_ref, keep_ref, send_ref):
    state = jnp.where(x_hi_ref[0] == 0, first_ref[...], arrived_ref[...])
    send_ref[...] = applied(other_ref[...], state)
    keep_ref[...] = applied(mine_ref[...], state)


def outputs(core_ref, keep_ref, got_ref, rows_ref, z_ref):
    core = core_ref[0]
    for h in range(2):
        state = jnp.where(core == h, keep_ref[...], got_ref[...])
        at = slice(h * HW, (h + 1) * HW)
        z = exact(rows_ref[:, at], state) + rows_ref[:, (2 + h) * HW : (3 + h) * HW]
        z_ref[:, at] = z.astype(bf16).astype(f32)


def pair_weights(to_ref, near_in, far_in, later_ref, near_ref, far_ref):
    del to_ref, later_ref
    near_ref[...] = near_in[...].astype(f32)
    far_ref[...] = far_in[...].astype(f32)


def own_weights(to_ref, w_ref, later_ref, out_ref):
    del to_ref, later_ref
    out_ref[...] = w_ref[...]


def piece(place, offset, z, z_pair, w_ref, *pair_refs):
    core_ref, y_ref = place
    chunk = w_ref.shape[1] // SIZES[4]
    at = pl.ds(pl.multiple_of(lax.rem(y_ref[0] + (offset + SIZES[4]), SIZES[4]) * chunk, HW), chunk)
    first = core_ref[0] == 0
    parts = []
    for mine, other in (pair_refs[:2], pair_refs[2:]):
        a, b = mine[:, at], other[:, at]
        parts += [jnp.where(first, a, b), jnp.where(first, b, a)]
    return single(z, w_ref[:, at]) + single(z_pair, jnp.concatenate(parts, axis=0).astype(bf16))


def farthest(core_ref, y_ref, z_ref, zx_ref, w_ref, p0, p1, p2, p3, low_ref, high_ref):
    half = low_ref.shape[0]
    z, zx = z_ref[...].astype(bf16), zx_ref[...].astype(bf16)
    out = piece((core_ref, y_ref), 4, z, zx, w_ref, p0, p1, p2, p3)
    low_ref[...] = out[:half]
    high_ref[...] = out[half:]


OFFSETS = (-3, 3, -2, 2, -1, 1, 0)


def nearer(core_ref, y_ref, z_ref, zx_ref, w_ref, p0, p1, p2, p3, *out_refs):
    z, zx = z_ref[...].astype(bf16), zx_ref[...].astype(bf16)
    for offset, out_ref in zip(OFFSETS, out_refs):
        out_ref[...] = piece((core_ref, y_ref), offset, z, zx, w_ref, p0, p1, p2, p3)


def swapped(x, axes):
    n = 2 ** len(axes)
    return lax.ppermute(x, axes, [(i, n - 1 - i) for i in range(n)])


def passed(x, axis, by):
    n = lax.axis_size(axis)
    return lax.ppermute(x, axis, [(i, (i + by) % n) for i in range(n)])


def local(queries, keys, values, rates, init_weight, out_weight):
    rows = queries.shape[0]
    x_hi, z, core, x_lo, y = (lax.axis_index(a).reshape(1) for a in (XH, Z, CORE, XL, Y))
    columns = out_weight.shape[1] // SIZES[3]
    chunk = columns // SIZES[4]
    square, wide, out_piece = ((HW, HW), f32), ((HW, 2 * HW), f32), ((rows, chunk), f32)

    keep, send, own_rows, first = call(
        shard_maps, [wide, wide, ((rows, 4 * HW), f32), square], [core],
        queries, keys, values, rates, init_weight,
        scratch=[pltpu.VMEM((rows, 2 * HW), bf16)] * 3
        + [pltpu.VMEM((2, rows), f32), pltpu.VMEM((2, rows, 2 * HW), f32)]
        + [pltpu.SemaphoreType.DMA] * 5,
        space=pltpu.HBM, limit=8, us=3,
    )
    got = swapped(send, (CORE,))

    def across_z(x, to):
        return lax.ppermute(x, Z, [(i, to(i)) for i in range(SIZES[1])])

    (chip,) = call(chip_map, [wide], [core], keep, got)
    parts = 2
    share = HW // 2
    near_out, far_out = pl.pallas_call(
        pair_weights,
        grid_spec=pltpu.PrefetchScalarGridSpec(
            num_scalar_prefetch=1,
            grid=(parts,),
            in_specs=[
                pl.BlockSpec((share, columns // parts), lambda i, to: (to[1], to[0] * parts + i)),
                pl.BlockSpec((share, columns // parts), lambda i, to: (to[1] + 2, to[0] * parts + i)),
                pl.BlockSpec(memory_space=pl.ANY),
            ],
            out_specs=[pl.BlockSpec((share, columns // parts), lambda i, to: (0, i))] * 2,
        ),
        out_shape=[jax.ShapeDtypeStruct((share, columns), f32)] * 2,
        compiler_params=pltpu.CompilerParams(vmem_limit_bytes=6 * MIB),
    )(jnp.concatenate([1 - x_lo, core]), out_weight, out_weight, chip)
    near = swapped(near_out, (XL,))
    far = swapped(far_out, (XH, XL))
    near_other, far_other = swapped(near, (CORE,)), swapped(far, (CORE,))
    own_half = pl.pallas_call(
        own_weights,
        grid_spec=pltpu.PrefetchScalarGridSpec(
            num_scalar_prefetch=1,
            grid=(4,),
            in_specs=[
                pl.BlockSpec((2 * HW, columns // 4), lambda i, to: (0, to[0] * 4 + i)),
                pl.BlockSpec(memory_space=pl.ANY),
            ],
            out_specs=pl.BlockSpec((2 * HW, columns // 4), lambda i, to: (0, i)),
        ),
        out_shape=jax.ShapeDtypeStruct((2 * HW, columns), bf16),
        compiler_params=pltpu.CompilerParams(vmem_limit_bytes=6 * MIB),
    )(x_lo, out_weight, near_out)

    both, pre = call(join_chips, [wide, wide], [z], chip, across_z(chip, lambda i: i ^ 1), later=[near_out], us=2.5)
    four, pre = call(join_pairs, [wide, wide], [z], both, across_z(both, lambda i: i ^ 2), pre, later=[own_half], us=2.5)
    end, pre = call(join_ring, [square, wide], [z], four, across_z(four, lambda i: 7 - i), pre, first, us=2.5)
    arrived = lax.ppermute(end, XH, [(0, 1)])
    mine, other = call(shard_prefixes, [wide, wide], [core], pre, keep, got, us=2.5)
    kept, leaving = call(shard_states, [square, square], [x_hi], mine, other, arrived, first, us=2.5)
    (z_rows,) = call(outputs, [((rows, 2 * HW), f32)], [core], kept, swapped(leaving, (CORE,)), own_rows)
    z_pair = swapped(z_rows, (XL,))

    factors = (z_rows, z_pair, own_half, near, near_other, far, far_other)
    low, high = call(farthest, [((rows // 2, chunk), f32)] * 2, [core, y], *factors, limit=16)
    down, up = passed(low, Y, -1), passed(high, Y, 1)
    pieces = call(nearer, [out_piece] * len(OFFSETS), [core, y], *factors, later=[low], limit=16)
    down = pieces[0] + jnp.concatenate([down, jnp.zeros_like(down)], axis=0)
    up = pieces[1] + jnp.concatenate([jnp.zeros_like(up), up], axis=0)
    for i in (2, 4):
        down = passed(down, Y, -1) + pieces[i]
        up = passed(up, Y, 1) + pieces[i + 1]
    return (passed(down, Y, -1) + passed(up, Y, 1) + pieces[6]).astype(bf16)


def solution(mesh):
    fine = Mesh(mesh.devices.reshape(SIZES), (XH, Z, CORE, XL, Y))
    ctx, tp = (XH, Z, CORE), (XL, Y)
    in_specs = (P(ctx, tp), P(ctx, tp), P(ctx, tp), P(tp, ctx), P(tp, None, None), P(tp, None))
    return jax.shard_map(local, mesh=fine, in_specs=in_specs, out_specs=P(ctx, tp), check_vma=False)
```

```python
import jax
import jax.numpy as jnp
from jax import lax
from jax.experimental import pallas as pl
from jax.experimental.pallas import tpu as pltpu
from jax.sharding import Mesh, PartitionSpec as P

MB = 16
HW = 128
XH, Z, CORE, XL, Y = "xh", "z", "core", "xl", "y"
SIZES = (2, 8, 2, 2, 8)
f32 = jnp.float32
bf16 = jnp.bfloat16
VM = pl.BlockSpec(memory_space=pltpu.VMEM)
SM = pl.BlockSpec(memory_space=pltpu.SMEM)
MIB = 2**20


def exact(a, b, contract=((1,), (0,))):
    return lax.dot_general(
        a, b, (contract, ((), ())), precision=lax.Precision.HIGH, preferred_element_type=f32
    )


def single(a, b, contract=((1,), (0,))):
    return lax.dot_general(a, b, (contract, ((), ())), preferred_element_type=f32)


def call(kernel, out_shapes, place, *args, later=(), scratch=(), limit=4, us=1.0, space=pltpu.VMEM, pinned=False):
    outs = [pltpu.VMEM(s, d) if pinned else jax.ShapeDtypeStruct(s, d) for s, d in out_shapes]
    n = len(place) + len(args)

    def body(*refs):
        kernel(*refs[:n], *refs[n + len(later) :])

    return pl.pallas_call(
        body,
        out_shape=outs,
        in_specs=[SM] * len(place) + [pl.BlockSpec(memory_space=space)] * len(args) + [pl.BlockSpec(memory_space=pl.ANY)] * len(later),
        out_specs=[VM] * len(outs),
        scratch_shapes=list(scratch),
        compiler_params=pltpu.CompilerParams(vmem_limit_bytes=limit * MIB),
        cost_estimate=pl.CostEstimate(flops=int(us * 1e9), bytes_accessed=1 << 17, transcendentals=0),
    )(*place, *(pltpu.with_memory_space_constraint(x, space) for x in args), *later)


def left_half(shape):
    return lax.broadcasted_iota(jnp.int32, shape, 1) < HW


def identity(columns):
    rows_at = lax.broadcasted_iota(jnp.int32, (HW, columns), 0)
    return (rows_at == lax.broadcasted_iota(jnp.int32, (HW, columns), 1)).astype(f32)


def after(second, first):
    return exact(second[:, :HW], first) + jnp.where(left_half(second.shape), 0.0, second)


def applied(pair, state):
    return exact(pair[:, :HW], state) + pair[:, HW:]


def gathered(copies):
    for copy in copies:
        copy.start()
    return copies


def shard_maps(core_ref, k_hbm, v_hbm, r_hbm, w_hbm, keep_ref, send_ref, x_ref, first_ref, k_ref, v_ref, r_ref, *done):
    copies = gathered(
        [
            pltpu.make_async_copy(source, target, semaphore)
            for source, target, semaphore in zip(
                (k_hbm, v_hbm, r_hbm, w_hbm), (k_ref, v_ref, r_ref, first_ref), done
            )
        ]
    )
    rows = k_ref.shape[0]
    s_at = lax.broadcasted_iota(jnp.int32, (rows, rows), 0)
    t_at = lax.broadcasted_iota(jnp.int32, (rows, rows), 1)
    earlier_block = (t_at // MB) < (s_at // MB)
    diagonal = t_at == s_at
    key_gram, columns = [], []
    for copy in copies[:3]:
        copy.wait()
    for h in range(2):
        at = slice(h * HW, (h + 1) * HW)
        k, r = k_ref[:, at], r_ref[h : h + 1, :]
        columns.append(jnp.sum(jnp.where(diagonal, r, 0.0), axis=1, keepdims=True))
        key_gram.append(jnp.where(earlier_block, single(k, k, ((1,), (1,))) * r, 0.0))
        x_ref[h, :, :HW] = k.astype(f32)
        x_ref[h, :, HW:] = v_ref[:, at].astype(f32)
    for i in range(1, rows // MB):
        at = slice(i * MB, (i + 1) * MB)
        for h in range(2):
            x_ref[h, at, :] = x_ref[h, at, :] - exact(key_gram[h][at, :], x_ref[h])
    maps = []
    for h in range(2):
        at = slice(h * HW, (h + 1) * HW)
        ab = exact(k_ref[:, at].astype(f32) * columns[h], x_ref[h], ((0,), (0,)))
        maps.append(identity(2 * HW) + jnp.where(left_half(ab.shape), -ab, ab))
    first = core_ref[0] == 0
    keep_ref[...] = jnp.where(first, maps[0], maps[1])
    send_ref[...] = jnp.where(first, maps[1], maps[0])
    copies[3].wait()


def shard_rows(q_ref, k_ref, r_ref, x_ref, rows_ref):
    rows = q_ref.shape[0]
    s_at = lax.broadcasted_iota(jnp.int32, (rows, rows), 0)
    t_at = lax.broadcasted_iota(jnp.int32, (rows, rows), 1)
    for h in range(2):
        at = slice(h * HW, (h + 1) * HW)
        q = q_ref[:, at]
        mix = jnp.where(t_at <= s_at, single(q, k_ref[:, at], ((1,), (1,))) * r_ref[h : h + 1, :], 0.0)
        y = exact(mix, x_ref[h])
        rows_ref[:, at] = q.astype(f32) - y[:, :HW]
        rows_ref[:, (2 + h) * HW : (3 + h) * HW] = y[:, HW:]


def chip_map(core_ref, keep_ref, got_ref, out_ref):
    first = core_ref[0] == 0
    early = jnp.where(first, keep_ref[...], got_ref[...])
    late = jnp.where(first, got_ref[...], keep_ref[...])
    out_ref[...] = after(late, early)


def join_chips(z_ref, own_ref, got_ref, both_ref, pre_ref):
    upper = lax.rem(z_ref[0], 2) == 1
    low = jnp.where(upper, got_ref[...], own_ref[...])
    high = jnp.where(upper, own_ref[...], got_ref[...])
    both_ref[...] = after(high, low)
    pre_ref[...] = jnp.where(upper, low, identity(2 * HW))


def join_pairs(z_ref, own_ref, got_ref, pre_in_ref, both_ref, pre_ref):
    upper = lax.rem(z_ref[0], 4) >= 2
    low = jnp.where(upper, got_ref[...], own_ref[...])
    high = jnp.where(upper, own_ref[...], got_ref[...])
    both_ref[...] = after(high, low)
    pre = pre_in_ref[...]
    pre_ref[...] = jnp.where(upper, after(pre, low), pre)


def join_ring(z_ref, core_ref, own_ref, got_ref, pre_in_ref, first_ref, end_ref, pre_ref):
    upper = z_ref[0] >= 4
    low = jnp.where(upper, got_ref[...], own_ref[...])
    high = jnp.where(upper, own_ref[...], got_ref[...])
    end_ref[...] = applied(high, applied(low, first_ref[core_ref[0]]))
    pre = pre_in_ref[...]
    pre_ref[...] = jnp.where(upper, after(pre, low), pre)


def shard_prefixes(core_ref, pre_ref, keep_ref, got_ref, mine_ref, other_ref):
    first = core_ref[0] == 0
    pre = pre_ref[...]
    middle = after(jnp.where(first, keep_ref[...], got_ref[...]), pre)
    mine_ref[...] = jnp.where(first, pre, middle)
    other_ref[...] = jnp.where(first, middle, pre)


def ring_states(x_hi_ref, core_ref, here_ref, there_ref, first_ref, out_ref):
    for h in range(2):
        arrived = jnp.where(core_ref[0] == h, here_ref[...], there_ref[...])
        out_ref[h] = jnp.where(x_hi_ref[0] == 0, first_ref[h], arrived)


def outputs(core_ref, mine_ref, got_ref, begin_ref, rows_ref, z_ref):
    for h in range(2):
        state = applied(jnp.where(core_ref[0] == h, mine_ref[...], got_ref[...]), begin_ref[h])
        at = slice(h * HW, (h + 1) * HW)
        z = exact(rows_ref[:, at], state) + rows_ref[:, (2 + h) * HW : (3 + h) * HW]
        z_ref[:, at] = z.astype(bf16).astype(f32)


def copied(column_ref, row_ref, w_ref, later_ref, out_ref):
    del column_ref, row_ref, later_ref
    out_ref[...] = w_ref[...].astype(out_ref.dtype)


def weight_share(weight, column, row, rows, dtype, later):
    columns, parts = weight.shape[1] // SIZES[3], 2
    return pl.pallas_call(
        copied,
        grid_spec=pltpu.PrefetchScalarGridSpec(
            num_scalar_prefetch=2,
            grid=(parts,),
            in_specs=[
                pl.BlockSpec((rows, columns // parts), lambda i, c, r: (r[0], c[0] * parts + i)),
                pl.BlockSpec(memory_space=pl.ANY),
            ],
            out_specs=pl.BlockSpec((rows, columns // parts), lambda i, c, r: (0, i)),
        ),
        out_shape=jax.ShapeDtypeStruct((rows, columns), dtype),
        compiler_params=pltpu.CompilerParams(vmem_limit_bytes=8 * MIB),
    )(column, row, weight, later)


def piece(place, offset, z, z_pair, w_ref, *pair_refs):
    core_ref, y_ref = place
    chunk = w_ref.shape[1] // SIZES[4]
    at = pl.ds(pl.multiple_of(lax.rem(y_ref[0] + (offset + SIZES[4]), SIZES[4]) * chunk, HW), chunk)
    first = core_ref[0] == 0
    parts = []
    for mine, other in (pair_refs[:2], pair_refs[2:]):
        a, b = mine[:, at], other[:, at]
        parts += [jnp.where(first, a, b), jnp.where(first, b, a)]
    return single(z, w_ref[:, at]) + single(z_pair, jnp.concatenate(parts, axis=0).astype(bf16))


def farthest(core_ref, y_ref, z_ref, zx_ref, w_ref, p0, p1, p2, p3, low_ref, high_ref):
    half = low_ref.shape[0]
    z, zx = z_ref[...].astype(bf16), zx_ref[...].astype(bf16)
    out = piece((core_ref, y_ref), 4, z, zx, w_ref, p0, p1, p2, p3)
    low_ref[...] = out[:half]
    high_ref[...] = out[half:]


OFFSETS = (-3, 3, -2, 2, -1, 1, 0)


def nearer(core_ref, y_ref, z_ref, zx_ref, w_ref, p0, p1, p2, p3, *out_refs):
    z, zx = z_ref[...].astype(bf16), zx_ref[...].astype(bf16)
    for offset, out_ref in zip(OFFSETS, out_refs):
        out_ref[...] = piece((core_ref, y_ref), offset, z, zx, w_ref, p0, p1, p2, p3)


def swapped(x, axes):
    n = 2 ** len(axes)
    return lax.ppermute(x, axes, [(i, n - 1 - i) for i in range(n)])


def passed(x, axis, by):
    n = lax.axis_size(axis)
    return lax.ppermute(x, axis, [(i, (i + by) % n) for i in range(n)])


def local(queries, keys, values, rates, init_weight, out_weight):
    rows = queries.shape[0]
    x_hi, z, core, x_lo, y = (lax.axis_index(a).reshape(1) for a in (XH, Z, CORE, XL, Y))
    columns = out_weight.shape[1] // SIZES[3]
    chunk = columns // SIZES[4]
    square, wide, out_piece = ((HW, HW), f32), ((HW, 2 * HW), f32), ((rows, chunk), f32)

    share = HW // 2
    keep, send, solved, first = call(
        shard_maps, [wide, wide, ((2, rows, 2 * HW), f32), ((2, HW, HW), f32)], [core],
        keys, values, rates, init_weight,
        scratch=[pltpu.VMEM((rows, 2 * HW), bf16)] * 2
        + [pltpu.VMEM((2, rows), f32)] + [pltpu.SemaphoreType.DMA] * 4,
        space=pltpu.HBM, limit=8, us=3,
    )
    got = swapped(send, (CORE,))

    def across_z(x, to):
        return lax.ppermute(x, Z, [(i, to(i)) for i in range(SIZES[1])])

    (chip,) = call(chip_map, [wide], [core], keep, got)
    (own_rows,) = call(shard_rows, [((rows, 4 * HW), f32)], [], queries, keys, rates, solved, later=[chip])
    near_out = weight_share(out_weight, 1 - x_lo, core, share, f32, chip)
    near = swapped(near_out, (XL,))
    both, pre = call(
        join_chips, [wide, wide], [z], chip, across_z(chip, lambda i: i ^ 1), later=[near_out, own_rows], us=2.5
    )
    far_out = weight_share(out_weight, 1 - x_lo, core + 2, share, f32, both)
    far = swapped(far_out, (XH, XL))
    four, pre = call(
        join_pairs, [wide, wide], [z], both, across_z(both, lambda i: i ^ 2), pre, later=[far_out], us=3
    )
    own_half = weight_share(out_weight, x_lo, 0 * core, 2 * HW, bf16, four)
    end, pre = call(
        join_ring, [square, wide], [z, core], four, across_z(four, lambda i: 7 - i), pre, first, later=[own_half], us=6
    )
    near_other, far_other = swapped(near, (CORE,)), swapped(far, (CORE,))
    here = lax.ppermute(end, (XH, CORE), [(0, 2), (1, 3)])
    there = lax.ppermute(end, (XH, CORE), [(0, 3), (1, 2)])
    mine, other = call(shard_prefixes, [wide, wide], [core], pre, keep, got, us=0.1)
    (begin,) = call(ring_states, [((2, HW, HW), f32)], [x_hi, core], here, there, first, us=5)
    (z_rows,) = call(
        outputs, [((rows, 2 * HW), f32)], [core], mine, swapped(other, (CORE,)), begin, own_rows, us=5
    )
    z_pair = swapped(z_rows, (XL,))

    factors = (z_rows, z_pair, own_half, near, near_other, far, far_other)
    low, high = call(farthest, [((rows // 2, chunk), f32)] * 2, [core, y], *factors, limit=16)
    down, up = passed(low, Y, -1), passed(high, Y, 1)
    pieces = call(nearer, [out_piece] * len(OFFSETS), [core, y], *factors, later=[low], limit=16)
    down = pieces[0] + jnp.concatenate([down, jnp.zeros_like(down)], axis=0)
    up = pieces[1] + jnp.concatenate([jnp.zeros_like(up), up], axis=0)
    for i in (2, 4):
        down = passed(down, Y, -1) + pieces[i]
        up = passed(up, Y, 1) + pieces[i + 1]
    return (passed(down, Y, -1) + passed(up, Y, 1) + pieces[6]).astype(bf16)


def solution(mesh):
    fine = Mesh(mesh.devices.reshape(SIZES), (XH, Z, CORE, XL, Y))
    ctx, tp = (XH, Z, CORE), (XL, Y)
    in_specs = (P(ctx, tp), P(ctx, tp), P(ctx, tp), P(tp, ctx), P(tp, None, None), P(tp, None))
    return jax.shard_map(local, mesh=fine, in_specs=in_specs, out_specs=P(ctx, tp), check_vma=False)
```

```python
import jax
import jax.numpy as jnp
from jax import lax
from jax.experimental import pallas as pl
from jax.experimental.pallas import tpu as pltpu
from jax.sharding import Mesh, PartitionSpec as P

MB = 16
HW = 128
XH, Z, CORE, XL, Y = "xh", "z", "core", "xl", "y"
SIZES = (2, 8, 2, 2, 8)
f32 = jnp.float32
bf16 = jnp.bfloat16
VM = pl.BlockSpec(memory_space=pltpu.VMEM)
SM = pl.BlockSpec(memory_space=pltpu.SMEM)
MIB = 2**20


def exact(a, b, contract=((1,), (0,))):
    return lax.dot_general(
        a, b, (contract, ((), ())), precision=lax.Precision.HIGH, preferred_element_type=f32
    )


def single(a, b, contract=((1,), (0,))):
    return lax.dot_general(a, b, (contract, ((), ())), preferred_element_type=f32)


def call(kernel, out_shapes, place, *args, later=(), scratch=(), limit=4, us=1.0, space=pltpu.VMEM, pinned=False):
    outs = [pltpu.VMEM(s, d) if pinned else jax.ShapeDtypeStruct(s, d) for s, d in out_shapes]
    n = len(place) + len(args)

    def body(*refs):
        kernel(*refs[:n], *refs[n + len(later) :])

    return pl.pallas_call(
        body,
        name=kernel.__name__,
        out_shape=outs,
        in_specs=[SM] * len(place) + [pl.BlockSpec(memory_space=space)] * len(args) + [pl.BlockSpec(memory_space=pl.ANY)] * len(later),
        out_specs=[VM] * len(outs),
        scratch_shapes=list(scratch),
        compiler_params=pltpu.CompilerParams(vmem_limit_bytes=limit * MIB),
        cost_estimate=pl.CostEstimate(flops=int(us * 1e9), bytes_accessed=1 << 17, transcendentals=0),
    )(*place, *(pltpu.with_memory_space_constraint(x, space) for x in args), *later)


def left_half(shape):
    return lax.broadcasted_iota(jnp.int32, shape, 1) < HW


def identity(columns):
    rows_at = lax.broadcasted_iota(jnp.int32, (HW, columns), 0)
    return (rows_at == lax.broadcasted_iota(jnp.int32, (HW, columns), 1)).astype(f32)


def after(second, first):
    return exact(second[:, :HW], first) + jnp.where(left_half(second.shape), 0.0, second)


def applied(pair, state):
    return exact(pair[:, :HW], state) + pair[:, HW:]


def gathered(copies):
    for copy in copies:
        copy.start()
    return copies


def shard_maps(core_ref, k_hbm, v_hbm, r_hbm, keep_ref, send_ref, x_ref, k_ref, v_ref, r_ref, *done):
    copies = gathered(
        [
            pltpu.make_async_copy(source, target, semaphore)
            for source, target, semaphore in zip(
                (k_hbm, v_hbm, r_hbm), (k_ref, v_ref, r_ref), done
            )
        ]
    )
    rows = k_ref.shape[0]
    s_at = lax.broadcasted_iota(jnp.int32, (rows, rows), 0)
    t_at = lax.broadcasted_iota(jnp.int32, (rows, rows), 1)
    earlier_block = (t_at // MB) < (s_at // MB)
    diagonal = t_at == s_at
    key_gram, columns = [], []
    for copy in copies:
        copy.wait()
    for h in range(2):
        at = slice(h * HW, (h + 1) * HW)
        k, r = k_ref[:, at], r_ref[h : h + 1, :]
        columns.append(jnp.sum(jnp.where(diagonal, r, 0.0), axis=1, keepdims=True))
        key_gram.append(jnp.where(earlier_block, single(k, k, ((1,), (1,))) * r, 0.0))
        x_ref[h, :, :HW] = k.astype(f32)
        x_ref[h, :, HW:] = v_ref[:, at].astype(f32)
    for i in range(1, rows // MB):
        at = slice(i * MB, (i + 1) * MB)
        for h in range(2):
            x_ref[h, at, :] = x_ref[h, at, :] - exact(key_gram[h][at, :], x_ref[h])
    maps = []
    for h in range(2):
        at = slice(h * HW, (h + 1) * HW)
        ab = exact(k_ref[:, at].astype(f32) * columns[h], x_ref[h], ((0,), (0,)))
        maps.append(identity(2 * HW) + jnp.where(left_half(ab.shape), -ab, ab))
    first = core_ref[0] == 0
    keep_ref[...] = jnp.where(first, maps[0], maps[1])
    send_ref[...] = jnp.where(first, maps[1], maps[0])


def shard_rows(q_ref, k_ref, r_ref, x_ref, rows_ref, token_ref):
    token_ref[...] = jnp.zeros_like(token_ref)
    rows = q_ref.shape[0]
    s_at = lax.broadcasted_iota(jnp.int32, (rows, rows), 0)
    t_at = lax.broadcasted_iota(jnp.int32, (rows, rows), 1)
    for h in range(2):
        at = slice(h * HW, (h + 1) * HW)
        q = q_ref[:, at]
        mix = jnp.where(t_at <= s_at, single(q, k_ref[:, at], ((1,), (1,))) * r_ref[h : h + 1, :], 0.0)
        y = exact(mix, x_ref[h])
        rows_ref[:, at] = q.astype(f32) - y[:, :HW]
        rows_ref[:, (2 + h) * HW : (3 + h) * HW] = y[:, HW:]


def in_order(first_core, keep_ref, got_ref):
    keep, got = keep_ref[...], got_ref[...]
    return jnp.where(first_core, keep, got), jnp.where(first_core, got, keep)


def chip_map(core_ref, keep_ref, got_ref, out_ref):
    early, late = in_order(core_ref[0] == 0, keep_ref, got_ref)
    out_ref[...] = after(late, early)


def first_map(core_ref, keep_ref, got_ref, out_ref):
    out_ref[...] = in_order(core_ref[0] == 0, keep_ref, got_ref)[0]


def is_upper(z, span):
    return lax.rem(z, 2 * span) >= span


def halves(upper, own_ref, got_ref):
    own, got = own_ref[...], got_ref[...]
    return jnp.where(upper, got, own), jnp.where(upper, own, got)


def prefixed(upper, low, pre):
    return jnp.where(upper, after(pre, low), pre)


def join_chips(z_ref, own_ref, got_ref, both_ref):
    low, high = halves(is_upper(z_ref[0], 1), own_ref, got_ref)
    both_ref[...] = after(high, low)


def join_pairs(z_ref, own_ref, got_ref, both_ref):
    low, high = halves(is_upper(z_ref[0], 2), own_ref, got_ref)
    both_ref[...] = after(high, low)


def join_ring(z_ref, core_ref, own_ref, got_ref, first_ref, end_ref):
    low, high = halves(is_upper(z_ref[0], 4), own_ref, got_ref)
    end_ref[...] = applied(high, applied(low, first_ref[core_ref[0]]))


def before_chips(z_ref, own_ref, got_ref, pre_ref):
    upper = is_upper(z_ref[0], 1)
    low, _ = halves(upper, own_ref, got_ref)
    pre_ref[...] = jnp.where(upper, low, identity(2 * HW))


def before_pairs(z_ref, own_ref, got_ref, pre_in_ref, pre_ref):
    upper = is_upper(z_ref[0], 2)
    low, _ = halves(upper, own_ref, got_ref)
    pre_ref[...] = prefixed(upper, low, pre_in_ref[...])


def shard_prefixes(z_ref, core_ref, own_ref, got_ref, pre_in_ref, early_ref, mine_ref, other_ref):
    upper = is_upper(z_ref[0], 4)
    low, _ = halves(upper, own_ref, got_ref)
    pre = prefixed(upper, low, pre_in_ref[...])
    middle = after(early_ref[...], pre)
    first = core_ref[0] == 0
    mine_ref[...] = jnp.where(first, pre, middle)
    other_ref[...] = jnp.where(first, middle, pre)


def ring_states(x_hi_ref, core_ref, here_ref, there_ref, first_ref, out_ref):
    for h in range(2):
        arrived = jnp.where(core_ref[0] == h, here_ref[...], there_ref[...])
        out_ref[h] = jnp.where(x_hi_ref[0] == 0, first_ref[h], arrived)


def fetched(in_ref, out_ref):
    out_ref[...] = in_ref[...]


def outputs(core_ref, mine_ref, got_ref, begin_ref, rows_ref, z_ref):
    for h in range(2):
        state = applied(jnp.where(core_ref[0] == h, mine_ref[...], got_ref[...]), begin_ref[h])
        at = slice(h * HW, (h + 1) * HW)
        z = exact(rows_ref[:, at], state) + rows_ref[:, (2 + h) * HW : (3 + h) * HW]
        z_ref[:, at] = z.astype(bf16).astype(f32)


def copied(column_ref, row_ref, w_ref, later_ref, out_ref):
    del column_ref, row_ref, later_ref
    out_ref[...] = w_ref[...].astype(out_ref.dtype)


def weight_share(weight, column, row, rows, dtype, later, name):
    columns, parts = weight.shape[1] // SIZES[3], 2
    return pl.pallas_call(
        copied,
        name=name,
        grid_spec=pltpu.PrefetchScalarGridSpec(
            num_scalar_prefetch=2,
            grid=(parts,),
            in_specs=[
                pl.BlockSpec((rows, columns // parts), lambda i, c, r: (r[0], c[0] * parts + i)),
                pl.BlockSpec(memory_space=pl.ANY),
            ],
            out_specs=pl.BlockSpec((rows, columns // parts), lambda i, c, r: (0, i)),
        ),
        out_shape=jax.ShapeDtypeStruct((rows, columns), dtype),
        compiler_params=pltpu.CompilerParams(vmem_limit_bytes=8 * MIB),
    )(column, row, weight, later)


OFFSETS = (4, -3, 3, -2, 2, -1, 1, 0)


def piece_weights(x_lo_ref, y_ref, core_ref, w_hbm, n0, n1, f0, f1, later_ref, out_ref, own_ref, done):
    del later_ref
    chunk = out_ref.shape[2]
    columns = own_ref.shape[1]
    copy = pltpu.make_async_copy(
        w_hbm.at[:, pl.ds(pl.multiple_of(x_lo_ref[0] * columns, HW), columns)], own_ref, done
    )
    copy.start()
    first = core_ref[0] == 0
    share = HW // 2
    places = [
        pl.ds(pl.multiple_of(lax.rem(y_ref[0] + (o + SIZES[4]), SIZES[4]) * chunk, HW), chunk) for o in OFFSETS
    ]
    for i, at in enumerate(places):
        for j, (mine, other) in enumerate(((n0, n1), (f0, f1))):
            a, b = mine[:, at], other[:, at]
            row = 2 * HW + j * HW
            out_ref[i, row : row + share, :] = jnp.where(first, a, b).astype(bf16)
            out_ref[i, row + share : row + HW, :] = jnp.where(first, b, a).astype(bf16)
    copy.wait()
    for i, at in enumerate(places):
        out_ref[i, : 2 * HW, :] = own_ref[:, at]


def piece(z_ref, zx_ref, w_ref, i):
    return single(z_ref[...].astype(bf16), w_ref[i, : 2 * HW, :]) + single(
        zx_ref[...].astype(bf16), w_ref[i, 2 * HW :, :]
    )


def farthest(z_ref, zx_ref, w_ref, low_ref, high_ref):
    half = low_ref.shape[0]
    out = piece(z_ref, zx_ref, w_ref, 0)
    low_ref[...] = out[:half]
    high_ref[...] = out[half:]


def nearer(z_ref, zx_ref, w_ref, *out_refs):
    for i, out_ref in enumerate(out_refs):
        out_ref[...] = piece(z_ref, zx_ref, w_ref, i + 1)


def swapped(x, axes):
    n = 2 ** len(axes)
    return lax.ppermute(x, axes, [(i, n - 1 - i) for i in range(n)])


def passed(x, axis, by):
    n = lax.axis_size(axis)
    return lax.ppermute(x, axis, [(i, (i + by) % n) for i in range(n)])


def local(queries, keys, values, rates, init_weight, out_weight):
    rows = queries.shape[0]
    x_hi, z, core, x_lo, y = (lax.axis_index(a).reshape(1) for a in (XH, Z, CORE, XL, Y))
    columns = out_weight.shape[1] // SIZES[3]
    chunk = columns // SIZES[4]
    square, wide, out_piece = ((HW, HW), f32), ((HW, 2 * HW), f32), ((rows, chunk), f32)

    share = HW // 2
    keep, send, solved = call(
        shard_maps, [wide, wide, ((2, rows, 2 * HW), f32)], [core],
        keys, values, rates,
        scratch=[pltpu.VMEM((rows, 2 * HW), bf16)] * 2
        + [pltpu.VMEM((2, rows), f32)] + [pltpu.SemaphoreType.DMA] * 3,
        space=pltpu.HBM, limit=8, us=3,
    )
    got = swapped(send, (CORE,))

    def across_z(x, to):
        return lax.ppermute(x, Z, [(i, to(i)) for i in range(SIZES[1])])

    own_rows, token = call(shard_rows, [((rows, 4 * HW), f32), ((8, HW), f32)], [], queries, keys, rates, solved, us=0.1)
    (chip,) = call(chip_map, [wide], [core], keep, got, later=[token])
    (early,) = call(first_map, [wide], [core], keep, got, later=[chip], us=0.1)
    near_out = weight_share(out_weight, 1 - x_lo, core, share, f32, early, "near")
    near = swapped(near_out, (XL,))
    got_chip = across_z(chip, lambda i: i ^ 1)
    (both,) = call(join_chips, [wide], [z], chip, got_chip, later=[near_out, early], us=0.5)
    (pre,) = call(before_chips, [wide], [z], chip, got_chip, later=[both], us=0.1)
    far_out = weight_share(out_weight, 1 - x_lo, core + 2, share, f32, both, "far")
    far = swapped(far_out, (XH, XL))
    got_both = across_z(both, lambda i: i ^ 2)
    (four,) = call(join_pairs, [wide], [z], both, got_both, later=[far_out, pre], us=6)
    (pre,) = call(before_pairs, [wide], [z], both, got_both, pre, later=[four], us=0.1)
    near_other = swapped(near, (CORE,))
    (first,) = call(fetched, [((2, HW, HW), f32)], [], init_weight, later=[four], us=0.1)
    got_four = across_z(four, lambda i: 7 - i)
    (end,) = call(join_ring, [square], [z, core], four, got_four, first, later=[pre], us=6)
    far_other = swapped(far, (CORE,))
    here = lax.ppermute(end, (XH, CORE), [(0, 2), (1, 3)])
    there = lax.ppermute(end, (XH, CORE), [(0, 3), (1, 2)])
    mine, other = call(shard_prefixes, [wide, wide], [z, core], four, got_four, pre, early, later=[end], us=0.1)
    (begin,) = call(ring_states, [((2, HW, HW), f32)], [x_hi, core], here, there, first, us=5)
    (late_rows,) = call(fetched, [((rows, 4 * HW), f32)], [], own_rows, later=[end], us=0.1)
    (z_rows,) = call(
        outputs, [((rows, 2 * HW), f32)], [core], mine, swapped(other, (CORE,)), begin, late_rows, us=1
    )
    z_pair = swapped(z_rows, (XL,))
    weights = pl.pallas_call(
        piece_weights,
        name="piece_weights",
        out_shape=jax.ShapeDtypeStruct((SIZES[4], 4 * HW, chunk), bf16),
        in_specs=[SM] * 3 + [pl.BlockSpec(memory_space=pltpu.HBM)] + [VM] * 4 + [pl.BlockSpec(memory_space=pl.ANY)],
        out_specs=VM,
        scratch_shapes=[pltpu.VMEM((2 * HW, columns), bf16), pltpu.SemaphoreType.DMA],
        compiler_params=pltpu.CompilerParams(vmem_limit_bytes=16 * MIB),
        cost_estimate=pl.CostEstimate(flops=int(0.5 * 1e9), bytes_accessed=1 << 17, transcendentals=0),
    )(
        x_lo, y, core, pltpu.with_memory_space_constraint(out_weight, pltpu.HBM),
        near, near_other, far, far_other, z_rows,
    )

    factors = (z_rows, z_pair, weights)
    low, high = call(farthest, [((rows // 2, chunk), f32)] * 2, [], *factors, limit=16)
    down, up = passed(low, Y, -1), passed(high, Y, 1)
    pieces = call(nearer, [out_piece] * (len(OFFSETS) - 1), [], *factors, later=[low], limit=16)
    down = pieces[0] + jnp.concatenate([down, jnp.zeros_like(down)], axis=0)
    up = pieces[1] + jnp.concatenate([jnp.zeros_like(up), up], axis=0)
    for i in (2, 4):
        down = passed(down, Y, -1) + pieces[i]
        up = passed(up, Y, 1) + pieces[i + 1]
    return (passed(down, Y, -1) + passed(up, Y, 1) + pieces[6]).astype(bf16)


def solution(mesh):
    fine = Mesh(mesh.devices.reshape(SIZES), (XH, Z, CORE, XL, Y))
    ctx, tp = (XH, Z, CORE), (XL, Y)
    in_specs = (P(ctx, tp), P(ctx, tp), P(ctx, tp), P(tp, ctx), P(tp, None, None), P(tp, None))
    return jax.shard_map(local, mesh=fine, in_specs=in_specs, out_specs=P(ctx, tp), check_vma=False)
```

```python
import jax
import jax.numpy as jnp
from jax import lax
from jax.experimental import pallas as pl
from jax.experimental.pallas import tpu as pltpu
from jax.sharding import Mesh, PartitionSpec as P

MB = 16
HW = 128
XH, Z, CORE, XL, Y = "xh", "z", "core", "xl", "y"
SIZES = (2, 8, 2, 2, 8)
f32 = jnp.float32
bf16 = jnp.bfloat16
VM = pl.BlockSpec(memory_space=pltpu.VMEM)
SM = pl.BlockSpec(memory_space=pltpu.SMEM)
MIB = 2**20


def exact(a, b, contract=((1,), (0,))):
    return lax.dot_general(
        a, b, (contract, ((), ())), precision=lax.Precision.HIGH, preferred_element_type=f32
    )


def single(a, b, contract=((1,), (0,))):
    return lax.dot_general(a, b, (contract, ((), ())), preferred_element_type=f32)


def call(kernel, out_shapes, place, *args, later=(), scratch=(), limit=4, us=1.0, space=pltpu.VMEM, pinned=False):
    outs = [pltpu.VMEM(s, d) if pinned else jax.ShapeDtypeStruct(s, d) for s, d in out_shapes]
    n = len(place) + len(args)

    def body(*refs):
        kernel(*refs[:n], *refs[n + len(later) :])

    return pl.pallas_call(
        body,
        name=kernel.__name__,
        out_shape=outs,
        in_specs=[SM] * len(place) + [pl.BlockSpec(memory_space=space)] * len(args) + [pl.BlockSpec(memory_space=pl.ANY)] * len(later),
        out_specs=[VM] * len(outs),
        scratch_shapes=list(scratch),
        compiler_params=pltpu.CompilerParams(vmem_limit_bytes=limit * MIB),
        cost_estimate=pl.CostEstimate(flops=int(us * 1e9), bytes_accessed=1 << 17, transcendentals=0),
    )(*place, *(pltpu.with_memory_space_constraint(x, space) for x in args), *later)


def left_half(shape):
    return lax.broadcasted_iota(jnp.int32, shape, 1) < HW


def identity(columns):
    rows_at = lax.broadcasted_iota(jnp.int32, (HW, columns), 0)
    return (rows_at == lax.broadcasted_iota(jnp.int32, (HW, columns), 1)).astype(f32)


def after(second, first):
    return exact(second[:, :HW], first) + jnp.where(left_half(second.shape), 0.0, second)


def applied(pair, state):
    return exact(pair[:, :HW], state) + pair[:, HW:]


def gathered(copies):
    for copy in copies:
        copy.start()
    return copies


def shard_maps(core_ref, k_hbm, v_hbm, r_hbm, keep_ref, send_ref, x_ref, k_ref, v_ref, r_ref, *done):
    copies = gathered(
        [
            pltpu.make_async_copy(source, target, semaphore)
            for source, target, semaphore in zip(
                (k_hbm, v_hbm, r_hbm), (k_ref, v_ref, r_ref), done
            )
        ]
    )
    rows = k_ref.shape[0]
    s_at = lax.broadcasted_iota(jnp.int32, (rows, rows), 0)
    t_at = lax.broadcasted_iota(jnp.int32, (rows, rows), 1)
    earlier_block = (t_at // MB) < (s_at // MB)
    diagonal = t_at == s_at
    key_gram, columns = [], []
    for copy in copies:
        copy.wait()
    for h in range(2):
        at = slice(h * HW, (h + 1) * HW)
        k, r = k_ref[:, at], r_ref[h : h + 1, :]
        columns.append(jnp.sum(jnp.where(diagonal, r, 0.0), axis=1, keepdims=True))
        key_gram.append(jnp.where(earlier_block, single(k, k, ((1,), (1,))) * r, 0.0))
        x_ref[h, :, :HW] = k.astype(f32)
        x_ref[h, :, HW:] = v_ref[:, at].astype(f32)
    for i in range(1, rows // MB):
        at = slice(i * MB, (i + 1) * MB)
        for h in range(2):
            x_ref[h, at, :] = x_ref[h, at, :] - exact(key_gram[h][at, :], x_ref[h])
    maps = []
    for h in range(2):
        at = slice(h * HW, (h + 1) * HW)
        ab = exact(k_ref[:, at].astype(f32) * columns[h], x_ref[h], ((0,), (0,)))
        maps.append(identity(2 * HW) + jnp.where(left_half(ab.shape), -ab, ab))
    first = core_ref[0] == 0
    keep_ref[...] = jnp.where(first, maps[0], maps[1])
    send_ref[...] = jnp.where(first, maps[1], maps[0])


def shard_rows(q_ref, k_ref, r_ref, x_ref, rows_ref, token_ref):
    token_ref[...] = jnp.zeros_like(token_ref)
    rows = q_ref.shape[0]
    s_at = lax.broadcasted_iota(jnp.int32, (rows, rows), 0)
    t_at = lax.broadcasted_iota(jnp.int32, (rows, rows), 1)
    for h in range(2):
        at = slice(h * HW, (h + 1) * HW)
        q = q_ref[:, at]
        mix = jnp.where(t_at <= s_at, single(q, k_ref[:, at], ((1,), (1,))) * r_ref[h : h + 1, :], 0.0)
        y = exact(mix, x_ref[h])
        rows_ref[:, at] = q.astype(f32) - y[:, :HW]
        rows_ref[:, (2 + h) * HW : (3 + h) * HW] = y[:, HW:]


def in_order(first_core, keep_ref, got_ref):
    keep, got = keep_ref[...], got_ref[...]
    return jnp.where(first_core, keep, got), jnp.where(first_core, got, keep)


def chip_map(core_ref, keep_ref, got_ref, out_ref):
    early, late = in_order(core_ref[0] == 0, keep_ref, got_ref)
    out_ref[...] = after(late, early)


def first_map(core_ref, keep_ref, got_ref, out_ref):
    out_ref[...] = in_order(core_ref[0] == 0, keep_ref, got_ref)[0]


def is_upper(z, span):
    return lax.rem(z, 2 * span) >= span


def halves(upper, own_ref, got_ref):
    own, got = own_ref[...], got_ref[...]
    return jnp.where(upper, got, own), jnp.where(upper, own, got)


def prefixed(upper, low, pre):
    return jnp.where(upper, after(pre, low), pre)


def join_chips(z_ref, own_ref, got_ref, both_ref):
    low, high = halves(is_upper(z_ref[0], 1), own_ref, got_ref)
    both_ref[...] = after(high, low)


def join_pairs(z_ref, own_ref, got_ref, both_ref):
    low, high = halves(is_upper(z_ref[0], 2), own_ref, got_ref)
    both_ref[...] = after(high, low)


def join_ring(z_ref, core_ref, own_ref, got_ref, first_ref, end_ref):
    low, high = halves(is_upper(z_ref[0], 4), own_ref, got_ref)
    end_ref[...] = applied(high, applied(low, first_ref[core_ref[0]]))


def before_chips(z_ref, own_ref, got_ref, pre_ref):
    upper = is_upper(z_ref[0], 1)
    low, _ = halves(upper, own_ref, got_ref)
    pre_ref[...] = jnp.where(upper, low, identity(2 * HW))


def before_pairs(z_ref, own_ref, got_ref, pre_in_ref, pre_ref):
    upper = is_upper(z_ref[0], 2)
    low, _ = halves(upper, own_ref, got_ref)
    pre_ref[...] = prefixed(upper, low, pre_in_ref[...])


def shard_prefixes(z_ref, core_ref, own_ref, got_ref, pre_in_ref, early_ref, mine_ref, other_ref):
    upper = is_upper(z_ref[0], 4)
    low, _ = halves(upper, own_ref, got_ref)
    pre = prefixed(upper, low, pre_in_ref[...])
    middle = after(early_ref[...], pre)
    first = core_ref[0] == 0
    mine_ref[...] = jnp.where(first, pre, middle)
    other_ref[...] = jnp.where(first, middle, pre)


def ring_states(x_hi_ref, core_ref, here_ref, there_ref, first_ref, out_ref):
    for h in range(2):
        arrived = jnp.where(core_ref[0] == h, here_ref[...], there_ref[...])
        out_ref[h] = jnp.where(x_hi_ref[0] == 0, first_ref[h], arrived)


def fetched(in_ref, out_ref):
    out_ref[...] = in_ref[...]


def outputs(core_ref, mine_ref, got_ref, begin_ref, rows_ref, z_ref):
    for h in range(2):
        state = applied(jnp.where(core_ref[0] == h, mine_ref[...], got_ref[...]), begin_ref[h])
        at = slice(h * HW, (h + 1) * HW)
        z = exact(rows_ref[:, at], state) + rows_ref[:, (2 + h) * HW : (3 + h) * HW]
        z_ref[:, at] = z.astype(bf16).astype(f32)


def copied(column_ref, row_ref, w_ref, later_ref, out_ref):
    del column_ref, row_ref, later_ref
    out_ref[...] = w_ref[...].astype(out_ref.dtype)


def weight_share(weight, column, row, rows, dtype, later, name):
    columns, parts = weight.shape[1] // SIZES[3], 2
    return pl.pallas_call(
        copied,
        name=name,
        grid_spec=pltpu.PrefetchScalarGridSpec(
            num_scalar_prefetch=2,
            grid=(parts,),
            in_specs=[
                pl.BlockSpec((rows, columns // parts), lambda i, c, r: (r[0], c[0] * parts + i)),
                pl.BlockSpec(memory_space=pl.ANY),
            ],
            out_specs=pl.BlockSpec((rows, columns // parts), lambda i, c, r: (0, i)),
        ),
        out_shape=jax.ShapeDtypeStruct((rows, columns), dtype),
        compiler_params=pltpu.CompilerParams(vmem_limit_bytes=8 * MIB),
    )(column, row, weight, later)


OFFSETS = (4, -3, 3, -2, 2, -1, 1, 0)


def piece_weights(x_lo_ref, y_ref, core_ref, w_hbm, n0, n1, f0, f1, later_ref, out_ref, own_ref, done):
    del later_ref
    chunk = out_ref.shape[2]
    columns = own_ref.shape[1]
    copy = pltpu.make_async_copy(
        w_hbm.at[:, pl.ds(pl.multiple_of(x_lo_ref[0] * columns, HW), columns)], own_ref, done
    )
    copy.start()
    first = core_ref[0] == 0
    share = HW // 2
    places = [
        pl.ds(pl.multiple_of(lax.rem(y_ref[0] + (o + SIZES[4]), SIZES[4]) * chunk, HW), chunk) for o in OFFSETS
    ]
    for i, at in enumerate(places):
        for j, (mine, other) in enumerate(((n0, n1), (f0, f1))):
            a, b = mine[:, at], other[:, at]
            row = 2 * HW + j * HW
            out_ref[i, row : row + share, :] = jnp.where(first, a, b).astype(bf16)
            out_ref[i, row + share : row + HW, :] = jnp.where(first, b, a).astype(bf16)
    copy.wait()
    for i, at in enumerate(places):
        out_ref[i, : 2 * HW, :] = own_ref[:, at]


def piece(z_ref, zx_ref, w_ref, i):
    return single(z_ref[...].astype(bf16), w_ref[i, : 2 * HW, :]) + single(
        zx_ref[...].astype(bf16), w_ref[i, 2 * HW :, :]
    )


def farthest(z_ref, zx_ref, w_ref, low_ref, high_ref):
    half = low_ref.shape[0]
    out = piece(z_ref, zx_ref, w_ref, 0)
    low_ref[...] = out[:half]
    high_ref[...] = out[half:]


def nearer(z_ref, zx_ref, w_ref, *out_refs):
    for i, out_ref in enumerate(out_refs):
        out_ref[...] = piece(z_ref, zx_ref, w_ref, i + 1)


def swapped(x, axes):
    n = 2 ** len(axes)
    return lax.ppermute(x, axes, [(i, n - 1 - i) for i in range(n)])


def passed(x, axis, by):
    n = lax.axis_size(axis)
    return lax.ppermute(x, axis, [(i, (i + by) % n) for i in range(n)])


def local(queries, keys, values, rates, init_weight, out_weight):
    rows = queries.shape[0]
    x_hi, z, core, x_lo, y = (lax.axis_index(a).reshape(1) for a in (XH, Z, CORE, XL, Y))
    columns = out_weight.shape[1] // SIZES[3]
    chunk = columns // SIZES[4]
    square, wide, out_piece = ((HW, HW), f32), ((HW, 2 * HW), f32), ((rows, chunk), f32)

    share = HW // 2
    keep, send, solved = call(
        shard_maps, [wide, wide, ((2, rows, 2 * HW), f32)], [core],
        keys, values, rates,
        scratch=[pltpu.VMEM((rows, 2 * HW), bf16)] * 2
        + [pltpu.VMEM((2, rows), f32)] + [pltpu.SemaphoreType.DMA] * 3,
        space=pltpu.HBM, limit=8, us=3,
    )
    got = swapped(send, (CORE,))

    def across_z(x, to):
        return lax.ppermute(x, Z, [(i, to(i)) for i in range(SIZES[1])])

    own_rows, token = call(shard_rows, [((rows, 4 * HW), f32), ((8, HW), f32)], [], queries, keys, rates, solved, us=0.1)
    (chip,) = call(chip_map, [wide], [core], keep, got, later=[token])
    (early,) = call(first_map, [wide], [core], keep, got, later=[chip], us=0.1)
    near_out = weight_share(out_weight, 1 - x_lo, core, share, f32, early, "near")
    far_out = weight_share(out_weight, 1 - x_lo, core + 2, share, f32, early, "far")
    near = swapped(near_out, (XL,))
    got_chip = across_z(chip, lambda i: i ^ 1)
    (both,) = call(join_chips, [wide], [z], chip, got_chip, later=[near_out, far_out, early], us=0.6)
    (pre,) = call(before_chips, [wide], [z], chip, got_chip, later=[both], us=0.1)
    far = swapped(far_out, (XH, XL))
    got_both = across_z(both, lambda i: i ^ 2)
    (four,) = call(join_pairs, [wide], [z], both, got_both, later=[pre], us=4)
    (pre,) = call(before_pairs, [wide], [z], both, got_both, pre, later=[four], us=0.1)
    near_other = swapped(near, (CORE,))
    (first,) = call(fetched, [((2, HW, HW), f32)], [], init_weight, later=[four], us=0.1)
    got_four = across_z(four, lambda i: 7 - i)
    (end,) = call(join_ring, [square], [z, core], four, got_four, first, later=[pre], us=3)
    far_other = swapped(far, (CORE,))
    here = lax.ppermute(end, (XH, CORE), [(0, 2), (1, 3)])
    there = lax.ppermute(end, (XH, CORE), [(0, 3), (1, 2)])
    mine, other = call(shard_prefixes, [wide, wide], [z, core], four, got_four, pre, early, later=[end], us=0.1)
    (begin,) = call(ring_states, [((2, HW, HW), f32)], [x_hi, core], here, there, first, us=12)
    (late_rows,) = call(fetched, [((rows, 4 * HW), f32)], [], own_rows, later=[end], us=0.1)
    (z_rows,) = call(
        outputs, [((rows, 2 * HW), f32)], [core], mine, swapped(other, (CORE,)), begin, late_rows, us=8
    )
    z_pair = swapped(z_rows, (XL,))
    weights = pl.pallas_call(
        piece_weights,
        name="piece_weights",
        out_shape=jax.ShapeDtypeStruct((SIZES[4], 4 * HW, chunk), bf16),
        in_specs=[SM] * 3 + [pl.BlockSpec(memory_space=pltpu.HBM)] + [VM] * 4 + [pl.BlockSpec(memory_space=pl.ANY)],
        out_specs=VM,
        scratch_shapes=[pltpu.VMEM((2 * HW, columns), bf16), pltpu.SemaphoreType.DMA],
        compiler_params=pltpu.CompilerParams(vmem_limit_bytes=16 * MIB),
        cost_estimate=pl.CostEstimate(flops=int(3 * 1e9), bytes_accessed=1 << 17, transcendentals=0),
    )(
        x_lo, y, core, pltpu.with_memory_space_constraint(out_weight, pltpu.HBM),
        near, near_other, far, far_other, z_rows,
    )

    factors = (z_rows, z_pair, weights)
    low, high = call(farthest, [((rows // 2, chunk), f32)] * 2, [], *factors, limit=16)
    down, up = passed(low, Y, -1), passed(high, Y, 1)
    pieces = call(nearer, [out_piece] * (len(OFFSETS) - 1), [], *factors, later=[low], limit=16)
    down = pieces[0] + jnp.concatenate([down, jnp.zeros_like(down)], axis=0)
    up = pieces[1] + jnp.concatenate([jnp.zeros_like(up), up], axis=0)
    for i in (2, 4):
        down = passed(down, Y, -1) + pieces[i]
        up = passed(up, Y, 1) + pieces[i + 1]
    return (passed(down, Y, -1) + passed(up, Y, 1) + pieces[6]).astype(bf16)


def solution(mesh):
    fine = Mesh(mesh.devices.reshape(SIZES), (XH, Z, CORE, XL, Y))
    ctx, tp = (XH, Z, CORE), (XL, Y)
    in_specs = (P(ctx, tp), P(ctx, tp), P(ctx, tp), P(tp, ctx), P(tp, None, None), P(tp, None))
    return jax.shard_map(local, mesh=fine, in_specs=in_specs, out_specs=P(ctx, tp), check_vma=False)
```

```python
import jax
import jax.numpy as jnp
from jax import lax
from jax.experimental import pallas as pl
from jax.experimental.pallas import tpu as pltpu
from jax.sharding import Mesh, PartitionSpec as P

MB = 16
HW = 128
XH, Z, CORE, XL, Y = "xh", "z", "core", "xl", "y"
SIZES = (2, 8, 2, 2, 8)
f32 = jnp.float32
bf16 = jnp.bfloat16
VM = pl.BlockSpec(memory_space=pltpu.VMEM)
SM = pl.BlockSpec(memory_space=pltpu.SMEM)
MIB = 2**20


def exact(a, b, contract=((1,), (0,))):
    return lax.dot_general(
        a, b, (contract, ((), ())), precision=lax.Precision.HIGH, preferred_element_type=f32
    )


def single(a, b, contract=((1,), (0,))):
    return lax.dot_general(a, b, (contract, ((), ())), preferred_element_type=f32)


def call(kernel, out_shapes, place, *args, later=(), scratch=(), limit=4, us=1.0, space=pltpu.VMEM, pinned=False):
    outs = [pltpu.VMEM(s, d) if pinned else jax.ShapeDtypeStruct(s, d) for s, d in out_shapes]
    n = len(place) + len(args)

    def body(*refs):
        kernel(*refs[:n], *refs[n + len(later) :])

    return pl.pallas_call(
        body,
        name=kernel.__name__,
        out_shape=outs,
        in_specs=[SM] * len(place) + [pl.BlockSpec(memory_space=space)] * len(args) + [pl.BlockSpec(memory_space=pl.ANY)] * len(later),
        out_specs=[VM] * len(outs),
        scratch_shapes=list(scratch),
        compiler_params=pltpu.CompilerParams(vmem_limit_bytes=limit * MIB),
        cost_estimate=pl.CostEstimate(flops=int(us * 1e9), bytes_accessed=1 << 17, transcendentals=0),
    )(*place, *(pltpu.with_memory_space_constraint(x, space) for x in args), *later)


def left_half(shape):
    return lax.broadcasted_iota(jnp.int32, shape, 1) < HW


def identity(columns):
    rows_at = lax.broadcasted_iota(jnp.int32, (HW, columns), 0)
    return (rows_at == lax.broadcasted_iota(jnp.int32, (HW, columns), 1)).astype(f32)


def after(second, first):
    return exact(second[:, :HW], first) + jnp.where(left_half(second.shape), 0.0, second)


def applied(pair, state):
    return exact(pair[:, :HW], state) + pair[:, HW:]


def gathered(copies):
    for copy in copies:
        copy.start()
    return copies


def shard_maps(core_ref, k_hbm, v_hbm, r_hbm, keep_ref, send_ref, x_ref, k_ref, v_ref, r_ref, *done):
    copies = gathered(
        [
            pltpu.make_async_copy(source, target, semaphore)
            for source, target, semaphore in zip(
                (k_hbm, v_hbm, r_hbm), (k_ref, v_ref, r_ref), done
            )
        ]
    )
    rows = k_ref.shape[0]
    s_at = lax.broadcasted_iota(jnp.int32, (rows, rows), 0)
    t_at = lax.broadcasted_iota(jnp.int32, (rows, rows), 1)
    earlier_block = (t_at // MB) < (s_at // MB)
    diagonal = t_at == s_at
    key_gram, columns = [], []
    for copy in copies:
        copy.wait()
    for h in range(2):
        at = slice(h * HW, (h + 1) * HW)
        k, r = k_ref[:, at], r_ref[h : h + 1, :]
        columns.append(jnp.sum(jnp.where(diagonal, r, 0.0), axis=1, keepdims=True))
        key_gram.append(jnp.where(earlier_block, single(k, k, ((1,), (1,))) * r, 0.0))
        x_ref[h, :, :HW] = k.astype(f32)
        x_ref[h, :, HW:] = v_ref[:, at].astype(f32)
    for i in range(1, rows // MB):
        at = slice(i * MB, (i + 1) * MB)
        for h in range(2):
            x_ref[h, at, :] = x_ref[h, at, :] - exact(key_gram[h][at, :], x_ref[h])
    maps = []
    for h in range(2):
        at = slice(h * HW, (h + 1) * HW)
        ab = exact(k_ref[:, at].astype(f32) * columns[h], x_ref[h], ((0,), (0,)))
        maps.append(identity(2 * HW) + jnp.where(left_half(ab.shape), -ab, ab))
    first = core_ref[0] == 0
    keep_ref[...] = jnp.where(first, maps[0], maps[1])
    send_ref[...] = jnp.where(first, maps[1], maps[0])


def shard_rows(q_ref, k_ref, r_ref, x_ref, rows_ref, token_ref):
    token_ref[...] = jnp.zeros_like(token_ref)
    rows = q_ref.shape[0]
    s_at = lax.broadcasted_iota(jnp.int32, (rows, rows), 0)
    t_at = lax.broadcasted_iota(jnp.int32, (rows, rows), 1)
    for h in range(2):
        at = slice(h * HW, (h + 1) * HW)
        q = q_ref[:, at]
        mix = jnp.where(t_at <= s_at, single(q, k_ref[:, at], ((1,), (1,))) * r_ref[h : h + 1, :], 0.0)
        y = exact(mix, x_ref[h])
        rows_ref[:, at] = q.astype(f32) - y[:, :HW]
        rows_ref[:, (2 + h) * HW : (3 + h) * HW] = y[:, HW:]


def in_order(first_core, keep_ref, got_ref):
    keep, got = keep_ref[...], got_ref[...]
    return jnp.where(first_core, keep, got), jnp.where(first_core, got, keep)


def chip_map(core_ref, keep_ref, got_ref, later_ref, out_ref, early_hbm, early_ref, done):
    del later_ref
    early, late = in_order(core_ref[0] == 0, keep_ref, got_ref)
    early_ref[...] = early
    copy = pltpu.make_async_copy(early_ref, early_hbm, done)
    copy.start()
    out_ref[...] = after(late, early)
    copy.wait()


def is_upper(z, span):
    return lax.rem(z, 2 * span) >= span


def halves(upper, own_ref, got_ref):
    own, got = own_ref[...], got_ref[...]
    return jnp.where(upper, got, own), jnp.where(upper, own, got)


def prefixed(upper, low, pre):
    return jnp.where(upper, after(pre, low), pre)


def join_chips(z_ref, own_ref, got_ref, both_ref):
    low, high = halves(is_upper(z_ref[0], 1), own_ref, got_ref)
    both_ref[...] = after(high, low)


def join_pairs(z_ref, own_ref, got_ref, both_ref):
    low, high = halves(is_upper(z_ref[0], 2), own_ref, got_ref)
    both_ref[...] = after(high, low)


def join_ring(z_ref, core_ref, own_ref, got_ref, first_ref, end_ref):
    low, high = halves(is_upper(z_ref[0], 4), own_ref, got_ref)
    end_ref[...] = applied(high, applied(low, first_ref[core_ref[0]]))


def before_chips(z_ref, own_ref, got_ref, pre_ref):
    upper = is_upper(z_ref[0], 1)
    low, _ = halves(upper, own_ref, got_ref)
    pre_ref[...] = jnp.where(upper, low, identity(2 * HW))


def before_pairs(z_ref, own_ref, got_ref, pre_in_ref, pre_ref):
    upper = is_upper(z_ref[0], 2)
    low, _ = halves(upper, own_ref, got_ref)
    pre_ref[...] = prefixed(upper, low, pre_in_ref[...])


def shard_prefixes(z_ref, core_ref, own_ref, got_ref, pre_in_ref, early_ref, mine_ref, other_ref):
    upper = is_upper(z_ref[0], 4)
    low, _ = halves(upper, own_ref, got_ref)
    pre = prefixed(upper, low, pre_in_ref[...])
    middle = after(early_ref[...], pre)
    first = core_ref[0] == 0
    mine_ref[...] = jnp.where(first, pre, middle)
    other_ref[...] = jnp.where(first, middle, pre)


def ring_states(x_hi_ref, core_ref, here_ref, there_ref, first_ref, out_ref):
    for h in range(2):
        arrived = jnp.where(core_ref[0] == h, here_ref[...], there_ref[...])
        out_ref[h] = jnp.where(x_hi_ref[0] == 0, first_ref[h], arrived)


def fetched(in_ref, out_ref):
    out_ref[...] = in_ref[...]


def outputs(core_ref, mine_ref, got_ref, begin_ref, rows_ref, z_ref):
    for h in range(2):
        state = applied(jnp.where(core_ref[0] == h, mine_ref[...], got_ref[...]), begin_ref[h])
        at = slice(h * HW, (h + 1) * HW)
        z = exact(rows_ref[:, at], state) + rows_ref[:, (2 + h) * HW : (3 + h) * HW]
        z_ref[:, at] = z.astype(bf16).astype(f32)


def share_weights(column_ref, row_ref, near_in, far_in, later_ref, near_ref, far_ref):
    del column_ref, row_ref, later_ref
    near_ref[...] = near_in[...].astype(f32)
    far_ref[...] = far_in[...].astype(f32)


def weight_shares(weight, column, row, rows, later):
    columns, parts = weight.shape[1] // SIZES[3], 2
    return pl.pallas_call(
        share_weights,
        name="share_weights",
        grid_spec=pltpu.PrefetchScalarGridSpec(
            num_scalar_prefetch=2,
            grid=(parts,),
            in_specs=[
                pl.BlockSpec((rows, columns // parts), lambda i, c, r: (r[0], c[0] * parts + i)),
                pl.BlockSpec((rows, columns // parts), lambda i, c, r: (r[0] + 2, c[0] * parts + i)),
                pl.BlockSpec(memory_space=pl.ANY),
            ],
            out_specs=[pl.BlockSpec((rows, columns // parts), lambda i, c, r: (0, i))] * 2,
        ),
        out_shape=[jax.ShapeDtypeStruct((rows, columns), f32)] * 2,
        compiler_params=pltpu.CompilerParams(vmem_limit_bytes=8 * MIB),
    )(column, row, weight, weight, later)


OFFSETS = (4, -3, 3, -2, 2, -1, 1, 0)


def piece_weights(x_lo_ref, y_ref, core_ref, w_hbm, n0, n1, f0, f1, later_ref, out_ref, own_ref, done):
    del later_ref
    chunk = out_ref.shape[2]
    columns = own_ref.shape[1]
    copy = pltpu.make_async_copy(
        w_hbm.at[:, pl.ds(pl.multiple_of(x_lo_ref[0] * columns, HW), columns)], own_ref, done
    )
    copy.start()
    first = core_ref[0] == 0
    share = HW // 2
    places = [
        pl.ds(pl.multiple_of(lax.rem(y_ref[0] + (o + SIZES[4]), SIZES[4]) * chunk, HW), chunk) for o in OFFSETS
    ]
    for i, at in enumerate(places):
        for j, (mine, other) in enumerate(((n0, n1), (f0, f1))):
            a, b = mine[:, at], other[:, at]
            row = 2 * HW + j * HW
            out_ref[i, row : row + share, :] = jnp.where(first, a, b).astype(bf16)
            out_ref[i, row + share : row + HW, :] = jnp.where(first, b, a).astype(bf16)
    copy.wait()
    for i, at in enumerate(places):
        out_ref[i, : 2 * HW, :] = own_ref[:, at]


def piece(z_ref, zx_ref, w_ref, i):
    return single(z_ref[...].astype(bf16), w_ref[i, : 2 * HW, :]) + single(
        zx_ref[...].astype(bf16), w_ref[i, 2 * HW :, :]
    )


def farthest(z_ref, zx_ref, w_ref, low_ref, high_ref):
    half = low_ref.shape[0]
    out = piece(z_ref, zx_ref, w_ref, 0)
    low_ref[...] = out[:half]
    high_ref[...] = out[half:]


def nearer(z_ref, zx_ref, w_ref, *out_refs):
    for i, out_ref in enumerate(out_refs):
        out_ref[...] = piece(z_ref, zx_ref, w_ref, i + 1)


def swapped(x, axes):
    n = 2 ** len(axes)
    return lax.ppermute(x, axes, [(i, n - 1 - i) for i in range(n)])


def passed(x, axis, by):
    n = lax.axis_size(axis)
    return lax.ppermute(x, axis, [(i, (i + by) % n) for i in range(n)])


def local(queries, keys, values, rates, init_weight, out_weight):
    rows = queries.shape[0]
    x_hi, z, core, x_lo, y = (lax.axis_index(a).reshape(1) for a in (XH, Z, CORE, XL, Y))
    columns = out_weight.shape[1] // SIZES[3]
    chunk = columns // SIZES[4]
    square, wide, out_piece = ((HW, HW), f32), ((HW, 2 * HW), f32), ((rows, chunk), f32)

    share = HW // 2
    keep, send, solved = call(
        shard_maps, [wide, wide, ((2, rows, 2 * HW), f32)], [core],
        keys, values, rates,
        scratch=[pltpu.VMEM((rows, 2 * HW), bf16)] * 2
        + [pltpu.VMEM((2, rows), f32)] + [pltpu.SemaphoreType.DMA] * 3,
        space=pltpu.HBM, limit=8, us=3,
    )
    got = swapped(send, (CORE,))

    def across_z(x, to):
        return lax.ppermute(x, Z, [(i, to(i)) for i in range(SIZES[1])])

    own_rows, token = call(shard_rows, [((rows, 4 * HW), f32), ((8, HW), f32)], [], queries, keys, rates, solved, us=0.1)
    chip, early = pl.pallas_call(
        chip_map,
        name="chip_map",
        out_shape=[jax.ShapeDtypeStruct((HW, 2 * HW), f32), pltpu.HBM((HW, 2 * HW), f32)],
        in_specs=[SM, VM, VM, pl.BlockSpec(memory_space=pl.ANY)],
        out_specs=[VM, pl.BlockSpec(memory_space=pltpu.HBM)],
        scratch_shapes=[pltpu.VMEM((HW, 2 * HW), f32), pltpu.SemaphoreType.DMA],
        compiler_params=pltpu.CompilerParams(vmem_limit_bytes=4 * MIB),
    )(core, keep, got, token)
    near_out, far_out = weight_shares(out_weight, 1 - x_lo, core, share, chip)
    near = swapped(near_out, (XL,))
    got_chip = across_z(chip, lambda i: i ^ 1)
    (both,) = call(join_chips, [wide], [z], chip, got_chip, later=[near_out], us=0.3)
    (pre,) = call(before_chips, [wide], [z], chip, got_chip, later=[both], us=0.1)
    far = swapped(far_out, (XH, XL))
    got_both = across_z(both, lambda i: i ^ 2)
    (four,) = call(join_pairs, [wide], [z], both, got_both, later=[pre], us=0.3)
    (pre,) = call(before_pairs, [wide], [z], both, got_both, pre, later=[four], us=0.1)
    near_other = swapped(near, (CORE,))
    (first,) = call(fetched, [((2, HW, HW), f32)], [], init_weight, later=[four], us=0.1)
    got_four = across_z(four, lambda i: 7 - i)
    (end,) = call(join_ring, [square], [z, core], four, got_four, first, later=[pre], us=3)
    far_other = swapped(far, (CORE,))
    here = lax.ppermute(end, (XH, CORE), [(0, 2), (1, 3)])
    there = lax.ppermute(end, (XH, CORE), [(0, 3), (1, 2)])
    mine, other = call(shard_prefixes, [wide, wide], [z, core], four, got_four, pre, early, later=[end], us=0.1)
    (begin,) = call(ring_states, [((2, HW, HW), f32)], [x_hi, core], here, there, first, us=12)
    (late_rows,) = call(fetched, [((rows, 4 * HW), f32)], [], own_rows, later=[end], us=0.1)
    (z_rows,) = call(
        outputs, [((rows, 2 * HW), f32)], [core], mine, swapped(other, (CORE,)), begin, late_rows, us=4
    )
    z_pair = swapped(z_rows, (XL,))
    weights = pl.pallas_call(
        piece_weights,
        name="piece_weights",
        out_shape=jax.ShapeDtypeStruct((SIZES[4], 4 * HW, chunk), bf16),
        in_specs=[SM] * 3 + [pl.BlockSpec(memory_space=pltpu.HBM)] + [VM] * 4 + [pl.BlockSpec(memory_space=pl.ANY)],
        out_specs=VM,
        scratch_shapes=[pltpu.VMEM((2 * HW, columns), bf16), pltpu.SemaphoreType.DMA],
        compiler_params=pltpu.CompilerParams(vmem_limit_bytes=16 * MIB),
        cost_estimate=pl.CostEstimate(flops=int(3 * 1e9), bytes_accessed=1 << 17, transcendentals=0),
    )(
        x_lo, y, core, pltpu.with_memory_space_constraint(out_weight, pltpu.HBM),
        near, near_other, far, far_other, z_rows,
    )

    factors = (z_rows, z_pair, weights)
    low, high = call(farthest, [((rows // 2, chunk), f32)] * 2, [], *factors, limit=16)
    down, up = passed(low, Y, -1), passed(high, Y, 1)
    pieces = call(nearer, [out_piece] * (len(OFFSETS) - 1), [], *factors, later=[low], limit=16)
    down = pieces[0] + jnp.concatenate([down, jnp.zeros_like(down)], axis=0)
    up = pieces[1] + jnp.concatenate([jnp.zeros_like(up), up], axis=0)
    for i in (2, 4):
        down = passed(down, Y, -1) + pieces[i]
        up = passed(up, Y, 1) + pieces[i + 1]
    return (passed(down, Y, -1) + passed(up, Y, 1) + pieces[6]).astype(bf16)


def solution(mesh):
    fine = Mesh(mesh.devices.reshape(SIZES), (XH, Z, CORE, XL, Y))
    ctx, tp = (XH, Z, CORE), (XL, Y)
    in_specs = (P(ctx, tp), P(ctx, tp), P(ctx, tp), P(tp, ctx), P(tp, None, None), P(tp, None))
    return jax.shard_map(local, mesh=fine, in_specs=in_specs, out_specs=P(ctx, tp), check_vma=False)
```

```python
import jax
import jax.numpy as jnp
from jax import lax
from jax.experimental import pallas as pl
from jax.experimental.pallas import tpu as pltpu
from jax.sharding import Mesh, PartitionSpec as P

MB = 16
HW = 128
XH, Z, CORE, XL, Y = "xh", "z", "core", "xl", "y"
SIZES = (2, 8, 2, 2, 8)
f32 = jnp.float32
bf16 = jnp.bfloat16
VM = pl.BlockSpec(memory_space=pltpu.VMEM)
SM = pl.BlockSpec(memory_space=pltpu.SMEM)
MIB = 2**20


def exact(a, b, contract=((1,), (0,))):
    return lax.dot_general(
        a, b, (contract, ((), ())), precision=lax.Precision.HIGH, preferred_element_type=f32
    )


def single(a, b, contract=((1,), (0,))):
    return lax.dot_general(a, b, (contract, ((), ())), preferred_element_type=f32)


def call(kernel, out_shapes, place, *args, later=(), scratch=(), limit=4, us=1.0, space=pltpu.VMEM, pinned=False):
    outs = [pltpu.VMEM(s, d) if pinned else jax.ShapeDtypeStruct(s, d) for s, d in out_shapes]
    n = len(place) + len(args)

    def body(*refs):
        kernel(*refs[:n], *refs[n + len(later) :])

    return pl.pallas_call(
        body,
        name=kernel.__name__,
        out_shape=outs,
        in_specs=[SM] * len(place) + [pl.BlockSpec(memory_space=space)] * len(args) + [pl.BlockSpec(memory_space=pl.ANY)] * len(later),
        out_specs=[VM] * len(outs),
        scratch_shapes=list(scratch),
        compiler_params=pltpu.CompilerParams(vmem_limit_bytes=limit * MIB),
        cost_estimate=pl.CostEstimate(flops=int(us * 1e9), bytes_accessed=1 << 17, transcendentals=0),
    )(*place, *(pltpu.with_memory_space_constraint(x, space) for x in args), *later)


def left_half(shape):
    return lax.broadcasted_iota(jnp.int32, shape, 1) < HW


def identity(columns):
    rows_at = lax.broadcasted_iota(jnp.int32, (HW, columns), 0)
    return (rows_at == lax.broadcasted_iota(jnp.int32, (HW, columns), 1)).astype(f32)


def after(second, first):
    return exact(second[:, :HW], first) + jnp.where(left_half(second.shape), 0.0, second)


def applied(pair, state):
    return exact(pair[:, :HW], state) + pair[:, HW:]


def gathered(copies):
    for copy in copies:
        copy.start()
    return copies


def shard_maps(core_ref, k_hbm, v_hbm, r_hbm, keep_ref, send_ref, x_ref, k_ref, v_ref, r_ref, *done):
    copies = gathered(
        [
            pltpu.make_async_copy(source, target, semaphore)
            for source, target, semaphore in zip(
                (k_hbm, v_hbm, r_hbm), (k_ref, v_ref, r_ref), done
            )
        ]
    )
    rows = k_ref.shape[0]
    s_at = lax.broadcasted_iota(jnp.int32, (rows, rows), 0)
    t_at = lax.broadcasted_iota(jnp.int32, (rows, rows), 1)
    earlier_block = (t_at // MB) < (s_at // MB)
    diagonal = t_at == s_at
    key_gram, columns = [], []
    for copy in copies:
        copy.wait()
    for h in range(2):
        at = slice(h * HW, (h + 1) * HW)
        k, r = k_ref[:, at], r_ref[h : h + 1, :]
        columns.append(jnp.sum(jnp.where(diagonal, r, 0.0), axis=1, keepdims=True))
        key_gram.append(jnp.where(earlier_block, single(k, k, ((1,), (1,))) * r, 0.0))
        x_ref[h, :, :HW] = k.astype(f32)
        x_ref[h, :, HW:] = v_ref[:, at].astype(f32)
    for i in range(1, rows // MB):
        at = slice(i * MB, (i + 1) * MB)
        for h in range(2):
            x_ref[h, at, :] = x_ref[h, at, :] - exact(key_gram[h][at, :], x_ref[h])
    maps = []
    for h in range(2):
        at = slice(h * HW, (h + 1) * HW)
        ab = exact(k_ref[:, at].astype(f32) * columns[h], x_ref[h], ((0,), (0,)))
        maps.append(identity(2 * HW) + jnp.where(left_half(ab.shape), -ab, ab))
    first = core_ref[0] == 0
    keep_ref[...] = jnp.where(first, maps[0], maps[1])
    send_ref[...] = jnp.where(first, maps[1], maps[0])


def shard_rows(q_ref, k_ref, r_ref, x_ref, rows_ref, token_ref):
    token_ref[...] = jnp.zeros_like(token_ref)
    rows = q_ref.shape[0]
    s_at = lax.broadcasted_iota(jnp.int32, (rows, rows), 0)
    t_at = lax.broadcasted_iota(jnp.int32, (rows, rows), 1)
    for h in range(2):
        at = slice(h * HW, (h + 1) * HW)
        q = q_ref[:, at]
        mix = jnp.where(t_at <= s_at, single(q, k_ref[:, at], ((1,), (1,))) * r_ref[h : h + 1, :], 0.0)
        y = exact(mix, x_ref[h])
        rows_ref[:, at] = q.astype(f32) - y[:, :HW]
        rows_ref[:, (2 + h) * HW : (3 + h) * HW] = y[:, HW:]


def in_order(first_core, keep_ref, got_ref):
    keep, got = keep_ref[...], got_ref[...]
    return jnp.where(first_core, keep, got), jnp.where(first_core, got, keep)


def chip_map(core_ref, keep_ref, got_ref, out_ref):
    early, late = in_order(core_ref[0] == 0, keep_ref, got_ref)
    out_ref[...] = after(late, early)


def first_map(core_ref, keep_ref, got_ref, out_ref):
    out_ref[...] = in_order(core_ref[0] == 0, keep_ref, got_ref)[0]


def is_upper(z, span):
    return lax.rem(z, 2 * span) >= span


def halves(upper, own_ref, got_ref):
    own, got = own_ref[...], got_ref[...]
    return jnp.where(upper, got, own), jnp.where(upper, own, got)


def prefixed(upper, low, pre):
    return jnp.where(upper, after(pre, low), pre)


def join_chips(z_ref, own_ref, got_ref, both_ref):
    low, high = halves(is_upper(z_ref[0], 1), own_ref, got_ref)
    both_ref[...] = after(high, low)


def join_pairs(z_ref, own_ref, got_ref, both_ref):
    low, high = halves(is_upper(z_ref[0], 2), own_ref, got_ref)
    both_ref[...] = after(high, low)


def join_ring(z_ref, core_ref, own_ref, got_ref, first_ref, end_ref):
    low, high = halves(is_upper(z_ref[0], 4), own_ref, got_ref)
    end_ref[...] = applied(high, applied(low, first_ref[core_ref[0]]))


def before_chips(z_ref, own_ref, got_ref, pre_ref):
    upper = is_upper(z_ref[0], 1)
    low, _ = halves(upper, own_ref, got_ref)
    pre_ref[...] = jnp.where(upper, low, identity(2 * HW))


def before_pairs(z_ref, own_ref, got_ref, pre_in_ref, pre_ref):
    upper = is_upper(z_ref[0], 2)
    low, _ = halves(upper, own_ref, got_ref)
    pre_ref[...] = prefixed(upper, low, pre_in_ref[...])


def shard_prefixes(z_ref, core_ref, own_ref, got_ref, pre_in_ref, early_ref, mine_ref, other_ref):
    upper = is_upper(z_ref[0], 4)
    low, _ = halves(upper, own_ref, got_ref)
    pre = prefixed(upper, low, pre_in_ref[...])
    middle = after(early_ref[...], pre)
    first = core_ref[0] == 0
    mine_ref[...] = jnp.where(first, pre, middle)
    other_ref[...] = jnp.where(first, middle, pre)


def ring_states(x_hi_ref, core_ref, here_ref, there_ref, first_ref, out_ref):
    for h in range(2):
        arrived = jnp.where(core_ref[0] == h, here_ref[...], there_ref[...])
        out_ref[h] = jnp.where(x_hi_ref[0] == 0, first_ref[h], arrived)


def fetched(in_ref, out_ref):
    out_ref[...] = in_ref[...]


def outputs(core_ref, mine_ref, got_ref, begin_ref, rows_ref, z_ref):
    for h in range(2):
        state = applied(jnp.where(core_ref[0] == h, mine_ref[...], got_ref[...]), begin_ref[h])
        at = slice(h * HW, (h + 1) * HW)
        z = exact(rows_ref[:, at], state) + rows_ref[:, (2 + h) * HW : (3 + h) * HW]
        z_ref[:, at] = z.astype(bf16).astype(f32)


def copied(column_ref, row_ref, w_ref, later_ref, out_ref):
    del column_ref, row_ref, later_ref
    out_ref[...] = w_ref[...].astype(out_ref.dtype)


def weight_share(weight, column, row, rows, dtype, later, name):
    columns, parts = weight.shape[1] // SIZES[3], 2
    return pl.pallas_call(
        copied,
        name=name,
        grid_spec=pltpu.PrefetchScalarGridSpec(
            num_scalar_prefetch=2,
            grid=(parts,),
            in_specs=[
                pl.BlockSpec((rows, columns // parts), lambda i, c, r: (r[0], c[0] * parts + i)),
                pl.BlockSpec(memory_space=pl.ANY),
            ],
            out_specs=pl.BlockSpec((rows, columns // parts), lambda i, c, r: (0, i)),
        ),
        out_shape=jax.ShapeDtypeStruct((rows, columns), dtype),
        compiler_params=pltpu.CompilerParams(vmem_limit_bytes=8 * MIB),
    )(column, row, weight, later)


OFFSETS = (4, -2, 2, -3, 3, -1, 1, 0)


def piece_weights(x_lo_ref, y_ref, core_ref, w_hbm, n0, n1, f0, f1, later_ref, out_ref, own_ref, done):
    del later_ref
    chunk = out_ref.shape[2]
    columns = own_ref.shape[1]
    copy = pltpu.make_async_copy(
        w_hbm.at[:, pl.ds(pl.multiple_of(x_lo_ref[0] * columns, HW), columns)], own_ref, done
    )
    copy.start()
    first = core_ref[0] == 0
    share = HW // 2
    places = [
        pl.ds(pl.multiple_of(lax.rem(y_ref[0] + (o + SIZES[4]), SIZES[4]) * chunk, HW), chunk) for o in OFFSETS
    ]
    for i, at in enumerate(places):
        for j, (mine, other) in enumerate(((n0, n1), (f0, f1))):
            a, b = mine[:, at], other[:, at]
            row = 2 * HW + j * HW
            out_ref[i, row : row + share, :] = jnp.where(first, a, b).astype(bf16)
            out_ref[i, row + share : row + HW, :] = jnp.where(first, b, a).astype(bf16)
    copy.wait()
    for i, at in enumerate(places):
        out_ref[i, : 2 * HW, :] = own_ref[:, at]


def piece(z_ref, zx_ref, w_ref, i):
    return single(z_ref[...].astype(bf16), w_ref[i, : 2 * HW, :]) + single(
        zx_ref[...].astype(bf16), w_ref[i, 2 * HW :, :]
    )


def leaving(z_ref, zx_ref, w_ref, down_ref, up_ref):
    half = z_ref.shape[0] // 2
    far = piece(z_ref, zx_ref, w_ref, 0)
    down_ref[:half, :] = far[:half]
    up_ref[:half, :] = far[half:]
    down_ref[half:, :] = piece(z_ref, zx_ref, w_ref, 1)
    up_ref[half:, :] = piece(z_ref, zx_ref, w_ref, 2)


def remaining(z_ref, zx_ref, w_ref, *out_refs):
    for i, out_ref in enumerate(out_refs):
        out_ref[...] = piece(z_ref, zx_ref, w_ref, i + 3)


def swapped(x, axes):
    n = 2 ** len(axes)
    return lax.ppermute(x, axes, [(i, n - 1 - i) for i in range(n)])


def passed(x, axis, by):
    n = lax.axis_size(axis)
    return lax.ppermute(x, axis, [(i, (i + by) % n) for i in range(n)])


def local(queries, keys, values, rates, init_weight, out_weight):
    rows = queries.shape[0]
    x_hi, z, core, x_lo, y = (lax.axis_index(a).reshape(1) for a in (XH, Z, CORE, XL, Y))
    columns = out_weight.shape[1] // SIZES[3]
    chunk = columns // SIZES[4]
    square, wide, out_piece = ((HW, HW), f32), ((HW, 2 * HW), f32), ((rows, chunk), f32)

    share = HW // 2
    keep, send, solved = call(
        shard_maps, [wide, wide, ((2, rows, 2 * HW), f32)], [core],
        keys, values, rates,
        scratch=[pltpu.VMEM((rows, 2 * HW), bf16)] * 2
        + [pltpu.VMEM((2, rows), f32)] + [pltpu.SemaphoreType.DMA] * 3,
        space=pltpu.HBM, limit=8, us=3,
    )
    got = swapped(send, (CORE,))

    def across_z(x, to):
        return lax.ppermute(x, Z, [(i, to(i)) for i in range(SIZES[1])])

    own_rows, token = call(shard_rows, [((rows, 4 * HW), f32), ((8, HW), f32)], [], queries, keys, rates, solved, us=0.1)
    (chip,) = call(chip_map, [wide], [core], keep, got, later=[token])
    (early,) = call(first_map, [wide], [core], keep, got, later=[chip], us=0.1)
    near_out = weight_share(out_weight, 1 - x_lo, core, share, f32, early, "near")
    far_out = weight_share(out_weight, 1 - x_lo, core + 2, share, f32, early, "far")
    near = swapped(near_out, (XL,))
    got_chip = across_z(chip, lambda i: i ^ 1)
    (both,) = call(join_chips, [wide], [z], chip, got_chip, later=[near_out, far_out, early], us=0.6)
    (pre,) = call(before_chips, [wide], [z], chip, got_chip, later=[both], us=0.1)
    far = swapped(far_out, (XH, XL))
    got_both = across_z(both, lambda i: i ^ 2)
    (four,) = call(join_pairs, [wide], [z], both, got_both, later=[pre], us=4)
    (pre,) = call(before_pairs, [wide], [z], both, got_both, pre, later=[four], us=0.1)
    near_other = swapped(near, (CORE,))
    (first,) = call(fetched, [((2, HW, HW), f32)], [], init_weight, later=[four], us=0.1)
    got_four = across_z(four, lambda i: 7 - i)
    (end,) = call(join_ring, [square], [z, core], four, got_four, first, later=[pre], us=3)
    far_other = swapped(far, (CORE,))
    here = lax.ppermute(end, (XH, CORE), [(0, 2), (1, 3)])
    there = lax.ppermute(end, (XH, CORE), [(0, 3), (1, 2)])
    mine, other = call(shard_prefixes, [wide, wide], [z, core], four, got_four, pre, early, later=[end], us=0.1)
    (begin,) = call(ring_states, [((2, HW, HW), f32)], [x_hi, core], here, there, first, us=12)
    (late_rows,) = call(fetched, [((rows, 4 * HW), f32)], [], own_rows, later=[end], us=0.1)
    (z_rows,) = call(
        outputs, [((rows, 2 * HW), f32)], [core], mine, swapped(other, (CORE,)), begin, late_rows, us=8
    )
    z_pair = swapped(z_rows, (XL,))
    weights = pl.pallas_call(
        piece_weights,
        name="piece_weights",
        out_shape=jax.ShapeDtypeStruct((SIZES[4], 4 * HW, chunk), bf16),
        in_specs=[SM] * 3 + [pl.BlockSpec(memory_space=pltpu.HBM)] + [VM] * 4 + [pl.BlockSpec(memory_space=pl.ANY)],
        out_specs=VM,
        scratch_shapes=[pltpu.VMEM((2 * HW, columns), bf16), pltpu.SemaphoreType.DMA],
        compiler_params=pltpu.CompilerParams(vmem_limit_bytes=16 * MIB),
        cost_estimate=pl.CostEstimate(flops=int(3 * 1e9), bytes_accessed=1 << 17, transcendentals=0),
    )(
        x_lo, y, core, pltpu.with_memory_space_constraint(out_weight, pltpu.HBM),
        near, near_other, far, far_other, z_rows,
    )

    factors = (z_rows, z_pair, weights)
    half = rows // 2
    down, up = call(leaving, [((half + rows, chunk), f32)] * 2, [], *factors, limit=16)
    down1, up1 = passed(down, Y, -1), passed(up, Y, 1)
    down3, up3, down0, up0, own = call(remaining, [out_piece] * 5, [], *factors, later=[down], limit=16)
    none = jnp.zeros((half, chunk), f32)
    down2 = passed(down3 + jnp.concatenate([down1[:half], none], axis=0), Y, -2)
    up2 = passed(up3 + jnp.concatenate([none, up1[:half]], axis=0), Y, 2)
    down = passed(down0 + down1[half:] + down2, Y, -1)
    up = passed(up0 + up1[half:] + up2, Y, 1)
    return (down + up + own).astype(bf16)


def solution(mesh):
    fine = Mesh(mesh.devices.reshape(SIZES), (XH, Z, CORE, XL, Y))
    ctx, tp = (XH, Z, CORE), (XL, Y)
    in_specs = (P(ctx, tp), P(ctx, tp), P(ctx, tp), P(tp, ctx), P(tp, None, None), P(tp, None))
    return jax.shard_map(local, mesh=fine, in_specs=in_specs, out_specs=P(ctx, tp), check_vma=False)
```

```python
import jax
import jax.numpy as jnp
from jax import lax
from jax.experimental import pallas as pl
from jax.experimental.pallas import tpu as pltpu
from jax.sharding import Mesh, PartitionSpec as P

MB = 16
HW = 128
XH, Z, CORE, XL, Y = "xh", "z", "core", "xl", "y"
SIZES = (2, 8, 2, 2, 8)
f32 = jnp.float32
bf16 = jnp.bfloat16
VM = pl.BlockSpec(memory_space=pltpu.VMEM)
SM = pl.BlockSpec(memory_space=pltpu.SMEM)
MIB = 2**20


def exact(a, b, contract=((1,), (0,))):
    return lax.dot_general(
        a, b, (contract, ((), ())), precision=lax.Precision.HIGH, preferred_element_type=f32
    )


def single(a, b, contract=((1,), (0,))):
    return lax.dot_general(a, b, (contract, ((), ())), preferred_element_type=f32)


def call(kernel, out_shapes, place, *args, later=(), scratch=(), limit=4, us=1.0, space=pltpu.VMEM, pinned=False):
    outs = [pltpu.VMEM(s, d) if pinned else jax.ShapeDtypeStruct(s, d) for s, d in out_shapes]
    n = len(place) + len(args)

    def body(*refs):
        kernel(*refs[:n], *refs[n + len(later) :])

    return pl.pallas_call(
        body,
        name=kernel.__name__,
        out_shape=outs,
        in_specs=[SM] * len(place) + [pl.BlockSpec(memory_space=space)] * len(args) + [pl.BlockSpec(memory_space=pl.ANY)] * len(later),
        out_specs=[VM] * len(outs),
        scratch_shapes=list(scratch),
        compiler_params=pltpu.CompilerParams(vmem_limit_bytes=limit * MIB),
        cost_estimate=pl.CostEstimate(flops=int(us * 1e9), bytes_accessed=1 << 17, transcendentals=0),
    )(*place, *(pltpu.with_memory_space_constraint(x, space) for x in args), *later)


def left_half(shape):
    return lax.broadcasted_iota(jnp.int32, shape, 1) < HW


def identity(columns):
    rows_at = lax.broadcasted_iota(jnp.int32, (HW, columns), 0)
    return (rows_at == lax.broadcasted_iota(jnp.int32, (HW, columns), 1)).astype(f32)


def after(second, first):
    return exact(second[:, :HW], first) + jnp.where(left_half(second.shape), 0.0, second)


def applied(pair, state):
    return exact(pair[:, :HW], state) + pair[:, HW:]


def gathered(copies):
    for copy in copies:
        copy.start()
    return copies


def shard_maps(core_ref, k_hbm, v_hbm, r_hbm, keep_ref, send_ref, x_ref, k_ref, v_ref, r_ref, *done):
    copies = gathered(
        [
            pltpu.make_async_copy(source, target, semaphore)
            for source, target, semaphore in zip(
                (k_hbm, v_hbm, r_hbm), (k_ref, v_ref, r_ref), done
            )
        ]
    )
    rows = k_ref.shape[0]
    s_at = lax.broadcasted_iota(jnp.int32, (rows, rows), 0)
    t_at = lax.broadcasted_iota(jnp.int32, (rows, rows), 1)
    earlier_block = (t_at // MB) < (s_at // MB)
    diagonal = t_at == s_at
    key_gram, columns = [], []
    for copy in copies:
        copy.wait()
    for h in range(2):
        at = slice(h * HW, (h + 1) * HW)
        k, r = k_ref[:, at], r_ref[h : h + 1, :]
        columns.append(jnp.sum(jnp.where(diagonal, r, 0.0), axis=1, keepdims=True))
        key_gram.append(jnp.where(earlier_block, single(k, k, ((1,), (1,))) * r, 0.0))
        x_ref[h, :, :HW] = k.astype(f32)
        x_ref[h, :, HW:] = v_ref[:, at].astype(f32)
    for i in range(1, rows // MB):
        at = slice(i * MB, (i + 1) * MB)
        for h in range(2):
            x_ref[h, at, :] = x_ref[h, at, :] - exact(key_gram[h][at, :], x_ref[h])
    maps = []
    for h in range(2):
        at = slice(h * HW, (h + 1) * HW)
        ab = exact(k_ref[:, at].astype(f32) * columns[h], x_ref[h], ((0,), (0,)))
        maps.append(identity(2 * HW) + jnp.where(left_half(ab.shape), -ab, ab))
    first = core_ref[0] == 0
    keep_ref[...] = jnp.where(first, maps[0], maps[1])
    send_ref[...] = jnp.where(first, maps[1], maps[0])


def shard_rows(q_ref, k_ref, r_ref, x_ref, rows_ref, token_ref):
    token_ref[...] = jnp.zeros_like(token_ref)
    rows = q_ref.shape[0]
    s_at = lax.broadcasted_iota(jnp.int32, (rows, rows), 0)
    t_at = lax.broadcasted_iota(jnp.int32, (rows, rows), 1)
    for h in range(2):
        at = slice(h * HW, (h + 1) * HW)
        q = q_ref[:, at]
        mix = jnp.where(t_at <= s_at, single(q, k_ref[:, at], ((1,), (1,))) * r_ref[h : h + 1, :], 0.0)
        y = exact(mix, x_ref[h])
        rows_ref[:, at] = q.astype(f32) - y[:, :HW]
        rows_ref[:, (2 + h) * HW : (3 + h) * HW] = y[:, HW:]


def in_order(first_core, keep_ref, got_ref):
    keep, got = keep_ref[...], got_ref[...]
    return jnp.where(first_core, keep, got), jnp.where(first_core, got, keep)


def chip_map(core_ref, keep_ref, got_ref, later_ref, out_ref, early_hbm, early_ref, done):
    del later_ref
    early, late = in_order(core_ref[0] == 0, keep_ref, got_ref)
    early_ref[...] = early
    copy = pltpu.make_async_copy(early_ref, early_hbm, done)
    copy.start()
    out_ref[...] = after(late, early)
    copy.wait()


def is_upper(z, span):
    return lax.rem(z, 2 * span) >= span


def halves(upper, own_ref, got_ref):
    own, got = own_ref[...], got_ref[...]
    return jnp.where(upper, got, own), jnp.where(upper, own, got)


def prefixed(upper, low, pre):
    return jnp.where(upper, after(pre, low), pre)


def join_chips(z_ref, own_ref, got_ref, both_ref):
    low, high = halves(is_upper(z_ref[0], 1), own_ref, got_ref)
    both_ref[...] = after(high, low)


def join_pairs(z_ref, own_ref, got_ref, both_ref):
    low, high = halves(is_upper(z_ref[0], 2), own_ref, got_ref)
    both_ref[...] = after(high, low)


def join_ring(z_ref, core_ref, own_ref, got_ref, first_ref, end_ref):
    low, high = halves(is_upper(z_ref[0], 4), own_ref, got_ref)
    end_ref[...] = applied(high, applied(low, first_ref[core_ref[0]]))


def before_chips(z_ref, own_ref, got_ref, pre_ref):
    upper = is_upper(z_ref[0], 1)
    low, _ = halves(upper, own_ref, got_ref)
    pre_ref[...] = jnp.where(upper, low, identity(2 * HW))


def before_pairs(z_ref, own_ref, got_ref, pre_in_ref, pre_ref):
    upper = is_upper(z_ref[0], 2)
    low, _ = halves(upper, own_ref, got_ref)
    pre_ref[...] = prefixed(upper, low, pre_in_ref[...])


def shard_prefixes(z_ref, core_ref, own_ref, got_ref, pre_in_ref, early_ref, mine_ref, other_ref):
    upper = is_upper(z_ref[0], 4)
    low, _ = halves(upper, own_ref, got_ref)
    pre = prefixed(upper, low, pre_in_ref[...])
    middle = after(early_ref[...], pre)
    first = core_ref[0] == 0
    mine_ref[...] = jnp.where(first, pre, middle)
    other_ref[...] = jnp.where(first, middle, pre)


def ring_states(x_hi_ref, core_ref, here_ref, there_ref, first_ref, out_ref):
    for h in range(2):
        arrived = jnp.where(core_ref[0] == h, here_ref[...], there_ref[...])
        out_ref[h] = jnp.where(x_hi_ref[0] == 0, first_ref[h], arrived)


def fetched(in_ref, out_ref):
    out_ref[...] = in_ref[...]


def outputs(core_ref, mine_ref, got_ref, begin_ref, rows_ref, z_ref):
    for h in range(2):
        state = applied(jnp.where(core_ref[0] == h, mine_ref[...], got_ref[...]), begin_ref[h])
        at = slice(h * HW, (h + 1) * HW)
        z = exact(rows_ref[:, at], state) + rows_ref[:, (2 + h) * HW : (3 + h) * HW]
        z_ref[:, at] = z.astype(bf16).astype(f32)


def share_weights(column_ref, row_ref, near_in, far_in, later_ref, near_ref, far_ref):
    del column_ref, row_ref, later_ref
    near_ref[...] = near_in[...].astype(f32)
    far_ref[...] = far_in[...].astype(f32)


def weight_shares(weight, column, row, rows, later):
    columns, parts = weight.shape[1] // SIZES[3], 2
    return pl.pallas_call(
        share_weights,
        name="share_weights",
        grid_spec=pltpu.PrefetchScalarGridSpec(
            num_scalar_prefetch=2,
            grid=(parts,),
            in_specs=[
                pl.BlockSpec((rows, columns // parts), lambda i, c, r: (r[0], c[0] * parts + i)),
                pl.BlockSpec((rows, columns // parts), lambda i, c, r: (r[0] + 2, c[0] * parts + i)),
                pl.BlockSpec(memory_space=pl.ANY),
            ],
            out_specs=[pl.BlockSpec((rows, columns // parts), lambda i, c, r: (0, i))] * 2,
        ),
        out_shape=[jax.ShapeDtypeStruct((rows, columns), f32)] * 2,
        compiler_params=pltpu.CompilerParams(vmem_limit_bytes=8 * MIB),
    )(column, row, weight, weight, later)


OFFSETS = (4, -3, 3, -2, 2, -1, 1, 0)


def piece_weights(x_lo_ref, y_ref, core_ref, w_hbm, n0, n1, f0, f1, later_ref, out_ref, own_ref, done):
    del later_ref
    chunk = out_ref.shape[2]
    columns = own_ref.shape[1]
    copy = pltpu.make_async_copy(
        w_hbm.at[:, pl.ds(pl.multiple_of(x_lo_ref[0] * columns, HW), columns)], own_ref, done
    )
    copy.start()
    first = core_ref[0] == 0
    share = HW // 2
    places = [
        pl.ds(pl.multiple_of(lax.rem(y_ref[0] + (o + SIZES[4]), SIZES[4]) * chunk, HW), chunk) for o in OFFSETS
    ]
    for i, at in enumerate(places):
        for j, (mine, other) in enumerate(((n0, n1), (f0, f1))):
            a, b = mine[:, at], other[:, at]
            row = 2 * HW + j * HW
            out_ref[i, row : row + share, :] = jnp.where(first, a, b).astype(bf16)
            out_ref[i, row + share : row + HW, :] = jnp.where(first, b, a).astype(bf16)
    copy.wait()
    for i, at in enumerate(places):
        out_ref[i, : 2 * HW, :] = own_ref[:, at]


def piece(z_ref, zx_ref, w_ref, i):
    return single(z_ref[...].astype(bf16), w_ref[i, : 2 * HW, :]) + single(
        zx_ref[...].astype(bf16), w_ref[i, 2 * HW :, :]
    )


def farthest(z_ref, zx_ref, w_ref, low_ref, high_ref):
    half = low_ref.shape[0]
    out = piece(z_ref, zx_ref, w_ref, 0)
    low_ref[...] = out[:half]
    high_ref[...] = out[half:]


def nearer(z_ref, zx_ref, w_ref, *out_refs):
    for i, out_ref in enumerate(out_refs):
        out_ref[...] = piece(z_ref, zx_ref, w_ref, i + 1)


def swapped(x, axes):
    n = 2 ** len(axes)
    return lax.ppermute(x, axes, [(i, n - 1 - i) for i in range(n)])


def passed(x, axis, by):
    n = lax.axis_size(axis)
    return lax.ppermute(x, axis, [(i, (i + by) % n) for i in range(n)])


def local(queries, keys, values, rates, init_weight, out_weight):
    rows = queries.shape[0]
    x_hi, z, core, x_lo, y = (lax.axis_index(a).reshape(1) for a in (XH, Z, CORE, XL, Y))
    columns = out_weight.shape[1] // SIZES[3]
    chunk = columns // SIZES[4]
    square, wide, out_piece = ((HW, HW), f32), ((HW, 2 * HW), f32), ((rows, chunk), f32)

    share = HW // 2
    keep, send, solved = call(
        shard_maps, [wide, wide, ((2, rows, 2 * HW), f32)], [core],
        keys, values, rates,
        scratch=[pltpu.VMEM((rows, 2 * HW), bf16)] * 2
        + [pltpu.VMEM((2, rows), f32)] + [pltpu.SemaphoreType.DMA] * 3,
        space=pltpu.HBM, limit=8, us=3,
    )
    got = swapped(send, (CORE,))

    def across_z(x, to):
        return lax.ppermute(x, Z, [(i, to(i)) for i in range(SIZES[1])])

    own_rows, token = call(shard_rows, [((rows, 4 * HW), f32), ((8, HW), f32)], [], queries, keys, rates, solved, us=0.1)
    chip, early = pl.pallas_call(
        chip_map,
        name="chip_map",
        out_shape=[jax.ShapeDtypeStruct((HW, 2 * HW), f32), pltpu.HBM((HW, 2 * HW), f32)],
        in_specs=[SM, VM, VM, pl.BlockSpec(memory_space=pl.ANY)],
        out_specs=[VM, pl.BlockSpec(memory_space=pltpu.HBM)],
        scratch_shapes=[pltpu.VMEM((HW, 2 * HW), f32), pltpu.SemaphoreType.DMA],
        compiler_params=pltpu.CompilerParams(vmem_limit_bytes=4 * MIB),
    )(core, keep, got, token)
    near_out, far_out = weight_shares(out_weight, 1 - x_lo, core, share, chip)
    near = swapped(near_out, (XL,))
    got_chip = across_z(chip, lambda i: i ^ 1)
    (both,) = call(join_chips, [wide], [z], chip, got_chip, later=[near_out], us=2)
    (pre,) = call(before_chips, [wide], [z], chip, got_chip, later=[both], us=0.1)
    far = swapped(far_out, (XH, XL))
    got_both = across_z(both, lambda i: i ^ 2)
    (four,) = call(join_pairs, [wide], [z], both, got_both, later=[pre], us=3)
    (pre,) = call(before_pairs, [wide], [z], both, got_both, pre, later=[four], us=0.1)
    near_other = swapped(near, (CORE,))
    (first,) = call(fetched, [((2, HW, HW), f32)], [], init_weight, later=[four], us=0.1)
    got_four = across_z(four, lambda i: 7 - i)
    (end,) = call(join_ring, [square], [z, core], four, got_four, first, later=[pre], us=2)
    far_other = swapped(far, (CORE,))
    here = lax.ppermute(end, (XH, CORE), [(0, 2), (1, 3)])
    there = lax.ppermute(end, (XH, CORE), [(0, 3), (1, 2)])
    mine, other = call(shard_prefixes, [wide, wide], [z, core], four, got_four, pre, early, later=[end], us=0.1)
    (begin,) = call(ring_states, [((2, HW, HW), f32)], [x_hi, core], here, there, first, us=6)
    (late_rows,) = call(fetched, [((rows, 4 * HW), f32)], [], own_rows, later=[end], us=0.1)
    (z_rows,) = call(
        outputs, [((rows, 2 * HW), f32)], [core], mine, swapped(other, (CORE,)), begin, late_rows, later=[near_other], us=4
    )
    z_pair = swapped(z_rows, (XL,))
    weights = pl.pallas_call(
        piece_weights,
        name="piece_weights",
        out_shape=jax.ShapeDtypeStruct((SIZES[4], 4 * HW, chunk), bf16),
        in_specs=[SM] * 3 + [pl.BlockSpec(memory_space=pltpu.HBM)] + [VM] * 4 + [pl.BlockSpec(memory_space=pl.ANY)],
        out_specs=VM,
        scratch_shapes=[pltpu.VMEM((2 * HW, columns), bf16), pltpu.SemaphoreType.DMA],
        compiler_params=pltpu.CompilerParams(vmem_limit_bytes=16 * MIB),
        cost_estimate=pl.CostEstimate(flops=int(3 * 1e9), bytes_accessed=1 << 17, transcendentals=0),
    )(
        x_lo, y, core, pltpu.with_memory_space_constraint(out_weight, pltpu.HBM),
        near, near_other, far, far_other, z_rows,
    )

    factors = (z_rows, z_pair, weights)
    low, high = call(farthest, [((rows // 2, chunk), f32)] * 2, [], *factors, limit=16)
    down, up = passed(low, Y, -1), passed(high, Y, 1)
    pieces = call(nearer, [out_piece] * (len(OFFSETS) - 1), [], *factors, later=[low], limit=16)
    down = pieces[0] + jnp.concatenate([down, jnp.zeros_like(down)], axis=0)
    up = pieces[1] + jnp.concatenate([jnp.zeros_like(up), up], axis=0)
    for i in (2, 4):
        down = passed(down, Y, -1) + pieces[i]
        up = passed(up, Y, 1) + pieces[i + 1]
    return (passed(down, Y, -1) + passed(up, Y, 1) + pieces[6]).astype(bf16)


def solution(mesh):
    fine = Mesh(mesh.devices.reshape(SIZES), (XH, Z, CORE, XL, Y))
    ctx, tp = (XH, Z, CORE), (XL, Y)
    in_specs = (P(ctx, tp), P(ctx, tp), P(ctx, tp), P(tp, ctx), P(tp, None, None), P(tp, None))
    return jax.shard_map(local, mesh=fine, in_specs=in_specs, out_specs=P(ctx, tp), check_vma=False)
```

```python
import jax
import jax.numpy as jnp
from jax import lax
from jax.experimental import pallas as pl
from jax.experimental.pallas import tpu as pltpu
from jax.sharding import Mesh, PartitionSpec as P

MB = 16
HW = 128
XH, Z, CORE, XL, Y = "xh", "z", "core", "xl", "y"
SIZES = (2, 8, 2, 2, 8)
f32 = jnp.float32
bf16 = jnp.bfloat16
VM = pl.BlockSpec(memory_space=pltpu.VMEM)
SM = pl.BlockSpec(memory_space=pltpu.SMEM)
MIB = 2**20


def exact(a, b, contract=((1,), (0,))):
    return lax.dot_general(
        a, b, (contract, ((), ())), precision=lax.Precision.HIGH, preferred_element_type=f32
    )


def single(a, b, contract=((1,), (0,))):
    return lax.dot_general(a, b, (contract, ((), ())), preferred_element_type=f32)


def call(kernel, out_shapes, place, *args, later=(), scratch=(), limit=4, us=1.0, space=pltpu.VMEM, pinned=False):
    outs = [pltpu.VMEM(s, d) if pinned else jax.ShapeDtypeStruct(s, d) for s, d in out_shapes]
    n = len(place) + len(args)

    def body(*refs):
        kernel(*refs[:n], *refs[n + len(later) :])

    return pl.pallas_call(
        body,
        name=kernel.__name__,
        out_shape=outs,
        in_specs=[SM] * len(place) + [pl.BlockSpec(memory_space=space)] * len(args) + [pl.BlockSpec(memory_space=pl.ANY)] * len(later),
        out_specs=[VM] * len(outs),
        scratch_shapes=list(scratch),
        compiler_params=pltpu.CompilerParams(vmem_limit_bytes=limit * MIB),
        cost_estimate=pl.CostEstimate(flops=int(us * 1e9), bytes_accessed=1 << 17, transcendentals=0),
    )(*place, *(pltpu.with_memory_space_constraint(x, space) for x in args), *later)


def left_half(shape):
    return lax.broadcasted_iota(jnp.int32, shape, 1) < HW


def identity(columns):
    rows_at = lax.broadcasted_iota(jnp.int32, (HW, columns), 0)
    return (rows_at == lax.broadcasted_iota(jnp.int32, (HW, columns), 1)).astype(f32)


def after(second, first):
    return exact(second[:, :HW], first) + jnp.where(left_half(second.shape), 0.0, second)


def applied(pair, state):
    return exact(pair[:, :HW], state) + pair[:, HW:]


def gathered(copies):
    for copy in copies:
        copy.start()
    return copies


def shard_maps(core_ref, k_hbm, v_hbm, r_hbm, keep_ref, send_ref, x_ref, k_ref, v_ref, r_ref, *done):
    copies = gathered(
        [
            pltpu.make_async_copy(source, target, semaphore)
            for source, target, semaphore in zip(
                (k_hbm, v_hbm, r_hbm), (k_ref, v_ref, r_ref), done
            )
        ]
    )
    rows = k_ref.shape[0]
    s_at = lax.broadcasted_iota(jnp.int32, (rows, rows), 0)
    t_at = lax.broadcasted_iota(jnp.int32, (rows, rows), 1)
    earlier_block = (t_at // MB) < (s_at // MB)
    diagonal = t_at == s_at
    key_gram, columns = [], []
    for copy in copies:
        copy.wait()
    for h in range(2):
        at = slice(h * HW, (h + 1) * HW)
        k, r = k_ref[:, at], r_ref[h : h + 1, :]
        columns.append(jnp.sum(jnp.where(diagonal, r, 0.0), axis=1, keepdims=True))
        key_gram.append(jnp.where(earlier_block, single(k, k, ((1,), (1,))) * r, 0.0))
        x_ref[h, :, :HW] = k.astype(f32)
        x_ref[h, :, HW:] = v_ref[:, at].astype(f32)
    for i in range(1, rows // MB):
        at = slice(i * MB, (i + 1) * MB)
        for h in range(2):
            x_ref[h, at, :] = x_ref[h, at, :] - exact(key_gram[h][at, :], x_ref[h])
    maps = []
    for h in range(2):
        at = slice(h * HW, (h + 1) * HW)
        ab = exact(k_ref[:, at].astype(f32) * columns[h], x_ref[h], ((0,), (0,)))
        maps.append(identity(2 * HW) + jnp.where(left_half(ab.shape), -ab, ab))
    first = core_ref[0] == 0
    keep_ref[...] = jnp.where(first, maps[0], maps[1])
    send_ref[...] = jnp.where(first, maps[1], maps[0])


def shard_rows(q_ref, k_ref, r_ref, x_ref, rows_ref, token_ref):
    token_ref[...] = jnp.zeros_like(token_ref)
    rows = q_ref.shape[0]
    s_at = lax.broadcasted_iota(jnp.int32, (rows, rows), 0)
    t_at = lax.broadcasted_iota(jnp.int32, (rows, rows), 1)
    for h in range(2):
        at = slice(h * HW, (h + 1) * HW)
        q = q_ref[:, at]
        mix = jnp.where(t_at <= s_at, single(q, k_ref[:, at], ((1,), (1,))) * r_ref[h : h + 1, :], 0.0)
        y = exact(mix, x_ref[h])
        rows_ref[:, at] = q.astype(f32) - y[:, :HW]
        rows_ref[:, (2 + h) * HW : (3 + h) * HW] = y[:, HW:]


def in_order(first_core, keep_ref, got_ref):
    keep, got = keep_ref[...], got_ref[...]
    return jnp.where(first_core, keep, got), jnp.where(first_core, got, keep)


def chip_map(core_ref, keep_ref, got_ref, later_ref, out_ref, early_hbm, early_ref, done):
    del later_ref
    early, late = in_order(core_ref[0] == 0, keep_ref, got_ref)
    early_ref[...] = early
    copy = pltpu.make_async_copy(early_ref, early_hbm, done)
    copy.start()
    out_ref[...] = after(late, early)
    copy.wait()


def is_upper(z, span):
    return lax.rem(z, 2 * span) >= span


def halves(upper, own_ref, got_ref):
    own, got = own_ref[...], got_ref[...]
    return jnp.where(upper, got, own), jnp.where(upper, own, got)


def prefixed(upper, low, pre):
    return jnp.where(upper, after(pre, low), pre)


def join_chips(z_ref, own_ref, got_ref, both_ref):
    low, high = halves(is_upper(z_ref[0], 1), own_ref, got_ref)
    both_ref[...] = after(high, low)


def join_pairs(z_ref, own_ref, got_ref, both_ref):
    low, high = halves(is_upper(z_ref[0], 2), own_ref, got_ref)
    both_ref[...] = after(high, low)


def join_ring(z_ref, core_ref, own_ref, got_ref, first_ref, end_ref):
    low, high = halves(is_upper(z_ref[0], 4), own_ref, got_ref)
    end_ref[...] = applied(high, applied(low, first_ref[core_ref[0]]))


def before_chips(z_ref, own_ref, got_ref, pre_ref):
    upper = is_upper(z_ref[0], 1)
    low, _ = halves(upper, own_ref, got_ref)
    pre_ref[...] = jnp.where(upper, low, identity(2 * HW))


def before_pairs(z_ref, own_ref, got_ref, pre_in_ref, pre_ref):
    upper = is_upper(z_ref[0], 2)
    low, _ = halves(upper, own_ref, got_ref)
    pre_ref[...] = prefixed(upper, low, pre_in_ref[...])


def shard_prefixes(z_ref, core_ref, own_ref, got_ref, pre_in_ref, early_ref, mine_ref, other_ref):
    upper = is_upper(z_ref[0], 4)
    low, _ = halves(upper, own_ref, got_ref)
    pre = prefixed(upper, low, pre_in_ref[...])
    middle = after(early_ref[...], pre)
    first = core_ref[0] == 0
    mine_ref[...] = jnp.where(first, pre, middle)
    other_ref[...] = jnp.where(first, middle, pre)


def ring_states(x_hi_ref, core_ref, here_ref, there_ref, first_ref, out_ref):
    for h in range(2):
        arrived = jnp.where(core_ref[0] == h, here_ref[...], there_ref[...])
        out_ref[h] = jnp.where(x_hi_ref[0] == 0, first_ref[h], arrived)


def fetched(in_ref, out_ref):
    out_ref[...] = in_ref[...]


def outputs(core_ref, mine_ref, got_ref, begin_ref, rows_ref, z_ref):
    for h in range(2):
        state = applied(jnp.where(core_ref[0] == h, mine_ref[...], got_ref[...]), begin_ref[h])
        at = slice(h * HW, (h + 1) * HW)
        z = exact(rows_ref[:, at], state) + rows_ref[:, (2 + h) * HW : (3 + h) * HW]
        z_ref[:, at] = z.astype(bf16).astype(f32)


def share_weights(column_ref, row_ref, near_in, far_in, later_ref, near_ref, far_ref):
    del column_ref, row_ref, later_ref
    near_ref[...] = near_in[...].astype(f32)
    far_ref[...] = far_in[...].astype(f32)


def weight_shares(weight, column, row, rows, later):
    columns, parts = weight.shape[1] // SIZES[3], 2
    return pl.pallas_call(
        share_weights,
        name="share_weights",
        grid_spec=pltpu.PrefetchScalarGridSpec(
            num_scalar_prefetch=2,
            grid=(parts,),
            in_specs=[
                pl.BlockSpec((rows, columns // parts), lambda i, c, r: (r[0], c[0] * parts + i)),
                pl.BlockSpec((rows, columns // parts), lambda i, c, r: (r[0] + 2, c[0] * parts + i)),
                pl.BlockSpec(memory_space=pl.ANY),
            ],
            out_specs=[pl.BlockSpec((rows, columns // parts), lambda i, c, r: (0, i))] * 2,
        ),
        out_shape=[jax.ShapeDtypeStruct((rows, columns), f32)] * 2,
        compiler_params=pltpu.CompilerParams(vmem_limit_bytes=8 * MIB),
    )(column, row, weight, weight, later)


OFFSETS = (4, -3, 3, -2, 2, -1, 1, 0)


def piece_weights(x_lo_ref, y_ref, core_ref, w_hbm, n0, n1, f0, f1, later_ref, out_ref, own_ref, done):
    del later_ref
    chunk = out_ref.shape[2]
    columns = own_ref.shape[1]
    copy = pltpu.make_async_copy(
        w_hbm.at[:, pl.ds(pl.multiple_of(x_lo_ref[0] * columns, HW), columns)], own_ref, done
    )
    copy.start()
    first = core_ref[0] == 0
    share = HW // 2
    places = [
        pl.ds(pl.multiple_of(lax.rem(y_ref[0] + (o + SIZES[4]), SIZES[4]) * chunk, HW), chunk) for o in OFFSETS
    ]
    for i, at in enumerate(places):
        for j, (mine, other) in enumerate(((n0, n1), (f0, f1))):
            a, b = mine[:, at], other[:, at]
            row = 2 * HW + j * HW
            out_ref[i, row : row + share, :] = jnp.where(first, a, b).astype(bf16)
            out_ref[i, row + share : row + HW, :] = jnp.where(first, b, a).astype(bf16)
    copy.wait()
    for i, at in enumerate(places):
        out_ref[i, : 2 * HW, :] = own_ref[:, at]


def piece(z_ref, zx_ref, w_ref, i):
    return single(z_ref[...].astype(bf16), w_ref[i, : 2 * HW, :]) + single(
        zx_ref[...].astype(bf16), w_ref[i, 2 * HW :, :]
    )


def farthest(z_ref, zx_ref, w_ref, low_ref, high_ref):
    half = low_ref.shape[0]
    out = piece(z_ref, zx_ref, w_ref, 0)
    low_ref[...] = out[:half]
    high_ref[...] = out[half:]


def nearer(z_ref, zx_ref, w_ref, *out_refs):
    for i, out_ref in enumerate(out_refs):
        out_ref[...] = piece(z_ref, zx_ref, w_ref, i + 1)


def swapped(x, axes):
    n = 2 ** len(axes)
    return lax.ppermute(x, axes, [(i, n - 1 - i) for i in range(n)])


def passed(x, axis, by):
    n = lax.axis_size(axis)
    return lax.ppermute(x, axis, [(i, (i + by) % n) for i in range(n)])


def local(queries, keys, values, rates, init_weight, out_weight):
    rows = queries.shape[0]
    x_hi, z, core, x_lo, y = (lax.axis_index(a).reshape(1) for a in (XH, Z, CORE, XL, Y))
    columns = out_weight.shape[1] // SIZES[3]
    chunk = columns // SIZES[4]
    square, wide, out_piece = ((HW, HW), f32), ((HW, 2 * HW), f32), ((rows, chunk), f32)

    share = HW // 2
    keep, send, solved = call(
        shard_maps, [wide, wide, ((2, rows, 2 * HW), f32)], [core],
        keys, values, rates,
        scratch=[pltpu.VMEM((rows, 2 * HW), bf16)] * 2
        + [pltpu.VMEM((2, rows), f32)] + [pltpu.SemaphoreType.DMA] * 3,
        space=pltpu.HBM, limit=8, us=3,
    )
    got = swapped(send, (CORE,))

    def across_z(x, to):
        return lax.ppermute(x, Z, [(i, to(i)) for i in range(SIZES[1])])

    own_rows, token = call(shard_rows, [((rows, 4 * HW), f32), ((8, HW), f32)], [], queries, keys, rates, solved, us=0.1)
    chip, early = pl.pallas_call(
        chip_map,
        name="chip_map",
        out_shape=[jax.ShapeDtypeStruct((HW, 2 * HW), f32), pltpu.HBM((HW, 2 * HW), f32)],
        in_specs=[SM, VM, VM, pl.BlockSpec(memory_space=pl.ANY)],
        out_specs=[VM, pl.BlockSpec(memory_space=pltpu.HBM)],
        scratch_shapes=[pltpu.VMEM((HW, 2 * HW), f32), pltpu.SemaphoreType.DMA],
        compiler_params=pltpu.CompilerParams(vmem_limit_bytes=4 * MIB),
    )(core, keep, got, token)
    near_out, far_out = weight_shares(out_weight, 1 - x_lo, core, share, chip)
    near = swapped(near_out, (XL,))
    got_chip = across_z(chip, lambda i: i ^ 1)
    (both,) = call(join_chips, [wide], [z], chip, got_chip, later=[near_out], us=2)
    (pre,) = call(before_chips, [wide], [z], chip, got_chip, later=[both], us=0.1)
    far = swapped(far_out, (XH, XL))
    got_both = across_z(both, lambda i: i ^ 2)
    (four,) = call(join_pairs, [wide], [z], both, got_both, later=[pre], us=3)
    (pre,) = call(before_pairs, [wide], [z], both, got_both, pre, later=[four], us=0.1)
    near_other = swapped(near, (CORE,))
    (first,) = call(fetched, [((2, HW, HW), f32)], [], init_weight, later=[four], us=0.1)
    got_four = across_z(four, lambda i: 7 - i)
    (end,) = call(join_ring, [square], [z, core], four, got_four, first, later=[pre], us=2)
    far_other = swapped(far, (CORE,))
    here = lax.ppermute(end, (XH, CORE), [(0, 2), (1, 3)])
    there = lax.ppermute(end, (XH, CORE), [(0, 3), (1, 2)])
    mine, other = call(shard_prefixes, [wide, wide], [z, core], four, got_four, pre, early, later=[end], us=0.1)
    (begin,) = call(ring_states, [((2, HW, HW), f32)], [x_hi, core], here, there, first, us=5)
    (late_rows,) = call(fetched, [((rows, 4 * HW), f32)], [], own_rows, later=[end], us=0.1)
    (z_rows,) = call(
        outputs, [((rows, 2 * HW), f32)], [core], mine, swapped(other, (CORE,)), begin, late_rows, later=[near_other], us=4
    )
    z_pair = swapped(z_rows, (XL,))
    weights = pl.pallas_call(
        piece_weights,
        name="piece_weights",
        out_shape=jax.ShapeDtypeStruct((SIZES[4], 4 * HW, chunk), bf16),
        in_specs=[SM] * 3 + [pl.BlockSpec(memory_space=pltpu.HBM)] + [VM] * 4 + [pl.BlockSpec(memory_space=pl.ANY)],
        out_specs=VM,
        scratch_shapes=[pltpu.VMEM((2 * HW, columns), bf16), pltpu.SemaphoreType.DMA],
        compiler_params=pltpu.CompilerParams(vmem_limit_bytes=16 * MIB),
        cost_estimate=pl.CostEstimate(flops=int(3 * 1e9), bytes_accessed=1 << 17, transcendentals=0),
    )(
        x_lo, y, core, pltpu.with_memory_space_constraint(out_weight, pltpu.HBM),
        near, near_other, far, far_other, z_rows,
    )

    factors = (z_rows, z_pair, weights)
    low, high = call(farthest, [((rows // 2, chunk), f32)] * 2, [], *factors, limit=16)
    down, up = passed(low, Y, -1), passed(high, Y, 1)
    pieces = call(nearer, [out_piece] * (len(OFFSETS) - 1), [], *factors, later=[low], limit=16)
    down = pieces[0] + jnp.concatenate([down, jnp.zeros_like(down)], axis=0)
    up = pieces[1] + jnp.concatenate([jnp.zeros_like(up), up], axis=0)
    for i in (2, 4):
        down = passed(down, Y, -1) + pieces[i]
        up = passed(up, Y, 1) + pieces[i + 1]
    return (passed(down, Y, -1) + passed(up, Y, 1) + pieces[6]).astype(bf16)


def solution(mesh):
    fine = Mesh(mesh.devices.reshape(SIZES), (XH, Z, CORE, XL, Y))
    ctx, tp = (XH, Z, CORE), (XL, Y)
    in_specs = (P(ctx, tp), P(ctx, tp), P(ctx, tp), P(tp, ctx), P(tp, None, None), P(tp, None))
    return jax.shard_map(local, mesh=fine, in_specs=in_specs, out_specs=P(ctx, tp), check_vma=False)
```

```python
import jax
import jax.numpy as jnp
from jax import lax
from jax.experimental import pallas as pl
from jax.experimental.pallas import tpu as pltpu
from jax.sharding import Mesh, PartitionSpec as P

MB = 16
HW = 128
XH, Z, CORE, XL, Y = "xh", "z", "core", "xl", "y"
SIZES = (2, 8, 2, 2, 8)
f32 = jnp.float32
bf16 = jnp.bfloat16
VM = pl.BlockSpec(memory_space=pltpu.VMEM)
SM = pl.BlockSpec(memory_space=pltpu.SMEM)
MIB = 2**20


def exact(a, b, contract=((1,), (0,))):
    return lax.dot_general(
        a, b, (contract, ((), ())), precision=lax.Precision.HIGH, preferred_element_type=f32
    )


def single(a, b, contract=((1,), (0,))):
    return lax.dot_general(a, b, (contract, ((), ())), preferred_element_type=f32)


def call(kernel, out_shapes, place, *args, later=(), scratch=(), limit=4, us=1.0, space=pltpu.VMEM, pinned=False):
    outs = [pltpu.VMEM(s, d) if pinned else jax.ShapeDtypeStruct(s, d) for s, d in out_shapes]
    n = len(place) + len(args)

    def body(*refs):
        kernel(*refs[:n], *refs[n + len(later) :])

    return pl.pallas_call(
        body,
        name=kernel.__name__,
        out_shape=outs,
        in_specs=[SM] * len(place) + [pl.BlockSpec(memory_space=space)] * len(args) + [pl.BlockSpec(memory_space=pl.ANY)] * len(later),
        out_specs=[VM] * len(outs),
        scratch_shapes=list(scratch),
        compiler_params=pltpu.CompilerParams(vmem_limit_bytes=limit * MIB),
        cost_estimate=pl.CostEstimate(flops=int(us * 1e9), bytes_accessed=1 << 17, transcendentals=0),
    )(*place, *(pltpu.with_memory_space_constraint(x, space) for x in args), *later)


def left_half(shape):
    return lax.broadcasted_iota(jnp.int32, shape, 1) < HW


def identity(columns):
    rows_at = lax.broadcasted_iota(jnp.int32, (HW, columns), 0)
    return (rows_at == lax.broadcasted_iota(jnp.int32, (HW, columns), 1)).astype(f32)


def after(second, first):
    return exact(second[:, :HW], first) + jnp.where(left_half(second.shape), 0.0, second)


def applied(pair, state):
    return exact(pair[:, :HW], state) + pair[:, HW:]


def gathered(copies):
    for copy in copies:
        copy.start()
    return copies


def shard_maps(core_ref, k_hbm, v_hbm, r_hbm, keep_ref, send_ref, x_ref, k_ref, v_ref, r_ref, *done):
    copies = gathered(
        [
            pltpu.make_async_copy(source, target, semaphore)
            for source, target, semaphore in zip(
                (k_hbm, v_hbm, r_hbm), (k_ref, v_ref, r_ref), done
            )
        ]
    )
    rows = k_ref.shape[0]
    s_at = lax.broadcasted_iota(jnp.int32, (rows, rows), 0)
    t_at = lax.broadcasted_iota(jnp.int32, (rows, rows), 1)
    earlier_block = (t_at // MB) < (s_at // MB)
    diagonal = t_at == s_at
    key_gram, columns = [], []
    for copy in copies:
        copy.wait()
    for h in range(2):
        at = slice(h * HW, (h + 1) * HW)
        k, r = k_ref[:, at], r_ref[h : h + 1, :]
        columns.append(jnp.sum(jnp.where(diagonal, r, 0.0), axis=1, keepdims=True))
        key_gram.append(jnp.where(earlier_block, single(k, k, ((1,), (1,))) * r, 0.0))
        x_ref[h, :, :HW] = k.astype(f32)
        x_ref[h, :, HW:] = v_ref[:, at].astype(f32)
    for i in range(1, rows // MB):
        at = slice(i * MB, (i + 1) * MB)
        for h in range(2):
            x_ref[h, at, :] = x_ref[h, at, :] - exact(key_gram[h][at, :], x_ref[h])
    maps = []
    for h in range(2):
        at = slice(h * HW, (h + 1) * HW)
        ab = exact(k_ref[:, at].astype(f32) * columns[h], x_ref[h], ((0,), (0,)))
        maps.append(identity(2 * HW) + jnp.where(left_half(ab.shape), -ab, ab))
    first = core_ref[0] == 0
    keep_ref[...] = jnp.where(first, maps[0], maps[1])
    send_ref[...] = jnp.where(first, maps[1], maps[0])


def shard_rows(q_ref, k_ref, r_ref, x_ref, rows_ref, token_ref):
    token_ref[...] = jnp.zeros_like(token_ref)
    rows = q_ref.shape[0]
    s_at = lax.broadcasted_iota(jnp.int32, (rows, rows), 0)
    t_at = lax.broadcasted_iota(jnp.int32, (rows, rows), 1)
    for h in range(2):
        at = slice(h * HW, (h + 1) * HW)
        q = q_ref[:, at]
        mix = jnp.where(t_at <= s_at, single(q, k_ref[:, at], ((1,), (1,))) * r_ref[h : h + 1, :], 0.0)
        y = exact(mix, x_ref[h])
        rows_ref[:, at] = q.astype(f32) - y[:, :HW]
        rows_ref[:, (2 + h) * HW : (3 + h) * HW] = y[:, HW:]


def in_order(first_core, keep_ref, got_ref):
    keep, got = keep_ref[...], got_ref[...]
    return jnp.where(first_core, keep, got), jnp.where(first_core, got, keep)


def chip_map(core_ref, keep_ref, got_ref, later_ref, out_ref, early_hbm, early_ref, done):
    del later_ref
    early, late = in_order(core_ref[0] == 0, keep_ref, got_ref)
    early_ref[...] = early
    copy = pltpu.make_async_copy(early_ref, early_hbm, done)
    copy.start()
    out_ref[...] = after(late, early)
    copy.wait()


def is_upper(z, span):
    return lax.rem(z, 2 * span) >= span


def halves(upper, own_ref, got_ref):
    own, got = own_ref[...], got_ref[...]
    return jnp.where(upper, got, own), jnp.where(upper, own, got)


def prefixed(upper, low, pre):
    return jnp.where(upper, after(pre, low), pre)


def join_chips(z_ref, own_ref, got_ref, both_ref):
    low, high = halves(is_upper(z_ref[0], 1), own_ref, got_ref)
    both_ref[...] = after(high, low)


def join_pairs(z_ref, own_ref, got_ref, both_ref):
    low, high = halves(is_upper(z_ref[0], 2), own_ref, got_ref)
    both_ref[...] = after(high, low)


def join_ring(z_ref, core_ref, own_ref, got_ref, first_ref, end_ref):
    low, high = halves(is_upper(z_ref[0], 4), own_ref, got_ref)
    end_ref[...] = applied(high, applied(low, first_ref[core_ref[0]]))


def before_chips(z_ref, own_ref, got_ref, pre_ref):
    upper = is_upper(z_ref[0], 1)
    low, _ = halves(upper, own_ref, got_ref)
    pre_ref[...] = jnp.where(upper, low, identity(2 * HW))


def before_pairs(z_ref, own_ref, got_ref, pre_in_ref, pre_ref):
    upper = is_upper(z_ref[0], 2)
    low, _ = halves(upper, own_ref, got_ref)
    pre_ref[...] = prefixed(upper, low, pre_in_ref[...])


def shard_prefixes(z_ref, core_ref, own_ref, got_ref, pre_in_ref, early_ref, mine_ref, other_ref):
    upper = is_upper(z_ref[0], 4)
    low, _ = halves(upper, own_ref, got_ref)
    pre = prefixed(upper, low, pre_in_ref[...])
    middle = after(early_ref[...], pre)
    first = core_ref[0] == 0
    mine_ref[...] = jnp.where(first, pre, middle)
    other_ref[...] = jnp.where(first, middle, pre)


def ring_states(x_hi_ref, core_ref, here_ref, there_ref, first_ref, out_ref):
    for h in range(2):
        arrived = jnp.where(core_ref[0] == h, here_ref[...], there_ref[...])
        out_ref[h] = jnp.where(x_hi_ref[0] == 0, first_ref[h], arrived)


def fetched(in_ref, out_ref):
    out_ref[...] = in_ref[...]


def outputs(core_ref, mine_ref, got_ref, begin_ref, rows_ref, z_ref):
    for h in range(2):
        state = applied(jnp.where(core_ref[0] == h, mine_ref[...], got_ref[...]), begin_ref[h])
        at = slice(h * HW, (h + 1) * HW)
        z = exact(rows_ref[:, at], state) + rows_ref[:, (2 + h) * HW : (3 + h) * HW]
        z_ref[:, at] = z.astype(bf16).astype(f32)


def share_weights(column_ref, row_ref, near_in, far_in, later_ref, near_ref, far_ref):
    del column_ref, row_ref, later_ref
    near_ref[...] = near_in[...].astype(f32)
    far_ref[...] = far_in[...].astype(f32)


def weight_shares(weight, column, row, rows, later):
    columns, parts = weight.shape[1] // SIZES[3], 2
    return pl.pallas_call(
        share_weights,
        name="share_weights",
        grid_spec=pltpu.PrefetchScalarGridSpec(
            num_scalar_prefetch=2,
            grid=(parts,),
            in_specs=[
                pl.BlockSpec((rows, columns // parts), lambda i, c, r: (r[0], c[0] * parts + i)),
                pl.BlockSpec((rows, columns // parts), lambda i, c, r: (r[0] + 2, c[0] * parts + i)),
                pl.BlockSpec(memory_space=pl.ANY),
            ],
            out_specs=[pl.BlockSpec((rows, columns // parts), lambda i, c, r: (0, i))] * 2,
        ),
        out_shape=[jax.ShapeDtypeStruct((rows, columns), f32)] * 2,
        compiler_params=pltpu.CompilerParams(vmem_limit_bytes=8 * MIB),
    )(column, row, weight, weight, later)


OFFSETS = (4, -3, 3, -2, 2, -1, 1, 0)


def piece_weights(x_lo_ref, y_ref, core_ref, w_hbm, n0, n1, f0, f1, later_ref, out_ref, own_ref, done):
    del later_ref
    chunk = out_ref.shape[2]
    columns = own_ref.shape[1]
    copy = pltpu.make_async_copy(
        w_hbm.at[:, pl.ds(pl.multiple_of(x_lo_ref[0] * columns, HW), columns)], own_ref, done
    )
    copy.start()
    first = core_ref[0] == 0
    share = HW // 2
    places = [
        pl.ds(pl.multiple_of(lax.rem(y_ref[0] + (o + SIZES[4]), SIZES[4]) * chunk, HW), chunk) for o in OFFSETS
    ]
    for i, at in enumerate(places):
        for j, (mine, other) in enumerate(((n0, n1), (f0, f1))):
            a, b = mine[:, at], other[:, at]
            row = 2 * HW + j * HW
            out_ref[i, row : row + share, :] = jnp.where(first, a, b).astype(bf16)
            out_ref[i, row + share : row + HW, :] = jnp.where(first, b, a).astype(bf16)
    copy.wait()
    for i, at in enumerate(places):
        out_ref[i, : 2 * HW, :] = own_ref[:, at]


def piece(z_ref, zx_ref, w_ref, i):
    return single(z_ref[...].astype(bf16), w_ref[i, : 2 * HW, :]) + single(
        zx_ref[...].astype(bf16), w_ref[i, 2 * HW :, :]
    )


def farthest(z_ref, zx_ref, w_ref, low_ref, high_ref):
    half = low_ref.shape[0]
    out = piece(z_ref, zx_ref, w_ref, 0)
    low_ref[...] = out[:half]
    high_ref[...] = out[half:]


def nearer(z_ref, zx_ref, w_ref, *out_refs):
    for i, out_ref in enumerate(out_refs):
        out_ref[...] = piece(z_ref, zx_ref, w_ref, i + 1)


def swapped(x, axes):
    n = 2 ** len(axes)
    return lax.ppermute(x, axes, [(i, n - 1 - i) for i in range(n)])


def passed(x, axis, by):
    n = lax.axis_size(axis)
    return lax.ppermute(x, axis, [(i, (i + by) % n) for i in range(n)])


def local(queries, keys, values, rates, init_weight, out_weight):
    rows = queries.shape[0]
    x_hi, z, core, x_lo, y = (lax.axis_index(a).reshape(1) for a in (XH, Z, CORE, XL, Y))
    columns = out_weight.shape[1] // SIZES[3]
    chunk = columns // SIZES[4]
    square, wide, out_piece = ((HW, HW), f32), ((HW, 2 * HW), f32), ((rows, chunk), f32)

    share = HW // 2
    keep, send, solved = call(
        shard_maps, [wide, wide, ((2, rows, 2 * HW), f32)], [core],
        keys, values, rates,
        scratch=[pltpu.VMEM((rows, 2 * HW), bf16)] * 2
        + [pltpu.VMEM((2, rows), f32)] + [pltpu.SemaphoreType.DMA] * 3,
        space=pltpu.HBM, limit=8, us=3,
    )
    got = swapped(send, (CORE,))

    def across_z(x, to):
        return lax.ppermute(x, Z, [(i, to(i)) for i in range(SIZES[1])])

    own_rows, token = call(shard_rows, [((rows, 4 * HW), f32), ((8, HW), f32)], [], queries, keys, rates, solved, us=0.1)
    chip, early = pl.pallas_call(
        chip_map,
        name="chip_map",
        out_shape=[jax.ShapeDtypeStruct((HW, 2 * HW), f32), pltpu.HBM((HW, 2 * HW), f32)],
        in_specs=[SM, VM, VM, pl.BlockSpec(memory_space=pl.ANY)],
        out_specs=[VM, pl.BlockSpec(memory_space=pltpu.HBM)],
        scratch_shapes=[pltpu.VMEM((HW, 2 * HW), f32), pltpu.SemaphoreType.DMA],
        compiler_params=pltpu.CompilerParams(vmem_limit_bytes=4 * MIB),
    )(core, keep, got, token)
    near_out, far_out = weight_shares(out_weight, 1 - x_lo, core, share, chip)
    near = swapped(near_out, (XL,))
    got_chip = across_z(chip, lambda i: i ^ 1)
    (both,) = call(join_chips, [wide], [z], chip, got_chip, later=[near_out], us=2)
    (pre,) = call(before_chips, [wide], [z], chip, got_chip, later=[both], us=0.1)
    far = swapped(far_out, (XH, XL))
    got_both = across_z(both, lambda i: i ^ 2)
    (four,) = call(join_pairs, [wide], [z], both, got_both, later=[pre], us=3)
    (pre,) = call(before_pairs, [wide], [z], both, got_both, pre, later=[four], us=0.1)
    near_other = swapped(near, (CORE,))
    (first,) = call(fetched, [((2, HW, HW), f32)], [], init_weight, later=[four], us=0.1)
    got_four = across_z(four, lambda i: 7 - i)
    (end,) = call(join_ring, [square], [z, core], four, got_four, first, later=[pre], us=2)
    far_other = swapped(far, (CORE,))
    here = lax.ppermute(end, (XH, CORE), [(0, 2), (1, 3)])
    there = lax.ppermute(end, (XH, CORE), [(0, 3), (1, 2)])
    mine, other = call(shard_prefixes, [wide, wide], [z, core], four, got_four, pre, early, later=[end], us=0.1)
    (begin,) = call(ring_states, [((2, HW, HW), f32)], [x_hi, core], here, there, first, us=8)
    (late_rows,) = call(fetched, [((rows, 4 * HW), f32)], [], own_rows, later=[end], us=0.1)
    (z_rows,) = call(
        outputs, [((rows, 2 * HW), f32)], [core], mine, swapped(other, (CORE,)), begin, late_rows, later=[near_other], us=4
    )
    z_pair = swapped(z_rows, (XL,))
    weights = pl.pallas_call(
        piece_weights,
        name="piece_weights",
        out_shape=jax.ShapeDtypeStruct((SIZES[4], 4 * HW, chunk), bf16),
        in_specs=[SM] * 3 + [pl.BlockSpec(memory_space=pltpu.HBM)] + [VM] * 4 + [pl.BlockSpec(memory_space=pl.ANY)],
        out_specs=VM,
        scratch_shapes=[pltpu.VMEM((2 * HW, columns), bf16), pltpu.SemaphoreType.DMA],
        compiler_params=pltpu.CompilerParams(vmem_limit_bytes=16 * MIB),
        cost_estimate=pl.CostEstimate(flops=int(3 * 1e9), bytes_accessed=1 << 17, transcendentals=0),
    )(
        x_lo, y, core, pltpu.with_memory_space_constraint(out_weight, pltpu.HBM),
        near, near_other, far, far_other, z_rows,
    )

    factors = (z_rows, z_pair, weights)
    low, high = call(farthest, [((rows // 2, chunk), f32)] * 2, [], *factors, limit=16)
    down, up = passed(low, Y, -1), passed(high, Y, 1)
    pieces = call(nearer, [out_piece] * (len(OFFSETS) - 1), [], *factors, later=[low], limit=16)
    down = pieces[0] + jnp.concatenate([down, jnp.zeros_like(down)], axis=0)
    up = pieces[1] + jnp.concatenate([jnp.zeros_like(up), up], axis=0)
    for i in (2, 4):
        down = passed(down, Y, -1) + pieces[i]
        up = passed(up, Y, 1) + pieces[i + 1]
    return (passed(down, Y, -1) + passed(up, Y, 1) + pieces[6]).astype(bf16)


def solution(mesh):
    fine = Mesh(mesh.devices.reshape(SIZES), (XH, Z, CORE, XL, Y))
    ctx, tp = (XH, Z, CORE), (XL, Y)
    in_specs = (P(ctx, tp), P(ctx, tp), P(ctx, tp), P(tp, ctx), P(tp, None, None), P(tp, None))
    return jax.shard_map(local, mesh=fine, in_specs=in_specs, out_specs=P(ctx, tp), check_vma=False)
```
